32 devices in a mesh: rep: 8 (over y, x, core), grp: 4 (over z).
Axes of the slice: x: 2, y: 2, z: 4, core: 2. Of those that a mesh axis runs over, the one named last changes fastest.
Arguments:
- latents: bfloat16 [256, 16, 256], P(('rep', 'grp')), may hold values from -6 to 6
- noise: bfloat16 [256, 16, 256], P(('rep', 'grp')), may hold values from -6 to 6
- timesteps: int32 [256], P(('rep', 'grp')), may hold values from 0 to 999
- labels: int32 [256], P(('rep', 'grp')), may hold values from 0 to 999
- emb_table: float32 [1656, 384], P('grp'), may hold values from -4 to 4
- emb_mom: float32 [1656, 384], P('grp'), may hold values from -0.005859375 to 0.005859375
- emb_ema: float32 [1656, 384], P('grp'), may hold values from -4 to 4
- w_in: float32 [2, 384, 4992], P(None, 'grp'), may hold values from -4 to 4
- in_mom: float32 [2, 384, 4992], P(None, 'grp'), may hold values from -0.005859375 to 0.005859375
- in_ema: float32 [2, 384, 4992], P(None, 'grp'), may hold values from -4 to 4
- w_out: float32 [2, 1920, 384], P(None, 'grp'), may hold values from -4 to 4
- out_mom: float32 [2, 1920, 384], P(None, 'grp'), may hold values from -0.005859375 to 0.005859375
- out_ema: float32 [2, 1920, 384], P(None, 'grp'), may hold values from -4 to 4
- head: float32 [384, 784], P('grp'), may hold values from -4 to 4
- head_mom: float32 [384, 784], P('grp'), may hold values from -0.005859375 to 0.005859375
- head_ema: float32 [384, 784], P('grp'), may hold values from -4 to 4
Outputs:
- loss: float32 [], replicated
- new_emb_table: float32 [1656, 384], P('grp')
- new_emb_mom: float32 [1656, 384], P('grp')
- new_emb_ema: float32 [1656, 384], P('grp')
- new_w_in: float32 [2, 384, 4992], P(None, 'grp')
- new_in_mom: float32 [2, 384, 4992], P(None, 'grp')
- new_in_ema: float32 [2, 384, 4992], P(None, 'grp')
- new_w_out: float32 [2, 1920, 384], P(None, 'grp')
- new_out_mom: float32 [2, 1920, 384], P(None, 'grp')
- new_out_ema: float32 [2, 1920, 384], P(None, 'grp')
- new_head: float32 [384, 784], P('grp')
- new_head_mom: float32 [384, 784], P('grp')
- new_head_ema: float32 [384, 784], P('grp')
The draws below stay inside these ranges and needn't reach their ends.
All inputs are finite; a program needn't handle non-finite values.
Results may differ from the reference program's by a relative error of at most 0.012.
Values may be sent and summed in bfloat16 or wider, within the bound.
No kernel may reach another device: no remote copies, remote signals or barrier semaphores. Data moves between devices by JAX's collectives and lax.ppermute only.
A program may use at most 256 MiB of HBM per device.

```python
import math
import jax
import jax.numpy as jnp
from jax import lax

D = 384
HEADS = 6
HEAD_DIM = 64
FF = 1536
FREQ = 256
CLASSES = 1000
PATCH_IN = 16
GRID = 16
LAYERS = 2
TOK = 256
IMAGES = 256
EMB_ROWS = 1656
IN_COLS = 4992
OUT_ROWS = 1920
HEAD_COLS = 784


def base_values(key, shape):
    values = jnp.clip(jax.random.normal(key, shape, jnp.float32), -4.0, 4.0)
    return values


def emb_scales():
    rows = jnp.arange(EMB_ROWS, dtype=jnp.int32)[:, None]
    return jnp.where(rows < PATCH_IN, PATCH_IN ** (-0.5), jnp.where(rows < PATCH_IN + FREQ, FREQ ** (-0.5), jnp.where(rows < PATCH_IN + FREQ + D, D ** (-0.5), 1.0)))


def out_scales():
    rows = jnp.arange(OUT_ROWS, dtype=jnp.int32)[None, :, None]
    return jnp.where(rows < D, 3.0 * D ** (-0.5), FF ** (-0.5))


def draw_emb_table(key, part):
    values = base_values(jax.random.fold_in(key, 101), (EMB_ROWS, D))
    return values * emb_scales()


def draw_emb_ema(key, part):
    values = base_values(jax.random.fold_in(key, 102), (EMB_ROWS, D))
    return values * emb_scales()


def draw_w_in(key, part):
    values = base_values(jax.random.fold_in(key, 103), (LAYERS, D, IN_COLS))
    return values * D ** (-0.5)


def draw_in_ema(key, part):
    values = base_values(jax.random.fold_in(key, 104), (LAYERS, D, IN_COLS))
    return values * D ** (-0.5)


def draw_w_out(key, part):
    values = base_values(jax.random.fold_in(key, 105), (LAYERS, OUT_ROWS, D))
    return values * out_scales()


def draw_out_ema(key, part):
    values = base_values(jax.random.fold_in(key, 106), (LAYERS, OUT_ROWS, D))
    return values * out_scales()


def draw_head(key, part):
    values = base_values(jax.random.fold_in(key, 107), (D, HEAD_COLS))
    return values * D ** (-0.5)


def draw_head_ema(key, part):
    values = base_values(jax.random.fold_in(key, 108), (D, HEAD_COLS))
    return values * D ** (-0.5)


def touch_ends(entries, own_key, least, largest):
    dims = entries.shape
    spot = [jax.random.randint(jax.random.fold_in(own_key, axis), (), 0, dims[axis]) for axis in range(len(dims))]
    entries = entries.at[tuple(spot)].set(least)
    longest = dims.index(max(dims))
    spot[longest] = (spot[longest] + 1) % dims[longest]
    return entries.at[tuple(spot)].set(largest)


def level_of(own_key, shape, cuts, smallest, largest):
    def one(position, shards_of):
        draws = jax.random.uniform(jax.random.fold_in(jax.random.fold_in(own_key, 6), position), (shards_of,), jnp.float32, smallest / len(cuts), largest / len(cuts))
        return jnp.repeat(jnp.exp(draws), shape[position] // shards_of).reshape((-1,) + (1,) * (len(shape) - position - 1))

    gain = one(*cuts[0])
    for cut in cuts[1:]:
        gain = gain * one(*cut)
    return gain


def normal_values(stream_key, shape, spread, limit, cuts=(), kind=jnp.bfloat16):
    values = jax.random.normal(stream_key, shape, jnp.float32) * spread
    if len(cuts) > 0:
        values = level_of(stream_key, shape, cuts, -0.22, 0.18) * values
    return jnp.clip(values, min=-limit, max=limit).astype(kind)


def setup_inputs(seed: int = 0) -> dict:
    splits = jax.random.split(jax.random.key(seed), 17)
    latents = normal_values(splits[0], (IMAGES, PATCH_IN, TOK), 1.0, 6.0, ((0, 32),))
    noise = normal_values(splits[1], (IMAGES, PATCH_IN, TOK), 1.0, 6.0, ((0, 32),))
    timesteps = touch_ends(jax.random.randint(splits[2], (IMAGES,), 0, 1000), jax.random.fold_in(splits[2], 1), 0, 999).astype(jnp.int32)
    labels = touch_ends(jax.random.randint(splits[3], (IMAGES,), 0, CLASSES), jax.random.fold_in(splits[3], 1), 0, CLASSES - 1).astype(jnp.int32)
    emb_table = draw_emb_table(jax.random.fold_in(splits[16], 71), 0)
    emb_mom = normal_values(splits[5], (EMB_ROWS, D), 0.001, 0.005859375, ((0, 4),), jnp.float32)
    emb_ema = draw_emb_ema(jax.random.fold_in(splits[16], 71), 0)
    w_in = draw_w_in(jax.random.fold_in(splits[16], 71), 0)
    in_mom = normal_values(splits[8], (LAYERS, D, IN_COLS), 0.001, 0.005859375, ((1, 4),), jnp.float32)
    in_ema = draw_in_ema(jax.random.fold_in(splits[16], 71), 0)
    w_out = draw_w_out(jax.random.fold_in(splits[16], 71), 0)
    out_mom = normal_values(splits[11], (LAYERS, OUT_ROWS, D), 0.001, 0.005859375, ((1, 4),), jnp.float32)
    out_ema = draw_out_ema(jax.random.fold_in(splits[16], 71), 0)
    head = draw_head(jax.random.fold_in(splits[16], 71), 0)
    head_mom = normal_values(splits[14], (D, HEAD_COLS), 0.001, 0.005859375, ((0, 4),), jnp.float32)
    head_ema = draw_head_ema(jax.random.fold_in(splits[16], 71), 0)
    return {"latents": latents, "noise": noise, "timesteps": timesteps, "labels": labels, "emb_table": emb_table, "emb_mom": emb_mom, "emb_ema": emb_ema, "w_in": w_in, "in_mom": in_mom, "in_ema": in_ema, "w_out": w_out, "out_mom": out_mom, "out_ema": out_ema, "head": head, "head_mom": head_mom, "head_ema": head_ema}


EPSILON = 1e-06
MOMENTUM = 0.9
LEARN = 30.0
DECAY = 0.7
HIGH = lax.Precision.HIGHEST

@jax.custom_vjp
def low(v):
    return lax.optimization_barrier(v.astype(jnp.bfloat16)).astype(jnp.float32)

@jax.custom_vjp
def low_back(v):
    return v

def low_keep(v):
    return (low(v), None)

def low_pass(kept, grad):
    return (grad,)

def back_keep(v):
    return (v, None)

def back_low(kept, grad):
    return (low(grad),)
low.defvjp(low_keep, low_pass)
low_back.defvjp(back_keep, back_low)

def plan(steps_in):
    anchor = math.cos(0.5 * math.pi * 0.008 / 1.008)
    fraction = (steps_in.astype(jnp.float32) / 1000.0 + 0.008) / 1.008
    levels = jnp.cos(0.5 * math.pi * fraction)
    return levels * levels / (anchor * anchor)

def time_features(steps_in, feat_width):
    half_width = feat_width // 2
    frequencies = jnp.exp(-math.log(10000.0) * jnp.arange(half_width, dtype=jnp.float32) / half_width)
    angles = steps_in.astype(jnp.float32)[:, None] * frequencies[None, :]
    return jnp.concatenate([jnp.cos(angles), jnp.sin(angles)], axis=1)

def positions(grid_side, model_width):
    quarter = model_width // 4
    omegas = jnp.exp(-math.log(10000.0) * jnp.arange(quarter, dtype=jnp.float32) / quarter)
    places = jnp.arange(grid_side * grid_side, dtype=jnp.int32)
    column = (places % grid_side).astype(jnp.float32)[:, None] * omegas[None, :]
    row_pos = (places // grid_side).astype(jnp.float32)[:, None] * omegas[None, :]
    return jnp.concatenate([jnp.sin(column), jnp.cos(column), jnp.sin(row_pos), jnp.cos(row_pos)], axis=1)

def swish_act(values):
    return values / (1.0 + jnp.exp(-values))

def gelu_tanh(values):
    return 0.5 * values * (1.0 + jnp.tanh(0.7978845608 * (values + 0.044715 * values * values * values)))

def modulate(hidden, shift_vec, scale_vec):
    centered = hidden - lax.optimization_barrier(jnp.mean(hidden, axis=-1, keepdims=True))
    variance = lax.optimization_barrier(jnp.mean(centered * centered, axis=-1, keepdims=True))
    normed = centered * lax.rsqrt(variance + EPSILON)
    return normed * (1.0 + scale_vec[:, None, :]) + shift_vec[:, None, :]

def matmul_hi(left, right):
    return jnp.dot(left, right, precision=HIGH, preferred_element_type=jnp.float32)

def group_loss(weights_low, group_data):
    emb_w, in_w, out_w, head_w = weights_low
    clean_in, target, steps_in, classes = group_data
    levels = plan(steps_in)
    noise_level = jnp.sqrt(jnp.maximum(1.0 - levels, 0.0))
    noisy_in = low(jnp.sqrt(levels)[:, None, None] * clean_in + noise_level[:, None, None] * target)
    time_feats = low(time_features(steps_in, FREQ))
    w_patch = emb_w[:PATCH_IN]
    w_time1 = emb_w[PATCH_IN:PATCH_IN + FREQ]
    w_time2 = emb_w[PATCH_IN + FREQ:PATCH_IN + FREQ + D]
    w_class = emb_w[PATCH_IN + FREQ + D:]
    pre_time = matmul_hi(time_feats, w_time1)
    time_act = low(swish_act(pre_time))
    condition = matmul_hi(time_act, w_time2) + w_class[classes]
    cond_act = low(swish_act(condition))
    hidden = low_back(jnp.einsum('icn,cd->ind', noisy_in, w_patch, precision=HIGH)) + positions(GRID, D)[None]
    score_scale = 1.0 / math.sqrt(HEAD_DIM)
    images = hidden.shape[0]
    for layer_idx in range(LAYERS):
        w_ada = in_w[layer_idx, :, :6 * D]
        w_qkv = in_w[layer_idx, :, 6 * D:9 * D]
        w_fc1 = in_w[layer_idx, :, 9 * D:]
        w_proj = out_w[layer_idx, :D]
        w_fc2 = out_w[layer_idx, D:]
        modulation = matmul_hi(cond_act, w_ada)
        shift_a, scale_a, gate_a, shift_b, scale_b, gate_b = jnp.split(modulation, 6, axis=1)
        normed_a = low(modulate(hidden, shift_a, scale_a))
        qkv_all = low_back(low(jnp.einsum('ind,dc->inc', normed_a, w_qkv, precision=HIGH)))
        split_qkv = qkv_all.reshape(images, TOK, 3, HEADS, HEAD_DIM)
        scores = low_back(jnp.einsum('inhe,imhe->ihnm', split_qkv[:, :, 0], split_qkv[:, :, 1], precision=HIGH) * score_scale)
        row_peak = lax.optimization_barrier(jnp.max(scores, axis=-1, keepdims=True))
        exps = jnp.exp(scores - row_peak)
        probabilities = exps / lax.optimization_barrier(jnp.sum(exps, axis=-1, keepdims=True))
        attended = jnp.einsum('ihnm,imhe->inhe', low(probabilities), split_qkv[:, :, 2], precision=HIGH).reshape(images, TOK, D)
        attended = low(low_back(attended))
        branch_a = low_back(jnp.einsum('ind,de->ine', attended, w_proj, precision=HIGH))
        middle = hidden + gate_a[:, None, :] * branch_a
        normed_b = low(modulate(middle, shift_b, scale_b))
        pre_act = low_back(jnp.einsum('ind,df->inf', normed_b, w_fc1, precision=HIGH))
        activated = low(gelu_tanh(pre_act))
        branch_b = low_back(jnp.einsum('inf,fd->ind', activated, w_fc2, precision=HIGH))
        hidden = middle + gate_b[:, None, :] * branch_b
    final_mods = matmul_hi(cond_act, head_w[:, :2 * D])
    shift_f, scale_f = jnp.split(final_mods, 2, axis=1)
    normed_f = low(modulate(hidden, shift_f, scale_f))
    output = low_back(jnp.einsum('ind,dc->icn', normed_f, head_w[:, 2 * D:], precision=HIGH))
    residue = output - target
    return jnp.sum(residue * residue)

def advance(weight, moment, average, gradient):
    new_moment = MOMENTUM * moment + gradient
    new_weight = weight - LEARN * (gradient + MOMENTUM * new_moment)
    new_average = DECAY * average + (1.0 - DECAY) * new_weight
    return (new_weight, new_moment, new_average)

def reference(latents, noise, timesteps, labels, emb_table, emb_mom, emb_ema, w_in, in_mom, in_ema, w_out, out_mom, out_ema, head, head_mom, head_ema):
    params = (emb_table, w_in, w_out, head)
    group_size = 16
    groups = IMAGES // group_size
    inputs_all = (latents.astype(jnp.float32), noise.astype(jnp.float32), timesteps, labels)
    stacked = tuple((member.reshape((groups, group_size) + member.shape[1:]) for member in inputs_all))

    def total_loss(weights):
        weights_low = tuple((low(member) for member in weights))

        def step_fn(running, group_data):
            return (running + group_loss(weights_low, group_data), None)
        summed, _ = lax.scan(jax.checkpoint(step_fn), jnp.zeros((), jnp.float32), stacked)
        return summed / (IMAGES * TOK * PATCH_IN)
    loss_value, pullback = jax.vjp(total_loss, params)
    gradients = pullback(jnp.ones((), jnp.float32))[0]
    emb_new = advance(emb_table, emb_mom, emb_ema, gradients[0])
    in_new = advance(w_in, in_mom, in_ema, gradients[1])
    out_new = advance(w_out, out_mom, out_ema, gradients[2])
    head_new = advance(head, head_mom, head_ema, gradients[3])
    return (loss_value, emb_new[0], emb_new[1], emb_new[2], in_new[0], in_new[1], in_new[2], out_new[0], out_new[1], out_new[2], head_new[0], head_new[1], head_new[2])
```

```python
import functools
import math

import jax
import jax.numpy as jnp
from jax import lax
from jax.experimental import pallas as pl
from jax.experimental.pallas import tpu as pltpu
from jax.sharding import PartitionSpec as P

D = 384
HEADS = 6
HEAD_DIM = 64
FF = 1536
TOK = 256
PATCH_IN = 16
EPSILON = 1e-06
BF = jnp.bfloat16
F32 = jnp.float32
VMEM_LIMIT = 58 * 1024 * 1024


def mm(left, right):
    return lax.dot_general(left, right, (((1,), (0,)), ((), ())), preferred_element_type=F32)


def mm_nt(left, right):
    return lax.dot_general(left, right, (((1,), (1,)), ((), ())), preferred_element_type=F32)


def norm_parts(x):
    centered = x - jnp.mean(x, axis=0, keepdims=True)
    variance = jnp.mean(centered * centered, axis=0, keepdims=True)
    inv = lax.rsqrt(variance + EPSILON)
    return centered * inv, inv


def norm_back(d, normed, inv, scale1):
    dn = d * scale1
    m1 = jnp.mean(dn, axis=0, keepdims=True)
    m2 = jnp.mean(dn * normed, axis=0, keepdims=True)
    return (dn - m1 - normed * m2) * inv


def column(mods_ref, index, image):
    block = mods_ref[pl.ds(index * D, D), :]
    lane = lax.broadcasted_iota(jnp.int32, block.shape, 1)
    return jnp.sum(jnp.where(lane == image, block, 0.0), axis=1, keepdims=True)


def put_column(out_ref, index, image, values):
    total = jnp.sum(values, axis=1, keepdims=True)
    rows = pl.ds(index * D, D)
    old = out_ref[rows, :]
    lane = lax.broadcasted_iota(jnp.int32, old.shape, 1)
    out_ref[rows, :] = jnp.where(lane == image, total, old)


def half_zero(x, half):
    row = lax.broadcasted_iota(jnp.int32, x.shape, 0)
    keep = row < HEAD_DIM if half == 0 else row >= HEAD_DIM
    return jnp.where(keep, x, jnp.zeros_like(x))


def attention_forward(qkv_ref, b, lse_ref, att_ref, att_lanes):
    for pair in range(HEADS // 2):
        lo = 2 * HEAD_DIM * pair
        q2 = qkv_ref[b, lo : lo + 128, :]
        k2 = qkv_ref[b, D + lo : D + lo + 128, :].T
        for half in range(2):
            head = 2 * pair + half
            scores = mm(k2, half_zero(q2, half))
            peak = jnp.max(scores, axis=0, keepdims=True)
            exps = jnp.exp(scores - peak)
            total = jnp.sum(exps, axis=0, keepdims=True)
            vrow = 2 * D + HEAD_DIM * head
            out = mm(qkv_ref[b, vrow : vrow + HEAD_DIM, :], exps.astype(BF))
            att_ref[HEAD_DIM * head : HEAD_DIM * (head + 1), att_lanes] = (
                out * (1.0 / total)
            ).astype(BF)
            lse_ref[b, head : head + 1, :] = peak + jnp.log(total)


def attention_backward(qkv_ref, b, lse_ref, go_ref, gqkv_ref, lanes):
    for pair in range(HEADS // 2):
        lo = 2 * HEAD_DIM * pair
        q2 = qkv_ref[b, lo : lo + 128, :]
        k2 = qkv_ref[b, D + lo : D + lo + 128, :].T
        v2 = qkv_ref[b, 2 * D + lo : 2 * D + lo + 128, :].T
        g2 = go_ref[b, lo : lo + 128, :]
        for half in range(2):
            head = 2 * pair + half
            row = HEAD_DIM * head
            scores = mm(k2, half_zero(q2, half))
            probs = jnp.exp(scores - lse_ref[b, head : head + 1, :])
            gprobs = mm(v2, half_zero(g2, half))
            inner = jnp.sum(probs * gprobs, axis=0, keepdims=True)
            gscores = (probs * (gprobs - inner)).astype(BF)
            gq = mm(qkv_ref[b, D + row : D + row + HEAD_DIM, :], gscores)
            gk = mm_nt(qkv_ref[b, row : row + HEAD_DIM, :], gscores)
            gv = mm_nt(go_ref[b, row : row + HEAD_DIM, :], probs.astype(BF))
            gqkv_ref[row : row + HEAD_DIM, lanes] = (gq * (1.0 / math.sqrt(HEAD_DIM))).astype(BF)
            gqkv_ref[D + row : D + row + HEAD_DIM, lanes] = gk.astype(BF)
            gqkv_ref[2 * D + row : 2 * D + row + HEAD_DIM, lanes] = gv.astype(BF)


def project_qkv(wqkv_t_ref, normed_ref, lanes, qkv_ref, b):
    qkv = mm(wqkv_t_ref[...], normed_ref[:, lanes])
    qkv_ref[b, 0:D, :] = (qkv[0:D] * (1.0 / math.sqrt(HEAD_DIM))).astype(BF)
    qkv_ref[b, D:, :] = qkv[D:].astype(BF)


GELU_C = 0.7978845608
GELU_A = 0.044715


def gelu_both(v):
    square = v * v
    t = jnp.tanh(v * (GELU_C + (GELU_C * GELU_A) * square))
    half = 0.5 + 0.5 * t
    slope = half + 0.5 * v * (1.0 - t * t) * (GELU_C + (3.0 * GELU_C * GELU_A) * square)
    return v * half, slope


def gelu_one(v):
    t = jnp.tanh(v * (GELU_C + (GELU_C * GELU_A) * (v * v)))
    return v * (0.5 + 0.5 * t)


def accumulate(acc_ref, value, first):
    @pl.when(first)
    def _():
        acc_ref[...] = value

    @pl.when(jnp.logical_not(first))
    def _():
        acc_ref[...] += value


FF_CHUNK = 512


def pack_blocks(pack_ref, start, acc_ref):
    members = pack_ref.shape[0]
    rows = D // members
    for g in range(members):
        for c in range(acc_ref.shape[1] // D):
            pack_ref[g, start + rows * c : start + rows * (c + 1), :] = acc_ref[
                rows * g : rows * (g + 1), D * c : D * (c + 1)
            ].astype(BF)


def pack_outer(pack_ref, awo_ref, awf_ref, awg_ref, awy_ref):
    members, total, _ = pack_ref.shape
    rows = (D + FF) // members
    for g in range(members):
        low, high = rows * g, rows * (g + 1)
        if low < D:
            cut = min(high, D)
            pack_ref[g, 0 : cut - low, :] = awo_ref[low:cut, :].astype(BF)
        if high > D:
            cut = max(low, D)
            pack_ref[g, cut - low : rows, :] = awg_ref[cut - D : high - D, :].astype(BF)
    pack_blocks(pack_ref, rows, awf_ref)
    used = rows + FF // members
    pack_ref[:, used:, :] = jnp.zeros_like(pack_ref[:, used:, :])
    if awy_ref is not None:
        for g in range(members):
            pack_ref[g, used : used + PATCH_IN, :] = awy_ref[...].astype(BF)


def att_fwd_kernel(B, noisy_ref, wp_t_ref, pos_ref, mods_ref, wqkv_t_ref, wo_t_ref,
                   qkv_ref, lse_ref, att_out_ref, br_ref, mid_ref, normed_ref, att_ref):
    step = pl.program_id(0)
    for b in range(B):
        image = step * B + b
        lanes = slice(TOK * b, TOK * (b + 1))
        hidden = mm(wp_t_ref[...], noisy_ref[b]) + pos_ref[...]
        normed, _ = norm_parts(hidden)
        shift = column(mods_ref, 0, image)
        scale = column(mods_ref, 1, image)
        gate = column(mods_ref, 2, image)
        normed_ref[:, lanes] = (normed * (1.0 + scale) + shift).astype(BF)
        project_qkv(wqkv_t_ref, normed_ref, lanes, qkv_ref, b)
        attention_forward(qkv_ref, b, lse_ref, att_ref, lanes)
        att_out_ref[b] = att_ref[:, lanes]
        branch = mm(wo_t_ref[...], att_ref[:, lanes])
        br_ref[b] = branch
        mid_ref[b] = hidden + gate * branch


def ffn_fwd_kernel(B, mid_ref, mods_ref, wf_t_ref, wg_t_ref, br_ref, hid_ref, normed_ref):
    step = pl.program_id(0)
    for b in range(B):
        image = step * B + b
        lanes = slice(TOK * b, TOK * (b + 1))
        mid = mid_ref[b]
        normed, _ = norm_parts(mid)
        shift = column(mods_ref, 3, image)
        scale = column(mods_ref, 4, image)
        gate = column(mods_ref, 5, image)
        normed_ref[:, lanes] = (normed * (1.0 + scale) + shift).astype(BF)
        branch = None
        for f in range(0, FF, FF_CHUNK):
            pre = mm(wf_t_ref[f : f + FF_CHUNK, :], normed_ref[:, lanes])
            part = mm(wg_t_ref[:, f : f + FF_CHUNK], gelu_one(pre).astype(BF))
            branch = part if branch is None else branch + part
        br_ref[b] = branch
        hid_ref[b] = mid + gate * branch


def out_bwd(b, image, lanes, gmid, branch, gate, wo_ref, gba_ref, go_ref, gm_ref, gm_base):
    put_column(gm_ref, gm_base, image, gmid * branch)
    gba_ref[:, lanes] = (gate * gmid).astype(BF)
    go_ref[b] = mm(wo_ref[...], gba_ref[:, lanes]).astype(BF)


def block_kernel(B, entries, hid_ref, noise_ref, mods_ref, modf_ref, wqkv_t_ref, wo_t_ref, wf_t_ref,
                 wg_t_ref, wo_ref, wf_ref, wg_ref, wy_t_ref, wy_ref,
                 qkv_ref, lse_ref, go_ref, gmid_ref, gm_ref, gmf_ref, loss_ref,
                 pack_ref,
                 normed_ref, att_ref, slope_ref, act_ref, gpre_ref, gba_ref, gbb_ref, normf_ref, gout_ref,
                 awo_ref, awf_ref, awg_ref, awy_ref):
    step = pl.program_id(0)
    first = step == 0

    @pl.when(first)
    def _():
        gm_ref[...] = jnp.zeros_like(gm_ref)
        gmf_ref[...] = jnp.zeros_like(gmf_ref)
        loss_ref[...] = jnp.zeros_like(loss_ref)

    for b in range(B):
        image = step * B + b
        lanes = slice(TOK * b, TOK * (b + 1))
        hidden = hid_ref[b]
        normed, _ = norm_parts(hidden)
        normed_ref[:, lanes] = (
            normed * (1.0 + column(mods_ref, 1, image)) + column(mods_ref, 0, image)
        ).astype(BF)
        project_qkv(wqkv_t_ref, normed_ref, lanes, qkv_ref, b)
        attention_forward(qkv_ref, b, lse_ref, att_ref, lanes)
        branch_a = mm(wo_t_ref[...], att_ref[:, lanes])
        gate_a = column(mods_ref, 2, image)
        mid = hidden + gate_a * branch_a
        normed_b, inv_b = norm_parts(mid)
        scale_b = 1.0 + column(mods_ref, 4, image)
        normed_ref[:, lanes] = (normed_b * scale_b + column(mods_ref, 3, image)).astype(BF)
        branch_b = None
        for f in range(0, FF, FF_CHUNK):
            rows = slice(f, f + FF_CHUNK)
            pre = mm(wf_t_ref[rows, :], normed_ref[:, lanes])
            act, slope = gelu_both(pre)
            slope_ref[rows, :] = slope
            act_ref[rows, lanes] = act.astype(BF)
            part = mm(wg_t_ref[:, rows], act_ref[rows, lanes])
            branch_b = part if branch_b is None else branch_b + part
        gate_b = column(mods_ref, 5, image)
        hidden2 = mid + gate_b * branch_b
        normed_f, inv_f = norm_parts(hidden2)
        scale_f = 1.0 + column(modf_ref, 1, image)
        normf_ref[:, lanes] = (normed_f * scale_f + column(modf_ref, 0, image)).astype(BF)
        residue = mm(wy_t_ref[...], normf_ref[:, lanes]) - noise_ref[b].astype(F32)
        loss_ref[...] += residue * residue
        gout_ref[:, lanes] = ((2.0 / entries) * residue).astype(BF)
        gnf = mm(wy_ref[...], gout_ref[:, lanes])
        put_column(gmf_ref, 0, image, gnf)
        put_column(gmf_ref, 1, image, gnf * normed_f)
        ghid = norm_back(gnf, normed_f, inv_f, scale_f)
        put_column(gm_ref, 3, image, ghid * branch_b)
        gbb_ref[:, lanes] = (gate_b * ghid).astype(BF)
        gnb = None
        for f in range(0, FF, FF_CHUNK):
            rows = slice(f, f + FF_CHUNK)
            gact = mm(wg_ref[rows, :], gbb_ref[:, lanes])
            gpre_ref[rows, lanes] = (gact * slope_ref[rows, :]).astype(BF)
            part = mm(wf_ref[:, rows], gpre_ref[rows, lanes])
            gnb = part if gnb is None else gnb + part
        put_column(gm_ref, 1, image, gnb)
        put_column(gm_ref, 2, image, gnb * normed_b)
        gmid = ghid + norm_back(gnb, normed_b, inv_b, scale_b)
        gmid_ref[b] = gmid
        out_bwd(b, image, lanes, gmid, branch_a, gate_a, wo_ref, gba_ref, go_ref, gm_ref, 0)
    accumulate(awo_ref, mm_nt(att_ref[...], gba_ref[...]), first)
    accumulate(awf_ref, mm_nt(normed_ref[...], gpre_ref[...]), first)
    accumulate(awg_ref, mm_nt(act_ref[...], gbb_ref[...]), first)
    accumulate(awy_ref, mm_nt(gout_ref[...], normf_ref[...]), first)

    @pl.when(step == pl.num_programs(0) - 1)
    def _():
        pack_outer(pack_ref, awo_ref, awf_ref, awg_ref, awy_ref)


def ffn_bwd_kernel(B, ghid_ref, mid_ref, att_ref, bra_ref, brb_ref, mods_ref, wf_t_ref, wo_ref, wf_ref,
                   wg_ref, go_ref, gmid_ref, gm_ref, pack_ref,
                   normed_ref, act_ref, gpre_ref, gba_ref, gbb_ref, atts_ref, awo_ref, awf_ref, awg_ref):
    step = pl.program_id(0)
    first = step == 0

    @pl.when(first)
    def _():
        gm_ref[...] = jnp.zeros_like(gm_ref)

    for b in range(B):
        image = step * B + b
        lanes = slice(TOK * b, TOK * (b + 1))
        ghid = ghid_ref[b]
        put_column(gm_ref, 3, image, ghid * brb_ref[b])
        gbb_ref[:, lanes] = (column(mods_ref, 5, image) * ghid).astype(BF)
        normed_b, inv_b = norm_parts(mid_ref[b])
        scale_b = 1.0 + column(mods_ref, 4, image)
        normed_ref[:, lanes] = (normed_b * scale_b + column(mods_ref, 3, image)).astype(BF)
        atts_ref[:, lanes] = att_ref[b]
        gnb = None
        for f in range(0, FF, FF_CHUNK):
            rows = slice(f, f + FF_CHUNK)
            act, slope = gelu_both(mm(wf_t_ref[rows, :], normed_ref[:, lanes]))
            act_ref[rows, lanes] = act.astype(BF)
            gact = mm(wg_ref[rows, :], gbb_ref[:, lanes])
            gpre_ref[rows, lanes] = (gact * slope).astype(BF)
            part = mm(wf_ref[:, rows], gpre_ref[rows, lanes])
            gnb = part if gnb is None else gnb + part
        put_column(gm_ref, 1, image, gnb)
        put_column(gm_ref, 2, image, gnb * normed_b)
        gmid = ghid + norm_back(gnb, normed_b, inv_b, scale_b)
        gmid_ref[b] = gmid
        out_bwd(b, image, lanes, gmid, bra_ref[b], column(mods_ref, 2, image), wo_ref, gba_ref, go_ref,
                gm_ref, 0)
    accumulate(awo_ref, mm_nt(atts_ref[...], gba_ref[...]), first)
    accumulate(awf_ref, mm_nt(normed_ref[...], gpre_ref[...]), first)
    accumulate(awg_ref, mm_nt(act_ref[...], gbb_ref[...]), first)

    @pl.when(step == pl.num_programs(0) - 1)
    def _():
        pack_outer(pack_ref, awo_ref, awf_ref, awg_ref, None)


def att_bwd_kernel(B, bottom, *refs):
    if bottom:
        (noisy_ref, wp_t_ref, pos_ref, qkv_ref, lse_ref, go_ref, gmid_ref, mods_ref, wqkv_ref,
         gm_ref, pack_ref, normed_ref, gqkv_ref, tok_ref, noi_ref, awqkv_ref, awp_ref) = refs
    else:
        (hid_ref, qkv_ref, lse_ref, go_ref, gmid_ref, mods_ref, wqkv_ref,
         ghid_ref, gm_ref, pack_ref, normed_ref, gqkv_ref, awqkv_ref) = refs
    step = pl.program_id(0)
    first = step == 0

    @pl.when(first)
    def _():
        gm_ref[...] = jnp.zeros_like(gm_ref)

    for b in range(B):
        image = step * B + b
        lanes = slice(TOK * b, TOK * (b + 1))
        hidden = mm(wp_t_ref[...], noisy_ref[b]) + pos_ref[...] if bottom else hid_ref[b]
        normed, inv = norm_parts(hidden)
        scale = 1.0 + column(mods_ref, 1, image)
        normed_ref[:, lanes] = (normed * scale + column(mods_ref, 0, image)).astype(BF)
        attention_backward(qkv_ref, b, lse_ref, go_ref, gqkv_ref, lanes)
        gna = mm(wqkv_ref[...], gqkv_ref[:, lanes])
        put_column(gm_ref, 0, image, gna)
        put_column(gm_ref, 1, image, gna * normed)
        ghid = gmid_ref[b] + norm_back(gna, normed, inv, scale)
        if bottom:
            tok_ref[:, lanes] = ghid.astype(BF)
            noi_ref[:, lanes] = noisy_ref[b]
        else:
            ghid_ref[b] = ghid
    accumulate(awqkv_ref, mm_nt(normed_ref[...], gqkv_ref[...]), first)
    if bottom:
        accumulate(awp_ref, mm_nt(noi_ref[...], tok_ref[...]), first)

    @pl.when(step == pl.num_programs(0) - 1)
    def _():
        pack_blocks(pack_ref, 0, awqkv_ref)
        used = 3 * D // pack_ref.shape[0]
        pack_ref[:, used:, :] = jnp.zeros_like(pack_ref[:, used:, :])
        if bottom:
            pack_ref[0, used : used + PATCH_IN, :] = awp_ref[...].astype(BF)


def whole(*shape):
    return pl.BlockSpec(shape, lambda i: (0,) * len(shape))


def images(B, *shape):
    return pl.BlockSpec((B,) + shape, lambda i: (i,) + (0,) * len(shape))


def sds(shape, dtype):
    return jax.ShapeDtypeStruct(shape, dtype)


def run_kernel(kernel, n, B, in_specs, outs, scratch, flops, args):
    out_specs = [spec for spec, _, _ in outs]
    out_shape = [sds(shape, dtype) for _, shape, dtype in outs]
    moved = sum(a.size * a.dtype.itemsize for a in args) + sum(
        math.prod(o.shape) * o.dtype.itemsize for o in out_shape
    )
    return pl.pallas_call(
        kernel,
        grid=(n // B,),
        in_specs=in_specs,
        out_specs=out_specs,
        out_shape=out_shape,
        scratch_shapes=[pltpu.VMEM(shape, dtype) for shape, dtype in scratch],
        compiler_params=pltpu.CompilerParams(vmem_limit_bytes=VMEM_LIMIT),
        cost_estimate=pl.CostEstimate(flops=flops, bytes_accessed=moved, transcendentals=0),
    )(*args)


MODS = whole(6 * D, 128)


def att_forward(noisy, wp_t, pos, mods, wqkv_t, wo_t, B):
    n = noisy.shape[0]
    T = B * TOK
    return run_kernel(
        functools.partial(att_fwd_kernel, B), n, B,
        [images(B, PATCH_IN, TOK), whole(D, PATCH_IN), whole(D, TOK), MODS, whole(3 * D, D), whole(D, D)],
        [(images(B, 3 * D, TOK), (n, 3 * D, TOK), BF), (images(B, 8, TOK), (n, 8, TOK), F32),
         (images(B, D, TOK), (n, D, TOK), BF), (images(B, D, TOK), (n, D, TOK), F32),
         (images(B, D, TOK), (n, D, TOK), F32)],
        [((D, T), BF), ((D, T), BF)],
        2 * n * TOK * (4 * D * D + 2 * D * TOK), (noisy, wp_t, pos, mods, wqkv_t, wo_t))


def ffn_forward(mid, mods, wf_t, wg_t, B):
    n = mid.shape[0]
    T = B * TOK
    return run_kernel(
        functools.partial(ffn_fwd_kernel, B), n, B,
        [images(B, D, TOK), MODS, whole(FF, D), whole(D, FF)],
        [(images(B, D, TOK), (n, D, TOK), F32), (images(B, D, TOK), (n, D, TOK), F32)],
        [((D, T), BF)],
        2 * n * TOK * 2 * D * FF, (mid, mods, wf_t, wg_t))


def block_step(hid, noise, mods, modf, wqkv_t, wo_t, wf_t, wg_t, wo, wf, wg, wy_t, wy, entries, B, pack):
    n = hid.shape[0]
    T = B * TOK
    return run_kernel(
        functools.partial(block_kernel, B, entries), n, B,
        [images(B, D, TOK), images(B, PATCH_IN, TOK), MODS, whole(2 * D, 128), whole(3 * D, D), whole(D, D),
         whole(FF, D), whole(D, FF), whole(D, D), whole(D, FF), whole(FF, D), whole(PATCH_IN, D),
         whole(D, PATCH_IN)],
        [(images(B, 3 * D, TOK), (n, 3 * D, TOK), BF), (images(B, 8, TOK), (n, 8, TOK), F32),
         (images(B, D, TOK), (n, D, TOK), BF), (images(B, D, TOK), (n, D, TOK), F32),
         (whole(4 * D, 128), (4 * D, 128), F32), (whole(2 * D, 128), (2 * D, 128), F32),
         (whole(PATCH_IN, TOK), (PATCH_IN, TOK), F32),
         (whole(*pack), pack, BF)],
        [((D, T), BF), ((D, T), BF), ((FF, TOK), F32), ((FF, T), BF), ((FF, T), BF), ((D, T), BF), ((D, T), BF),
         ((D, T), BF), ((PATCH_IN, T), BF), ((D, D), F32), ((D, FF), F32), ((FF, D), F32), ((PATCH_IN, D), F32)],
        2 * n * TOK * (4 * D * D + 2 * D * TOK + 6 * D * FF + 2 * D * D),
        (hid, noise, mods, modf, wqkv_t, wo_t, wf_t, wg_t, wo, wf, wg, wy_t, wy))


def ffn_backward(ghid, mid, att, bra, brb, mods, wf_t, wo, wf, wg, B, pack):
    n = mid.shape[0]
    T = B * TOK
    full = images(B, D, TOK)
    return run_kernel(
        functools.partial(ffn_bwd_kernel, B), n, B,
        [full, full, full, full, full, MODS, whole(FF, D), whole(D, D), whole(D, FF), whole(FF, D)],
        [(full, (n, D, TOK), BF), (full, (n, D, TOK), F32), (whole(4 * D, 128), (4 * D, 128), F32),
         (whole(*pack), pack, BF)],
        [((D, T), BF), ((FF, T), BF), ((FF, T), BF), ((D, T), BF), ((D, T), BF), ((D, T), BF),
         ((D, D), F32), ((D, FF), F32), ((FF, D), F32)],
        2 * n * TOK * (5 * D * FF + 2 * D * D), (ghid, mid, att, bra, brb, mods, wf_t, wo, wf, wg))


def att_backward(source, qkv, lse, go, gmid, mods, wqkv, B, bottom, pack):
    n = qkv.shape[0]
    T = B * TOK
    full = images(B, D, TOK)
    rest = [images(B, 3 * D, TOK), images(B, 8, TOK), full, full, MODS, whole(D, 3 * D)]
    tail = [(whole(2 * D, 128), (2 * D, 128), F32), (whole(*pack), pack, BF)]
    if bottom:
        ins = [images(B, PATCH_IN, TOK), whole(D, PATCH_IN), whole(D, TOK)] + rest
        outs = tail
        scratch = [((D, T), BF), ((3 * D, T), BF), ((D, T), BF), ((PATCH_IN, T), BF), ((D, 3 * D), F32),
                   ((PATCH_IN, D), F32)]
    else:
        ins = [full] + rest
        outs = [(full, (n, D, TOK), F32)] + tail
        scratch = [((D, T), BF), ((3 * D, T), BF), ((D, 3 * D), F32)]
    return run_kernel(
        functools.partial(att_bwd_kernel, B, bottom), n, B, ins, outs, scratch,
        2 * n * TOK * (6 * D * D + 5 * D * TOK), tuple(source) + (qkv, lse, go, gmid, mods, wqkv))

FREQ = 256
CLASSES = 1000
GRID = 16
LAYERS = 2
MOMENTUM = 0.9
LEARN = 30.0
DECAY = 0.7
IMAGES_PER_STEP = 2


def plan(steps_in):
    anchor = math.cos(0.5 * math.pi * 0.008 / 1.008)
    fraction = (steps_in.astype(F32) / 1000.0 + 0.008) / 1.008
    levels = jnp.cos(0.5 * math.pi * fraction)
    return levels * levels / (anchor * anchor)


def time_features(steps_in):
    half_width = FREQ // 2
    frequencies = jnp.exp(-math.log(10000.0) * jnp.arange(half_width, dtype=F32) / half_width)
    angles = steps_in.astype(F32)[:, None] * frequencies[None, :]
    return jnp.concatenate([jnp.cos(angles), jnp.sin(angles)], axis=1)


def positions():
    quarter = D // 4
    omegas = jnp.exp(-math.log(10000.0) * jnp.arange(quarter, dtype=F32) / quarter)
    places = jnp.arange(GRID * GRID, dtype=jnp.int32)
    column = omegas[:, None] * (places % GRID).astype(F32)[None, :]
    row_pos = omegas[:, None] * (places // GRID).astype(F32)[None, :]
    return jnp.concatenate(
        [jnp.sin(column), jnp.cos(column), jnp.sin(row_pos), jnp.cos(row_pos)], axis=0
    )


def swish_act(values):
    return values / (1.0 + jnp.exp(-values))


def swish_slope(values):
    s = 1.0 / (1.0 + jnp.exp(-values))
    return s * (1.0 + values * (1.0 - s))


def advance(weight, moment, average, gradient):
    new_moment = MOMENTUM * moment + gradient
    new_weight = weight - LEARN * (gradient + MOMENTUM * new_moment)
    new_average = DECAY * average + (1.0 - DECAY) * new_weight
    return (new_weight, new_moment, new_average)


def swap(x, axis, mask):
    pairs = [(i, i ^ mask) for i in range(lax.axis_size(axis))]
    return lax.ppermute(x, axis, pairs)


def digit_list(n):
    found, shift = [], 0
    while (1 << shift) < n:
        left = n >> shift
        size = 2 if shift == 0 or left == 2 else 4
        found.append((shift, size))
        shift += size.bit_length() - 1
    return found


def place_of(index, n):
    place = 0
    for shift, size in digit_list(n):
        place = place * size + ((index >> shift) & (size - 1))
    return place


def pick(x, index, axis=0):
    return lax.dynamic_index_in_dim(x, index, axis, keepdims=False)


def add_low(parts):
    total = parts[0].astype(F32)
    for part in parts[1:]:
        total = total + part.astype(F32)
    return total.astype(BF)


def spread(piece, n):
    pieces = {0: piece}
    digits = digit_list(n)
    for shift, size in digits[1:] + digits[:1]:
        known = dict(pieces)
        for j in range(1, size):
            for mask, value in known.items():
                pieces[mask ^ (j << shift)] = swap(value, "rep", j << shift)
    return pieces


def gather_rows(rows):
    nr, ng = lax.axis_size("rep"), lax.axis_size("grp")
    cur = jnp.concatenate([rows] + [swap(rows, "grp", k) for k in range(1, ng)], axis=0)
    digits = digit_list(nr)
    for shift, size in digits[1:] + digits[:1]:
        cur = jnp.concatenate([cur] + [swap(cur, "rep", j << shift) for j in range(1, size)], axis=0)
    return cur


def gather_start(shard):
    nr, ng = lax.axis_size("rep"), lax.axis_size("grp")
    rows = shard.shape[0] // nr
    me = lax.axis_index("rep")
    mine = lax.dynamic_slice_in_dim(shard, place_of(me, nr) * rows, rows, 0)
    got = [swap(mine, "grp", k) for k in range(1, ng)]
    if not got:
        return {}
    return spread(jnp.stack(got), nr)


def place_table():
    nr, ng = lax.axis_size("rep"), lax.axis_size("grp")
    me, member = lax.axis_index("rep"), lax.axis_index("grp")
    entries = [place_of(me ^ mask, nr) for mask in range(nr)] + [member ^ k for k in range(ng)]
    return jnp.stack([jnp.asarray(e, jnp.int32) for e in entries])


def reduce_rows(packed):
    nr, ng = lax.axis_size("rep"), lax.axis_size("grp")
    me, member = lax.axis_index("rep"), lax.axis_index("grp")
    cur = packed
    for shift, size in digit_list(nr):
        digit = (me >> shift) & (size - 1)
        cut = cur.reshape(ng, size, cur.shape[1] // size, D)
        got = [swap(pick(cut, digit ^ j, 1), "rep", j << shift) for j in range(1, size)]
        cur = add_low([pick(cut, digit, 1)] + got)
    got = [swap(pick(cur, member ^ k), "grp", k) for k in range(1, ng)]
    return add_low([pick(cur, member)] + got)


def assemble_shard_kernel(masks, table_ref, *refs):
    out_ref = refs[-1]
    for mask, ref in zip(masks, refs[:-1]):
        rows = ref.shape[0]
        out_ref[pl.ds(pl.multiple_of(table_ref[mask] * rows, rows), rows), :] = ref[...]


def in_vmem():
    return pl.BlockSpec(memory_space=pltpu.VMEM)


def assemble_shard(piece, table):
    nr = lax.axis_size("rep")
    pieces = spread(piece, nr)
    masks = tuple(sorted(pieces))
    return pl.pallas_call(
        functools.partial(assemble_shard_kernel, masks),
        in_specs=[pl.BlockSpec(memory_space=pltpu.SMEM)] + [in_vmem()] * len(masks),
        out_specs=in_vmem(),
        out_shape=sds((piece.shape[0] * nr, D), BF),
    )(table, *[pieces[m] for m in masks])


def assemble_kernel(masks, nr, layout, table_ref, shard_ref, *refs):
    pieces, rest = refs[: len(masks)], refs[len(masks) :]
    outs, full_ref = list(rest[:-1]), rest[-1]
    ng = full_ref.shape[0]
    full_ref[table_ref[nr]] = shard_ref[...]
    for mask, ref in zip(masks, pieces):
        rows = ref.shape[1]
        at = pl.ds(pl.multiple_of(table_ref[mask] * rows, rows), rows)
        for k in range(1, ng):
            full_ref[table_ref[nr + k], at, :] = ref[k - 1]
    step = D // ng
    for kind, start, size in layout:
        if kind == "rows":
            outs.pop(0)[...] = full_ref[:, start : start + size, :]
        elif kind == "blocks":
            out_ref = outs.pop(0)
            for g in range(ng):
                for c in range(size):
                    out_ref[step * g : step * (g + 1), D * c : D * (c + 1)] = full_ref[
                        g, start + step * c : start + step * (c + 1), :
                    ]
            flip_ref = outs.pop(0)
            flip_ref[...] = out_ref[...].T
        else:
            wo_ref, wg_ref = outs.pop(0), outs.pop(0)
            wide = (D + FF) // ng
            for g in range(ng):
                low, high = wide * g, wide * (g + 1)
                if low < D:
                    cut = min(high, D)
                    wo_ref[low:cut, :] = full_ref[g, start : start + cut - low, :]
                if high > D:
                    cut = max(low, D)
                    wg_ref[cut - D : high - D, :] = full_ref[g, start + cut - low : start + wide, :]
            outs.pop(0)[...] = wo_ref[...].T
            outs.pop(0)[...] = wg_ref[...].T


def assemble(shard, pieces, table, layout):
    nr, ng = lax.axis_size("rep"), lax.axis_size("grp")
    masks = tuple(sorted(pieces))
    out_shape = []
    for kind, _, size in layout:
        if kind == "rows":
            out_shape.append(sds((ng, size, D), BF))
        elif kind == "blocks":
            out_shape += [sds((D, size * D), BF), sds((size * D, D), BF)]
        else:
            out_shape += [sds(s, BF) for s in ((D, D), (FF, D), (D, D), (D, FF))]
    return pl.pallas_call(
        functools.partial(assemble_kernel, masks, nr, layout),
        in_specs=[pl.BlockSpec(memory_space=pltpu.SMEM)] + [in_vmem()] * (1 + len(masks)),
        out_specs=[in_vmem()] * len(out_shape),
        out_shape=out_shape,
        scratch_shapes=[pltpu.VMEM((ng,) + shard.shape, BF)],
        compiler_params=pltpu.CompilerParams(vmem_limit_bytes=VMEM_LIMIT),
    )(table, shard, *[pieces[m] for m in masks])


def pad_rows(x, multiple):
    short = -x.shape[0] % multiple
    return jnp.pad(x, ((0, short), (0, 0))) if short else x


def column_blocks(low, first, count):
    return [low[:, D * c : D * (c + 1)] for c in range(first, first + count)]


def local(
    latents, noise, timesteps, labels, emb_table, emb_mom, emb_ema, w_in, in_mom, in_ema,
    w_out, out_mom, out_ema, head, head_mom, head_ema,
):
    nr, ng = lax.axis_size("rep"), lax.axis_size("grp")
    member = lax.axis_index("grp")
    n = latents.shape[0]
    B = IMAGES_PER_STEP
    unit = 16 * nr
    rows_d = D // ng
    rows_out = (D + FF) // ng
    emb_rows = emb_table.shape[0]
    emb_pad = -(-emb_rows // 16) * 16
    low_emb, low_in, low_out, low_head = (a.astype(BF) for a in (emb_table, w_in, w_out, head))
    table = place_table()
    shard1 = pad_rows(
        jnp.concatenate([pad_rows(low_emb, 16)] + column_blocks(low_in[0], 0, 9), axis=0), unit
    )
    shard2 = pad_rows(jnp.concatenate([low_out[0]] + column_blocks(low_in[0], 9, 4), axis=0), unit)
    wy_block = jnp.pad(low_head[:, 2 * D :], ((0, 0), (0, D - PATCH_IN)))
    shard3 = pad_rows(
        jnp.concatenate(
            column_blocks(low_in[1], 0, 9) + column_blocks(low_head, 0, 2) + [wy_block], axis=0
        ),
        unit,
    )
    shard4 = pad_rows(jnp.concatenate([low_out[1]] + column_blocks(low_in[1], 9, 4), axis=0), unit)
    pieces1, pieces2, pieces3, pieces4 = (gather_start(s) for s in (shard1, shard2, shard3, shard4))

    levels = plan(timesteps)
    noise_level = jnp.sqrt(jnp.maximum(1.0 - levels, 0.0))
    noisy = (
        jnp.sqrt(levels)[:, None, None] * latents.astype(F32)
        + noise_level[:, None, None] * noise.astype(F32)
    ).astype(BF)
    time_feats = time_features(timesteps).astype(BF)
    one_hot = (labels[:, None] == jnp.arange(CLASSES, dtype=jnp.int32)[None, :]).astype(BF)
    pos = positions()

    emb3, wa0, wa0_t, wqkv0, wqkv0_t = assemble(
        shard1, pieces1, table,
        (("rows", 0, emb_pad), ("blocks", emb_pad, 6), ("blocks", emb_pad + 6 * rows_d, 3)),
    )
    emb_full = emb3[:, :emb_rows].reshape(ng * emb_rows, D)
    w_patch = emb_full[:PATCH_IN]
    w_time1 = emb_full[PATCH_IN : PATCH_IN + FREQ]
    w_time2 = emb_full[PATCH_IN + FREQ : PATCH_IN + FREQ + D]
    w_class = emb_full[PATCH_IN + FREQ + D :]
    pre_time = jnp.dot(time_feats, w_time1, preferred_element_type=F32)
    time_act = swish_act(pre_time).astype(BF)
    condition = jnp.dot(time_act, w_time2, preferred_element_type=F32) + jnp.dot(
        one_hot, w_class, preferred_element_type=F32
    )
    cond_act = swish_act(condition).astype(BF)

    def mods_of(weights_t):
        columns = lax.dot_general(
            weights_t, cond_act, (((1,), (1,)), ((), ())), preferred_element_type=F32
        )
        return jnp.pad(columns, ((0, 0), (0, 128 - n)))

    mods0 = mods_of(wa0_t)
    wp_t = w_patch.T
    wo0, wg0, wo0_t, wg0_t, wf0, wf0_t = assemble(
        shard2, pieces2, table, (("outer", 0, 0), ("blocks", rows_out, 4))
    )
    qkv0, lse0, att0, bra0, mid0 = att_forward(noisy, wp_t, pos, mods0, wqkv0_t, wo0_t, B)
    brb0, hid1 = ffn_forward(mid0, mods0, wf0_t, wg0_t, B)
    wa1, wa1_t, wqkv1, wqkv1_t, wm, wm_t, wy_wide, wy_wide_t = assemble(
        shard3, pieces3, table,
        (("blocks", 0, 6), ("blocks", 6 * rows_d, 3), ("blocks", 9 * rows_d, 2),
         ("blocks", 11 * rows_d, 1)),
    )
    wo1, wg1, wo1_t, wg1_t, wf1, wf1_t = assemble(
        shard4, pieces4, table, (("outer", 0, 0), ("blocks", rows_out, 4))
    )
    mods1 = mods_of(wa1_t)
    modf = mods_of(wm_t)
    wy = wy_wide[:, :PATCH_IN]
    wy_t = wy_wide_t[:PATCH_IN]
    entries = n * nr * ng * TOK * PATCH_IN
    outer_rows = -(-(rows_out + FF // ng + PATCH_IN) // unit) * unit
    qkv_rows = -(-(3 * rows_d + PATCH_IN) // unit) * unit
    outer_pack = (ng, outer_rows, D)
    qkv_pack = (ng, qkv_rows, D)
    qkv1, lse1, go1, gmid1, gm1, gmf, squares, pack_f1 = block_step(
        hid1, noise, mods1, modf, wqkv1_t, wo1_t, wf1_t, wg1_t, wo1, wf1, wg1, wy_t, wy,
        float(entries), B, outer_pack,
    )
    ghid1, gma1, pack_a1 = att_backward((hid1,), qkv1, lse1, go1, gmid1, mods1, wqkv1, B, False, qkv_pack)
    piece_f1 = reduce_rows(pack_f1)
    gm_rows1 = jnp.concatenate([gma1, gm1], axis=0)[:, :n].T
    gf_rows = gmf[:, :n].T
    loss_sum = jnp.sum(squares)
    loss_parts = []
    for _ in range(3):
        part = loss_sum.astype(BF)
        loss_parts.append(part)
        loss_sum = loss_sum - part.astype(F32)
    loss_row = jnp.stack(loss_parts)[None, :] * jnp.where(jnp.arange(n) == 0, 1.0, 0.0).astype(BF)[:, None]
    rows1 = gather_rows(
        jnp.concatenate([cond_act, gm_rows1.astype(BF), gf_rows.astype(BF), loss_row], axis=1)
    )
    go0, gmid0, gm0, pack_f0 = ffn_backward(
        ghid1, mid0, att0, bra0, brb0, mods0, wf0_t, wo0, wf0, wg0, B, outer_pack
    )
    piece_a1 = reduce_rows(pack_a1)
    gma0, pack_a0 = att_backward(
        (noisy, wp_t, pos), qkv0, lse0, go0, gmid0, mods0, wqkv0, B, True, qkv_pack
    )
    piece_f0 = reduce_rows(pack_f0)
    piece_a0 = reduce_rows(pack_a0)

    gm_rows0 = jnp.concatenate([gma0, gm0], axis=0)[:, :n].T

    def low_dot(left, right):
        return jnp.dot(left.astype(BF), right, preferred_element_type=F32)

    gcond_act = low_dot(gf_rows, wm_t) + low_dot(gm_rows1, wa1_t) + low_dot(gm_rows0, wa0_t)
    gcond = gcond_act * swish_slope(condition)
    gpre_time = low_dot(gcond, w_time2.T) * swish_slope(pre_time)
    label_parts = jnp.stack([labels >> 5, labels & 31], axis=1).astype(BF)
    rows0 = gather_rows(
        jnp.concatenate(
            [time_act, gcond.astype(BF), gpre_time.astype(BF), time_feats, gm_rows0.astype(BF), label_parts],
            axis=1,
        )
    )
    shard_f1, shard_a1, shard_f0, shard_a0 = (
        assemble_shard(piece, table) for piece in (piece_f1, piece_a1, piece_f0, piece_a0)
    )

    cond_all = lax.dynamic_slice_in_dim(rows1[:, :D], member * rows_d, rows_d, 1)

    def tall_dot(left, right):
        return lax.dot_general(left, right, (((0,), (0,)), ((), ())), preferred_element_type=F32)

    ga1 = tall_dot(cond_all, rows1[:, D : 7 * D])
    gm_head = tall_dot(cond_all, rows1[:, 7 * D : 9 * D])
    loss_value = jnp.sum(rows1[:, 9 * D :].astype(F32)) / entries
    at = 3 * D + FREQ
    ga0 = tall_dot(cond_all, rows0[:, at : at + 6 * D])
    split_labels = rows0[:, at + 6 * D :].astype(jnp.int32)
    all_labels = split_labels[:, 0] * 32 + split_labels[:, 1]
    class_hot = (all_labels[:, None] == jnp.arange(CLASSES, dtype=jnp.int32)[None, :]).astype(BF)
    left = jnp.concatenate(
        [jnp.zeros((rows0.shape[0], PATCH_IN), BF), rows0[:, 3 * D : at], rows0[:, :D], class_hot], axis=1
    )
    left = lax.dynamic_slice_in_dim(left, member * emb_rows, emb_rows, 1)
    row_id = member * emb_rows + jnp.arange(emb_rows, dtype=jnp.int32)
    emb_grad = jnp.where(
        (row_id < PATCH_IN + FREQ)[:, None],
        tall_dot(left, rows0[:, 2 * D : 3 * D]),
        tall_dot(left, rows0[:, D : 2 * D]),
    )
    patch_grad = shard_a0[3 * rows_d : 3 * rows_d + PATCH_IN].astype(F32)
    emb_grad = emb_grad + jnp.pad(patch_grad, ((0, emb_rows - PATCH_IN), (0, 0)))

    def wide(shard, start, count):
        blocks = shard[start : start + count * rows_d].reshape(count, rows_d, D)
        return blocks.transpose(1, 0, 2).reshape(rows_d, count * D).astype(F32)

    in_grad = jnp.stack(
        [
            jnp.concatenate([ga0, wide(shard_a0, 0, 3), wide(shard_f0, rows_out, 4)], axis=1),
            jnp.concatenate([ga1, wide(shard_a1, 0, 3), wide(shard_f1, rows_out, 4)], axis=1),
        ]
    )
    out_grad = jnp.stack([shard_f0[:rows_out], shard_f1[:rows_out]]).astype(F32)
    wy_rows = rows_out + FF // ng
    wy_grad = lax.dynamic_slice_in_dim(
        shard_f1[wy_rows : wy_rows + PATCH_IN], member * rows_d, rows_d, 1
    ).T.astype(F32)
    head_grad = jnp.concatenate([gm_head, wy_grad], axis=1)
    emb_new = advance(emb_table, emb_mom, emb_ema, emb_grad)
    in_new = advance(w_in, in_mom, in_ema, in_grad)
    out_new = advance(w_out, out_mom, out_ema, out_grad)
    head_new = advance(head, head_mom, head_ema, head_grad)
    return (loss_value, *emb_new, *in_new, *out_new, *head_new)


def solution(mesh):
    data = P(("rep", "grp"), None, None)
    vector = P(("rep", "grp"))
    flat = P("grp", None)
    deep = P(None, "grp", None)
    return jax.shard_map(
        local,
        mesh=mesh,
        in_specs=(data, data, vector, vector, flat, flat, flat, deep, deep, deep, deep, deep, deep,
                  flat, flat, flat),
        out_specs=(P(), flat, flat, flat, deep, deep, deep, deep, deep, deep, flat, flat, flat),
        check_vma=False,
    )
```

```python
import functools
import math

import jax
import jax.numpy as jnp
from jax import lax
from jax.experimental import pallas as pl
from jax.experimental.pallas import tpu as pltpu
from jax.sharding import PartitionSpec as P

D = 384
HEADS = 6
HEAD_DIM = 64
FF = 1536
TOK = 256
PATCH_IN = 16
EPSILON = 1e-06
BF = jnp.bfloat16
F32 = jnp.float32
VMEM_LIMIT = 58 * 1024 * 1024


def mm(left, right):
    return lax.dot_general(left, right, (((1,), (0,)), ((), ())), preferred_element_type=F32)


def mm_nt(left, right):
    return lax.dot_general(left, right, (((1,), (1,)), ((), ())), preferred_element_type=F32)


def norm_parts(x):
    centered = x - jnp.mean(x, axis=0, keepdims=True)
    variance = jnp.mean(centered * centered, axis=0, keepdims=True)
    inv = lax.rsqrt(variance + EPSILON)
    return centered * inv, inv


def norm_back(d, normed, inv, scale1):
    dn = d * scale1
    m1 = jnp.mean(dn, axis=0, keepdims=True)
    m2 = jnp.mean(dn * normed, axis=0, keepdims=True)
    return (dn - m1 - normed * m2) * inv


def column(mods_ref, index, image):
    block = mods_ref[pl.ds(index * D, D), :]
    lane = lax.broadcasted_iota(jnp.int32, block.shape, 1)
    return jnp.sum(jnp.where(lane == image, block, 0.0), axis=1, keepdims=True)


def put_column(out_ref, index, image, values):
    total = jnp.sum(values, axis=1, keepdims=True)
    rows = pl.ds(index * D, D)
    old = out_ref[rows, :]
    lane = lax.broadcasted_iota(jnp.int32, old.shape, 1)
    out_ref[rows, :] = jnp.where(lane == image, total, old)


def half_zero(x, half):
    row = lax.broadcasted_iota(jnp.int32, x.shape, 0)
    keep = row < HEAD_DIM if half == 0 else row >= HEAD_DIM
    return jnp.where(keep, x, jnp.zeros_like(x))


def attention_forward(qkv_ref, b, lse_ref, att_ref, att_lanes):
    for pair in range(HEADS // 2):
        lo = 2 * HEAD_DIM * pair
        q2 = qkv_ref[b, lo : lo + 128, :]
        k2 = qkv_ref[b, D + lo : D + lo + 128, :].T
        for half in range(2):
            head = 2 * pair + half
            scores = mm(k2, half_zero(q2, half))
            peak = jnp.max(scores, axis=0, keepdims=True)
            exps = jnp.exp(scores - peak)
            total = jnp.sum(exps, axis=0, keepdims=True)
            vrow = 2 * D + HEAD_DIM * head
            out = mm(qkv_ref[b, vrow : vrow + HEAD_DIM, :], exps.astype(BF))
            att_ref[HEAD_DIM * head : HEAD_DIM * (head + 1), att_lanes] = (
                out * (1.0 / total)
            ).astype(BF)
            lse_ref[b, head : head + 1, :] = peak + jnp.log(total)


def attention_backward(qkv_ref, b, lse_ref, go_ref, gqkv_ref, lanes):
    for pair in range(HEADS // 2):
        lo = 2 * HEAD_DIM * pair
        q2 = qkv_ref[b, lo : lo + 128, :]
        k2 = qkv_ref[b, D + lo : D + lo + 128, :].T
        v2 = qkv_ref[b, 2 * D + lo : 2 * D + lo + 128, :].T
        g2 = go_ref[b, lo : lo + 128, :]
        for half in range(2):
            head = 2 * pair + half
            row = HEAD_DIM * head
            scores = mm(k2, half_zero(q2, half))
            probs = jnp.exp(scores - lse_ref[b, head : head + 1, :])
            gprobs = mm(v2, half_zero(g2, half))
            inner = jnp.sum(probs * gprobs, axis=0, keepdims=True)
            gscores = (probs * (gprobs - inner)).astype(BF)
            gq = mm(qkv_ref[b, D + row : D + row + HEAD_DIM, :], gscores)
            gk = mm_nt(qkv_ref[b, row : row + HEAD_DIM, :], gscores)
            gv = mm_nt(go_ref[b, row : row + HEAD_DIM, :], probs.astype(BF))
            gqkv_ref[row : row + HEAD_DIM, lanes] = (gq * (1.0 / math.sqrt(HEAD_DIM))).astype(BF)
            gqkv_ref[D + row : D + row + HEAD_DIM, lanes] = gk.astype(BF)
            gqkv_ref[2 * D + row : 2 * D + row + HEAD_DIM, lanes] = gv.astype(BF)


def project_qkv(wqkv_t_ref, normed_ref, lanes, qkv_ref, b):
    qkv = mm(wqkv_t_ref[...], normed_ref[:, lanes])
    qkv_ref[b, 0:D, :] = (qkv[0:D] * (1.0 / math.sqrt(HEAD_DIM))).astype(BF)
    qkv_ref[b, D:, :] = qkv[D:].astype(BF)


GELU_C = 0.7978845608
GELU_A = 0.044715


def gelu_both(v):
    square = v * v
    t = jnp.tanh(v * (GELU_C + (GELU_C * GELU_A) * square))
    half = 0.5 + 0.5 * t
    slope = half + 0.5 * v * (1.0 - t * t) * (GELU_C + (3.0 * GELU_C * GELU_A) * square)
    return v * half, slope


def gelu_one(v):
    t = jnp.tanh(v * (GELU_C + (GELU_C * GELU_A) * (v * v)))
    return v * (0.5 + 0.5 * t)


def accumulate(acc_ref, value, first):
    @pl.when(first)
    def _():
        acc_ref[...] = value

    @pl.when(jnp.logical_not(first))
    def _():
        acc_ref[...] += value


FF_CHUNK = 512


def pack_blocks(pack_ref, start, value):
    members = pack_ref.shape[0]
    rows = D // members
    count = value.shape[1] // D
    for g in range(members):
        for c in range(count):
            pack_ref[g, start + rows * c : start + rows * (c + 1), :] = value[
                rows * g : rows * (g + 1), D * c : D * (c + 1)
            ].astype(BF)
    return start + rows * count


def pack_outer(pack_ref, awo_ref, awf_ref, awg_ref):
    members = pack_ref.shape[0]
    rows = (D + FF) // members
    for g in range(members):
        low, high = rows * g, rows * (g + 1)
        if low < D:
            cut = min(high, D)
            pack_ref[g, 0 : cut - low, :] = awo_ref[low:cut, :].astype(BF)
        if high > D:
            cut = max(low, D)
            pack_ref[g, cut - low : rows, :] = awg_ref[cut - D : high - D, :].astype(BF)
    return pack_blocks(pack_ref, rows, awf_ref)


def pack_rest(pack_ref, used, extra):
    if extra is not None:
        for g in range(pack_ref.shape[0]):
            pack_ref[g, used : used + PATCH_IN, :] = extra.astype(BF)
        used += PATCH_IN
    if used < pack_ref.shape[1]:
        pack_ref[:, used:, :] = jnp.zeros_like(pack_ref[:, used:, :])


def split_pack(pack_ref, table_ref, offset, outs):
    for j, out_ref in enumerate(outs):
        rows = out_ref.shape[1]
        at = pl.multiple_of(table_ref[offset + j] * rows, rows)
        out_ref[...] = pack_ref[:, pl.ds(at, rows), :]


def att_fwd_kernel(B, offset, held, noisy_ref, wp_t_ref, pos_ref, mods_ref, wqkv_t_ref, *refs):
    qkv_ref, lse_ref, att_out_ref, normed_ref, att_ref = refs[held:]
    step = pl.program_id(0)
    for b in range(B):
        image = (offset + step) * B + b
        lanes = slice(TOK * b, TOK * (b + 1))
        hidden = mm(wp_t_ref[...], noisy_ref[b]) + pos_ref[...]
        normed, _ = norm_parts(hidden)
        normed_ref[:, lanes] = (
            normed * (1.0 + column(mods_ref, 1, image)) + column(mods_ref, 0, image)
        ).astype(BF)
        project_qkv(wqkv_t_ref, normed_ref, lanes, qkv_ref, b)
        attention_forward(qkv_ref, b, lse_ref, att_ref, lanes)
        att_out_ref[b] = att_ref[:, lanes]


def ffn_fwd_kernel(B, noisy_ref, wp_t_ref, pos_ref, att_ref, mods_a_ref, mods_b_ref, wo_t_ref, wf_t_ref,
                   wg_t_ref, mid_ref, bra_ref, brb_ref, hid_ref, normed_ref):
    step = pl.program_id(0)
    for b in range(B):
        image = step * B + b
        lanes = slice(TOK * b, TOK * (b + 1))
        hidden = mm(wp_t_ref[...], noisy_ref[b]) + pos_ref[...]
        branch_a = mm(wo_t_ref[...], att_ref[b])
        bra_ref[b] = branch_a
        mid = hidden + column(mods_a_ref, 2, image) * branch_a
        mid_ref[b] = mid
        normed, _ = norm_parts(mid)
        normed_ref[:, lanes] = (
            normed * (1.0 + column(mods_b_ref, 1, image)) + column(mods_b_ref, 0, image)
        ).astype(BF)
        branch = None
        for f in range(0, FF, FF_CHUNK):
            pre = mm(wf_t_ref[f : f + FF_CHUNK, :], normed_ref[:, lanes])
            part = mm(wg_t_ref[:, f : f + FF_CHUNK], gelu_one(pre).astype(BF))
            branch = part if branch is None else branch + part
        brb_ref[b] = branch
        hid_ref[b] = mid + column(mods_b_ref, 2, image) * branch


def out_bwd(b, image, lanes, gmid, branch, gate, wo_ref, gba_ref, go_ref, gm_ref, gm_base):
    put_column(gm_ref, gm_base, image, gmid * branch)
    gba_ref[:, lanes] = (gate * gmid).astype(BF)
    go_ref[b] = mm(wo_ref[...], gba_ref[:, lanes]).astype(BF)


def block_kernel(B, entries, table_ref, hid_ref, noise_ref, mods_ref, modf_ref, wqkv_t_ref, wo_t_ref, wf_t_ref,
                 wg_t_ref, wo_ref, wf_ref, wg_ref, wy_t_ref, wy_ref, cond_ref,
                 qkv_ref, lse_ref, go_ref, gmid_ref, gm_ref, gmf_ref, loss_ref,
                 keep_ref, send_ref,
                 pack_ref, normed_ref, att_ref, slope_ref, act_ref, gpre_ref, gba_ref, gbb_ref, normf_ref, gout_ref,
                 awo_ref, awf_ref, awg_ref, awy_ref):
    step = pl.program_id(0)
    first = step == 0

    @pl.when(first)
    def _():
        gm_ref[...] = jnp.zeros_like(gm_ref)
        gmf_ref[...] = jnp.zeros_like(gmf_ref)
        loss_ref[...] = jnp.zeros_like(loss_ref)

    for b in range(B):
        image = step * B + b
        lanes = slice(TOK * b, TOK * (b + 1))
        hidden = hid_ref[b]
        normed, _ = norm_parts(hidden)
        normed_ref[:, lanes] = (
            normed * (1.0 + column(mods_ref, 1, image)) + column(mods_ref, 0, image)
        ).astype(BF)
        project_qkv(wqkv_t_ref, normed_ref, lanes, qkv_ref, b)
        attention_forward(qkv_ref, b, lse_ref, att_ref, lanes)
        branch_a = mm(wo_t_ref[...], att_ref[:, lanes])
        gate_a = column(mods_ref, 2, image)
        mid = hidden + gate_a * branch_a
        normed_b, inv_b = norm_parts(mid)
        scale_b = 1.0 + column(mods_ref, 4, image)
        normed_ref[:, lanes] = (normed_b * scale_b + column(mods_ref, 3, image)).astype(BF)
        branch_b = None
        for f in range(0, FF, FF_CHUNK):
            rows = slice(f, f + FF_CHUNK)
            pre = mm(wf_t_ref[rows, :], normed_ref[:, lanes])
            act, slope = gelu_both(pre)
            slope_ref[rows, :] = slope
            act_ref[rows, lanes] = act.astype(BF)
            part = mm(wg_t_ref[:, rows], act_ref[rows, lanes])
            branch_b = part if branch_b is None else branch_b + part
        gate_b = column(mods_ref, 5, image)
        hidden2 = mid + gate_b * branch_b
        normed_f, inv_f = norm_parts(hidden2)
        scale_f = 1.0 + column(modf_ref, 1, image)
        normf_ref[:, lanes] = (normed_f * scale_f + column(modf_ref, 0, image)).astype(BF)
        residue = mm(wy_t_ref[...], normf_ref[:, lanes]) - noise_ref[b].astype(F32)
        loss_ref[...] += residue * residue
        gout_ref[:, lanes] = ((2.0 / entries) * residue).astype(BF)
        gnf = mm(wy_ref[...], gout_ref[:, lanes])
        put_column(gmf_ref, 0, image, gnf)
        put_column(gmf_ref, 1, image, gnf * normed_f)
        ghid = norm_back(gnf, normed_f, inv_f, scale_f)
        put_column(gm_ref, 3, image, ghid * branch_b)
        gbb_ref[:, lanes] = (gate_b * ghid).astype(BF)
        gnb = None
        for f in range(0, FF, FF_CHUNK):
            rows = slice(f, f + FF_CHUNK)
            gact = mm(wg_ref[rows, :], gbb_ref[:, lanes])
            gpre_ref[rows, lanes] = (gact * slope_ref[rows, :]).astype(BF)
            part = mm(wf_ref[:, rows], gpre_ref[rows, lanes])
            gnb = part if gnb is None else gnb + part
        put_column(gm_ref, 1, image, gnb)
        put_column(gm_ref, 2, image, gnb * normed_b)
        gmid = ghid + norm_back(gnb, normed_b, inv_b, scale_b)
        gmid_ref[b] = gmid
        out_bwd(b, image, lanes, gmid, branch_a, gate_a, wo_ref, gba_ref, go_ref, gm_ref, 0)
    accumulate(awo_ref, mm_nt(att_ref[...], gba_ref[...]), first)
    accumulate(awf_ref, mm_nt(normed_ref[...], gpre_ref[...]), first)
    accumulate(awg_ref, mm_nt(act_ref[...], gbb_ref[...]), first)
    accumulate(awy_ref, mm_nt(gout_ref[...], normf_ref[...]), first)

    @pl.when(step == pl.num_programs(0) - 1)
    def _():
        used = pack_outer(pack_ref, awo_ref, awf_ref, awg_ref)
        used = pack_blocks(pack_ref, used, mm_nt(cond_ref[...], gm_ref[...].astype(BF)))
        pack_rest(pack_ref, used, awy_ref[...])
        split_pack(pack_ref, table_ref, 0, (keep_ref, send_ref))


def ffn_bwd_kernel(B, table_ref, ghid_ref, mid_ref, att_ref, bra_ref, brb_ref, mods_a_ref, mods_b_ref, wf_t_ref, wo_ref, wf_ref,
                   wg_ref, cond_ref, go_ref, gmid_ref, gm_ref, keep_ref, send_ref, pack_ref,
                   normed_ref, act_ref, gpre_ref, gba_ref, gbb_ref, atts_ref, awo_ref, awf_ref, awg_ref):
    step = pl.program_id(0)
    first = step == 0

    @pl.when(first)
    def _():
        gm_ref[...] = jnp.zeros_like(gm_ref)

    for b in range(B):
        image = step * B + b
        lanes = slice(TOK * b, TOK * (b + 1))
        ghid = ghid_ref[b]
        put_column(gm_ref, 3, image, ghid * brb_ref[b])
        gbb_ref[:, lanes] = (column(mods_b_ref, 2, image) * ghid).astype(BF)
        normed_b, inv_b = norm_parts(mid_ref[b])
        scale_b = 1.0 + column(mods_b_ref, 1, image)
        normed_ref[:, lanes] = (normed_b * scale_b + column(mods_b_ref, 0, image)).astype(BF)
        atts_ref[:, lanes] = att_ref[b]
        gnb = None
        for f in range(0, FF, FF_CHUNK):
            rows = slice(f, f + FF_CHUNK)
            act, slope = gelu_both(mm(wf_t_ref[rows, :], normed_ref[:, lanes]))
            act_ref[rows, lanes] = act.astype(BF)
            gact = mm(wg_ref[rows, :], gbb_ref[:, lanes])
            gpre_ref[rows, lanes] = (gact * slope).astype(BF)
            part = mm(wf_ref[:, rows], gpre_ref[rows, lanes])
            gnb = part if gnb is None else gnb + part
        put_column(gm_ref, 1, image, gnb)
        put_column(gm_ref, 2, image, gnb * normed_b)
        gmid = ghid + norm_back(gnb, normed_b, inv_b, scale_b)
        gmid_ref[b] = gmid
        out_bwd(b, image, lanes, gmid, bra_ref[b], column(mods_a_ref, 2, image), wo_ref, gba_ref, go_ref,
                gm_ref, 0)
    accumulate(awo_ref, mm_nt(atts_ref[...], gba_ref[...]), first)
    accumulate(awf_ref, mm_nt(normed_ref[...], gpre_ref[...]), first)
    accumulate(awg_ref, mm_nt(act_ref[...], gbb_ref[...]), first)

    @pl.when(step == pl.num_programs(0) - 1)
    def _():
        used = pack_outer(pack_ref, awo_ref, awf_ref, awg_ref)
        used = pack_blocks(pack_ref, used, mm_nt(cond_ref[...], gm_ref[...].astype(BF)))
        pack_rest(pack_ref, used, None)
        split_pack(pack_ref, table_ref, 0, (keep_ref, send_ref))


def att_bwd_kernel(B, offset, bottom, opens, closes, *refs):
    refs = list(refs)
    take = lambda count: [refs.pop(0) for _ in range(count)]
    (table_ref,) = take(1)
    noisy_ref, wp_t_ref, pos_ref = take(3) if bottom else (None, None, None)
    (hid_ref,) = (None,) if bottom else take(1)
    qkv_ref, lse_ref, go_ref, gmid_ref, mods_ref, wqkv_ref, cond_ref = take(7)
    (gmf_ref,) = (None,) if bottom else take(1)
    before = take(3 if bottom else 2) if not opens else []
    (ghid_ref,) = (None,) if bottom else take(1)
    (gm_ref,) = take(1)
    sums = 2 if bottom else 1
    keep_ref, send_ref, pack_ref, accs = None, None, None, None
    if closes:
        keep_ref, send_ref = take(2)
    else:
        accs = take(sums)
    if closes:
        (pack_ref,) = take(1)
    normed_ref, gqkv_ref = take(2)
    tok_ref, noi_ref = take(2) if bottom else (None, None)
    if closes:
        accs = take(sums)
    step = pl.program_id(0)
    first = step == 0

    @pl.when(first)
    def _():
        if opens:
            gm_ref[...] = jnp.zeros_like(gm_ref)
            for acc_ref in accs:
                acc_ref[...] = jnp.zeros_like(acc_ref)
        else:
            for to_ref, from_ref in zip([gm_ref] + accs, before):
                to_ref[...] = from_ref[...]

    for b in range(B):
        image = (offset + step) * B + b
        lanes = slice(TOK * b, TOK * (b + 1))
        hidden = mm(wp_t_ref[...], noisy_ref[b]) + pos_ref[...] if bottom else hid_ref[b]
        normed, inv = norm_parts(hidden)
        scale = 1.0 + column(mods_ref, 1, image)
        normed_ref[:, lanes] = (normed * scale + column(mods_ref, 0, image)).astype(BF)
        attention_backward(qkv_ref, b, lse_ref, go_ref, gqkv_ref, lanes)
        gna = mm(wqkv_ref[...], gqkv_ref[:, lanes])
        put_column(gm_ref, 0, image, gna)
        put_column(gm_ref, 1, image, gna * normed)
        ghid = gmid_ref[b] + norm_back(gna, normed, inv, scale)
        if bottom:
            tok_ref[:, lanes] = ghid.astype(BF)
            noi_ref[:, lanes] = noisy_ref[b]
        else:
            ghid_ref[b] = ghid
    accs[0][...] += mm_nt(normed_ref[...], gqkv_ref[...])
    if bottom:
        accs[1][...] += mm_nt(noi_ref[...], tok_ref[...])

    if closes:
        @pl.when(step == pl.num_programs(0) - 1)
        def _():
            used = pack_blocks(pack_ref, 0, accs[0])
            used = pack_blocks(pack_ref, used, mm_nt(cond_ref[...], gm_ref[...].astype(BF)))
            if not bottom:
                used = pack_blocks(pack_ref, used, mm_nt(cond_ref[...], gmf_ref[...].astype(BF)))
            pack_rest(pack_ref, used, accs[1][...] if bottom else None)
            split_pack(pack_ref, table_ref, 0, (keep_ref, send_ref))


def whole(*shape):
    return pl.BlockSpec(shape, lambda i: (0,) * len(shape))


def images(B, *shape, offset=0):
    return pl.BlockSpec((B,) + shape, lambda i: (i + offset,) + (0,) * len(shape))


def sds(shape, dtype):
    return jax.ShapeDtypeStruct(shape, dtype)


def run_kernel(kernel, steps, in_specs, outs, scratch, flops, args, aliases=None):
    out_specs = [spec for spec, _, _ in outs]
    out_shape = [sds(shape, dtype) for _, shape, dtype in outs]
    moved = sum(a.size * a.dtype.itemsize for a in args) + sum(
        math.prod(o.shape) * o.dtype.itemsize for o in out_shape
    )
    return pl.pallas_call(
        kernel,
        grid=(steps,),
        in_specs=in_specs,
        out_specs=out_specs,
        out_shape=out_shape,
        scratch_shapes=[pltpu.VMEM(shape, dtype) for shape, dtype in scratch],
        input_output_aliases=aliases or {},
        compiler_params=pltpu.CompilerParams(vmem_limit_bytes=VMEM_LIMIT),
        cost_estimate=pl.CostEstimate(flops=8 * flops, bytes_accessed=moved, transcendentals=0),
    )(*args)


MODS = whole(6 * D, 128)
HALF_MODS = whole(3 * D, 128)
COND = whole(D, 128)
SCALARS = pl.BlockSpec(memory_space=pltpu.SMEM)


def halves(pack):
    ng, rows, _ = pack
    half = (ng, rows // 2, D)
    return [(whole(*half), half, BF)] * 2


def att_forward(noisy, wp_t, pos, mods, wqkv_t, B, part, parts, before):
    n = noisy.shape[0]
    T = B * TOK
    steps = n // B // parts
    here = functools.partial(images, B, offset=part * steps)
    return run_kernel(
        functools.partial(att_fwd_kernel, B, part * steps, len(before)), steps,
        [here(PATCH_IN, TOK), whole(D, PATCH_IN), whole(D, TOK), HALF_MODS, whole(3 * D, D)]
        + [pl.BlockSpec(memory_space=pl.ANY)] * len(before),
        [(here(3 * D, TOK), (n, 3 * D, TOK), BF), (here(8, TOK), (n, 8, TOK), F32),
         (here(D, TOK), (n, D, TOK), BF)],
        [((D, T), BF), ((D, T), BF)],
        2 * n * TOK * (3 * D * D + 2 * D * TOK) // parts, (noisy, wp_t, pos, mods, wqkv_t) + tuple(before),
        aliases={5 + i: i for i in range(len(before))})


def ffn_forward(noisy, wp_t, pos, att, mods_a, mods_b, wo_t, wf_t, wg_t, B):
    n = noisy.shape[0]
    T = B * TOK
    full = images(B, D, TOK)
    return run_kernel(
        functools.partial(ffn_fwd_kernel, B), n // B,
        [images(B, PATCH_IN, TOK), whole(D, PATCH_IN), whole(D, TOK), full, HALF_MODS, HALF_MODS, whole(D, D),
         whole(FF, D), whole(D, FF)],
        [(full, (n, D, TOK), F32)] * 4,
        [((D, T), BF)],
        2 * n * TOK * (2 * D * FF + D * D), (noisy, wp_t, pos, att, mods_a, mods_b, wo_t, wf_t, wg_t))


def block_step(table, hid, noise, mods, modf, wqkv_t, wo_t, wf_t, wg_t, wo, wf, wg, wy_t, wy, cond, entries, B, pack):
    n = hid.shape[0]
    T = B * TOK
    full = images(B, D, TOK)
    return run_kernel(
        functools.partial(block_kernel, B, entries), n // B,
        [SCALARS, full, images(B, PATCH_IN, TOK), MODS, whole(2 * D, 128), whole(3 * D, D), whole(D, D),
         whole(FF, D), whole(D, FF), whole(D, D), whole(D, FF), whole(FF, D), whole(PATCH_IN, D),
         whole(D, PATCH_IN), COND],
        [(images(B, 3 * D, TOK), (n, 3 * D, TOK), BF), (images(B, 8, TOK), (n, 8, TOK), F32),
         (full, (n, D, TOK), BF), (full, (n, D, TOK), F32),
         (whole(4 * D, 128), (4 * D, 128), F32), (whole(2 * D, 128), (2 * D, 128), F32),
         (whole(PATCH_IN, TOK), (PATCH_IN, TOK), F32)] + halves(pack),
        [(pack, BF), ((D, T), BF), ((D, T), BF), ((FF, TOK), F32), ((FF, T), BF), ((FF, T), BF), ((D, T), BF),
         ((D, T), BF), ((D, T), BF), ((PATCH_IN, T), BF), ((D, D), F32), ((D, FF), F32), ((FF, D), F32),
         ((PATCH_IN, D), F32)],
        2 * n * TOK * (4 * D * D + 2 * D * TOK + 6 * D * FF + 2 * D * D),
        (table, hid, noise, mods, modf, wqkv_t, wo_t, wf_t, wg_t, wo, wf, wg, wy_t, wy, cond))


def ffn_backward(table, ghid, mid, att, bra, brb, mods_a, mods_b, wf_t, wo, wf, wg, cond, B, pack):
    n = mid.shape[0]
    T = B * TOK
    full = images(B, D, TOK)
    return run_kernel(
        functools.partial(ffn_bwd_kernel, B), n // B,
        [SCALARS, full, full, full, full, full, HALF_MODS, HALF_MODS, whole(FF, D), whole(D, D), whole(D, FF),
         whole(FF, D), COND],
        [(full, (n, D, TOK), BF), (full, (n, D, TOK), F32), (whole(4 * D, 128), (4 * D, 128), F32)] + halves(pack),
        [(pack, BF), ((D, T), BF), ((FF, T), BF), ((FF, T), BF), ((D, T), BF), ((D, T), BF), ((D, T), BF),
         ((D, D), F32), ((D, FF), F32), ((FF, D), F32)],
        2 * n * TOK * (5 * D * FF + 2 * D * D),
        (table, ghid, mid, att, bra, brb, mods_a, mods_b, wf_t, wo, wf, wg, cond))


def att_backward(table, source, qkv, lse, go, gmid, mods, wqkv, cond, gmf, B, bottom, pack, part=0, parts=1, before=()):
    n = qkv.shape[0]
    T = B * TOK
    steps = n // B // parts
    offset = part * steps
    opens, closes = part == 0, part == parts - 1
    here = functools.partial(images, B, offset=offset)
    full = here(D, TOK)
    gm = (whole(2 * D, 128), (2 * D, 128), F32)
    sums = [(whole(D, 3 * D), (D, 3 * D), F32)] + ([(whole(PATCH_IN, D), (PATCH_IN, D), F32)] if bottom else [])
    ins = [SCALARS] + ([here(PATCH_IN, TOK), whole(D, PATCH_IN), whole(D, TOK)] if bottom else [full])
    ins += [here(3 * D, TOK), here(8, TOK), full, full, HALF_MODS if bottom else MODS, whole(D, 3 * D), COND]
    ins += [] if bottom else [whole(2 * D, 128)]
    args = (table,) + tuple(source) + (qkv, lse, go, gmid, mods, wqkv, cond) + (() if bottom else (gmf,))
    if not opens:
        ins += [gm[0]] + [s[0] for s in sums]
        args += tuple(before)
    outs = ([] if bottom else [(full, (n, D, TOK), F32)]) + [gm] + (halves(pack) if closes else sums)
    scratch = ([(pack, BF)] if closes else []) + [((D, T), BF), ((3 * D, T), BF)]
    scratch += [((D, T), BF), ((PATCH_IN, T), BF)] if bottom else []
    scratch += [(s[1], F32) for s in sums] if closes else []
    return run_kernel(
        functools.partial(att_bwd_kernel, B, offset, bottom, opens, closes), steps, ins, outs, scratch,
        2 * n * TOK * (6 * D * D + 5 * D * TOK) // parts, args)


FREQ = 256
CLASSES = 1000
GRID = 16
LAYERS = 2
MOMENTUM = 0.9
LEARN = 30.0
DECAY = 0.7
IMAGES_PER_STEP = 2
SMALL_COST = 8 * 10**9


def plan(steps_in):
    anchor = math.cos(0.5 * math.pi * 0.008 / 1.008)
    fraction = (steps_in.astype(F32) / 1000.0 + 0.008) / 1.008
    levels = jnp.cos(0.5 * math.pi * fraction)
    return levels * levels / (anchor * anchor)


def time_features(steps_in):
    half_width = FREQ // 2
    frequencies = jnp.exp(-math.log(10000.0) * jnp.arange(half_width, dtype=F32) / half_width)
    angles = steps_in.astype(F32)[:, None] * frequencies[None, :]
    return jnp.concatenate([jnp.cos(angles), jnp.sin(angles)], axis=1)


def positions():
    quarter = D // 4
    omegas = jnp.exp(-math.log(10000.0) * jnp.arange(quarter, dtype=F32) / quarter)
    places = jnp.arange(GRID * GRID, dtype=jnp.int32)
    column = omegas[:, None] * (places % GRID).astype(F32)[None, :]
    row_pos = omegas[:, None] * (places // GRID).astype(F32)[None, :]
    return jnp.concatenate(
        [jnp.sin(column), jnp.cos(column), jnp.sin(row_pos), jnp.cos(row_pos)], axis=0
    )


def swish_parts(values):
    s = 1.0 / (1.0 + jnp.exp(-values))
    return values * s, s * (1.0 + values * (1.0 - s))


def advance(weight, moment, average, gradient):
    new_moment = MOMENTUM * moment + gradient
    new_weight = weight - LEARN * (gradient + MOMENTUM * new_moment)
    new_average = DECAY * average + (1.0 - DECAY) * new_weight
    return (new_weight, new_moment, new_average)


def after(x, *others):
    return lax.optimization_barrier((x,) + others)[0]


def swap(x, axis, mask):
    pairs = [(i, i ^ mask) for i in range(lax.axis_size(axis))]
    return lax.ppermute(x, axis, pairs)


def digit_list(n):
    found, shift = [], 0
    while (1 << shift) < n:
        left = n >> shift
        size = 2 if shift == 0 or left == 2 else 4
        found.append((shift, size))
        shift += size.bit_length() - 1
    return found


def place_of(index, n):
    place = 0
    for shift, size in digit_list(n):
        place = place * size + ((index >> shift) & (size - 1))
    return place


def place_table(emb_rows):
    nr, ng = lax.axis_size("rep"), lax.axis_size("grp")
    me, member = lax.axis_index("rep"), lax.axis_index("grp")
    entries, offsets = [], {}
    for shift, size in digit_list(nr):
        offsets[shift] = len(entries)
        entries += [((me >> shift) & (size - 1)) ^ j for j in range(size)]
    if not entries:
        entries = [0, 1]
    offsets["place"] = len(entries)
    entries += [place_of(me ^ mask, nr) for mask in range(nr)]
    offsets["member"] = len(entries)
    entries += [member ^ k for k in range(ng)]
    offsets["lead"] = len(entries)
    entries.append(emb_rows * member % 16)
    return jnp.stack([jnp.asarray(e, jnp.int32) for e in entries]), offsets


def in_vmem():
    return pl.BlockSpec(memory_space=pltpu.VMEM)


def small_kernel(kernel, outs, scratch, args, scalars=1):
    return pl.pallas_call(
        kernel,
        in_specs=[SCALARS] * scalars + [in_vmem()] * (len(args) - scalars),
        out_specs=[in_vmem()] * len(outs),
        out_shape=[sds(shape, dtype) for shape, dtype in outs],
        scratch_shapes=[pltpu.VMEM(shape, dtype) for shape, dtype in scratch],
        compiler_params=pltpu.CompilerParams(vmem_limit_bytes=VMEM_LIMIT),
        cost_estimate=pl.CostEstimate(flops=SMALL_COST, bytes_accessed=0, transcendentals=0),
    )(*args)


def spread_outer(piece, n):
    pieces = [((0,), piece)]
    digits = digit_list(n)[1:]
    for shift, size in digits:
        if len(pieces) > 1:
            pieces = [(sum((m for m, _ in pieces), ()), jnp.concatenate([v for _, v in pieces], axis=0))]
        masks, value = pieces[0]
        pieces = pieces + [
            (tuple(m ^ (j << shift) for m in masks), swap(value, "rep", j << shift)) for j in range(1, size)
        ]
    return pieces


def spread_core(pieces, n):
    if n == 1:
        return pieces
    return pieces + [(tuple(m ^ 1 for m in masks), swap(value, "rep", 1)) for masks, value in pieces]


def gather_members(mine):
    got = [swap(mine, "grp", k) for k in range(1, lax.axis_size("grp"))]
    return jnp.concatenate(got, axis=0) if got else None


def sum_parts(parts):
    total = parts[0][...].astype(F32)
    for part in parts[1:]:
        total = total + part[...].astype(F32)
    return total.astype(BF)


def rows_kernel(count, offset, table_ref, *refs):
    parts, outs, total_ref = refs[:count], refs[count:-1], refs[-1]
    total_ref[...] = sum_parts(parts)
    split_pack(total_ref, table_ref, offset, outs)


def members_kernel(counts, offset, has_extra, table_ref, *refs):
    refs = list(refs)
    groups = [[refs.pop(0) for _ in range(c)] for c in counts]
    extra_ref = refs.pop(0) if has_extra else None
    outs, totals = refs[: -len(counts)], refs[-len(counts) :]
    for parts, total_ref in zip(groups, totals):
        total_ref[...] = sum_parts(parts)
    for k, out_ref in enumerate(outs):
        at = 0
        for total_ref in totals:
            rows = total_ref.shape[1]
            out_ref[at : at + rows, :] = total_ref[table_ref[offset + k]]
            at += rows
        if has_extra:
            out_ref[at:, :] = extra_ref[...]


def last_kernel(count, extra, table_ref, *refs):
    parts, out_ref = refs[:count], refs[-1]
    rows = parts[0].shape[0] - extra
    total = parts[0][0:rows, :].astype(F32)
    for part in parts[1:]:
        total = total + part[0:rows, :].astype(F32)
    out_ref[0:rows, :] = total.astype(BF)
    if extra:
        for i, part in enumerate(parts):
            out_ref[rows + extra * i : rows + extra * (i + 1), :] = part[rows:, :]


def reduce_first(keep, send):
    return [keep, swap(send, "rep", 1)] if lax.axis_size("rep") > 1 else [keep]


def reduce_outer(parts, table, offsets, number):
    shift, size = digit_list(lax.axis_size("rep"))[number]
    ng, rows, _ = parts[0].shape
    one = lambda r: pl.BlockSpec((1, r, D), lambda i: (i, 0, 0))
    cut = pl.pallas_call(
        functools.partial(rows_kernel, len(parts), offsets[shift]),
        grid=(ng,),
        in_specs=[SCALARS] + [one(rows)] * len(parts),
        out_specs=[one(rows // size)] * size,
        out_shape=[sds((ng, rows // size, D), BF)] * size,
        scratch_shapes=[pltpu.VMEM((1, rows, D), BF)],
    )(table, *parts)
    return [cut[0]], cut[1:], shift


def exchange(own, sends, axis, shift):
    return own + [swap(x, axis, (j + 1) << shift) for j, x in enumerate(sends)]


def reduce_members(groups, extra, table, offsets):
    ng = groups[0][0].shape[0]
    rows = sum(g[0].shape[1] for g in groups) + (0 if extra is None else extra.shape[0])
    cut = small_kernel(
        functools.partial(members_kernel, tuple(len(g) for g in groups), offsets["member"], extra is not None),
        [((rows, D), BF)] * ng, [(g[0].shape, BF) for g in groups],
        (table, *sum(groups, []), *([] if extra is None else [extra])),
    )
    return [cut[0]], cut[1:], 0


def reduce_last(parts, extra, table):
    rows = parts[0].shape[0] + extra * (len(parts) - 1)
    return small_kernel(
        functools.partial(last_kernel, len(parts), extra), [((rows, D), BF)], [], (table, *parts)
    )[0]


def pack_first_kernel(lead_at, emb_real, shard_place, table_ref, emb_ref, wa_ref, wqkv_ref, shard_ref, mine_ref, wide_ref):
    wide_ref[...] = jnp.zeros_like(wide_ref)
    wide_ref[0:emb_real, :] = emb_ref[...]
    seg = wide_ref.shape[0]
    shard_ref[0:seg, :] = pltpu.roll(wide_ref[...], table_ref[lead_at], 0).astype(BF)
    at = seg
    for ref in (wa_ref, wqkv_ref):
        for c in range(3):
            rows = ref.shape[1]
            shard_ref[at : at + rows, :] = ref[0, :, D * c : D * (c + 1)].astype(BF)
            at += rows
    if at < shard_ref.shape[0]:
        shard_ref[at:, :] = jnp.zeros_like(shard_ref[at:, :])
    rows = mine_ref.shape[0]
    mine_ref[...] = shard_ref[pl.ds(pl.multiple_of(table_ref[shard_place] * rows, rows), rows), :]


def pack_first(table, offsets, emb_table, w_in, seg, unit):
    nr = lax.axis_size("rep")
    rows = w_in.shape[1]
    total = -(-(seg + 6 * rows) // unit) * unit
    part = lambda c: pl.BlockSpec((1, rows, 3 * D), lambda i: (0, 0, c))
    return pl.pallas_call(
        functools.partial(pack_first_kernel, offsets["lead"], emb_table.shape[0], offsets["place"]),
        grid=(1,),
        in_specs=[SCALARS, whole(*emb_table.shape), part(0), part(2)],
        out_specs=[whole(total, D), whole(total // nr, D)],
        out_shape=[sds((total, D), BF), sds((total // nr, D), BF)],
        scratch_shapes=[pltpu.VMEM((seg, D), F32)],
        compiler_params=pltpu.CompilerParams(vmem_limit_bytes=VMEM_LIMIT),
    )(table, emb_table, w_in, w_in)


def pack_other_kernel(layouts, shard_place, table_ref, *refs):
    refs = list(refs)
    inputs = [[refs.pop(0) for _ in layout] for layout in layouts]
    shard_refs, mine_ref = refs[:-1], refs[-1]
    put = 0
    for layout, ins, shard_ref in zip(layouts, inputs, shard_refs):
        at = 0
        for ref, count in zip(ins, layout):
            rows = ref.shape[-2]
            for c in range(count):
                cols = slice(D * c, D * (c + 1))
                value = ref[0, :, cols] if len(ref.shape) == 3 else ref[:, cols]
                shard_ref[at : at + rows, :] = value.astype(BF)
                at += rows
            if len(ref.shape) == 2:
                value = ref[:, D * count :]
                shard_ref[at : at + rows, :] = jnp.concatenate(
                    [value, jnp.zeros((rows, D - value.shape[1]), F32)], axis=1
                ).astype(BF)
                at += rows
        if at < shard_ref.shape[0]:
            shard_ref[at:, :] = jnp.zeros_like(shard_ref[at:, :])
        rows = shard_ref.shape[0] * mine_ref.shape[0] // sum(r.shape[0] for r in shard_refs)
        from_rows = pl.ds(pl.multiple_of(table_ref[shard_place] * rows, rows), rows)
        mine_ref[put : put + rows, :] = shard_ref[from_rows, :]
        put += rows


def pack_other(table, offsets, shards):
    nr = lax.axis_size("rep")
    spec = lambda shape, index: pl.BlockSpec(shape, lambda i: index)
    parts = sum((p for _, p in shards), [])
    shapes = [(rows, D) for rows, _ in shards] + [(sum(rows for rows, _ in shards) // nr, D)]
    return pl.pallas_call(
        functools.partial(
            pack_other_kernel, tuple(tuple(p[3] for p in ps) for _, ps in shards), offsets["place"]
        ),
        grid=(1,),
        in_specs=[SCALARS] + [spec(p[1], p[2]) for p in parts],
        out_specs=[whole(*shape) for shape in shapes],
        out_shape=[sds(shape, BF) for shape in shapes],
        compiler_params=pltpu.CompilerParams(vmem_limit_bytes=VMEM_LIMIT),
    )(table, *[p[0] for p in parts])


def fill_full(full_ref, masks, place, member, table_ref, shard_ref, pieces):
    ng = full_ref.shape[0]
    full_ref[table_ref[member]] = shard_ref[...]
    for group, ref in zip(masks, pieces):
        rows = ref.shape[0] // (len(group) * (ng - 1))
        for i, mask in enumerate(group):
            at = pl.ds(pl.multiple_of(table_ref[place + mask] * rows, rows), rows)
            for k in range(1, ng):
                start = (i * (ng - 1) + k - 1) * rows
                full_ref[table_ref[member + k], at, :] = ref[start : start + rows, :]


def take_blocks(full_ref, start, count, out_ref):
    ng = full_ref.shape[0]
    step = D // ng
    for g in range(ng):
        for c in range(count):
            out_ref[step * g : step * (g + 1), D * c : D * (c + 1)] = full_ref[
                g, start + step * c : start + step * (c + 1), :
            ]
    return start + step * count


def take_outer(full_ref, start, wo_ref, wg_ref):
    ng = full_ref.shape[0]
    wide = (D + FF) // ng
    for g in range(ng):
        low, high = wide * g, wide * (g + 1)
        if low < D:
            cut = min(high, D)
            wo_ref[low:cut, :] = full_ref[g, start : start + cut - low, :]
        if high > D:
            cut = max(low, D)
            wg_ref[cut - D : high - D, :] = full_ref[g, start + cut - low : start + wide, :]
    return start + wide


def first_kernel(emb_rows, seg, masks, place, member, table_ref, shard_ref, feats_ref, labels_ref, *refs):
    pieces, rest = refs[: len(masks)], refs[len(masks) :]
    (wp_t_ref, w2_ref, wa_ref, wqkv_ref, wqkv_t_ref, mods_ref, time_act_ref, pre_ref, cond_ref, act_t_ref,
     full_ref, emb_ref) = rest
    fill_full(full_ref, masks, place, member, table_ref, shard_ref, pieces)
    ng = full_ref.shape[0]
    emb_ref[...] = jnp.zeros_like(emb_ref)
    for g in range(ng):
        base = emb_rows * g // 16 * 16
        emb_ref[base : base + seg, :] = emb_ref[base : base + seg, :] + full_ref[g, 0:seg, :]
    at = take_blocks(full_ref, seg, 3, wa_ref)
    take_blocks(full_ref, at, 3, wqkv_ref)
    wqkv_t_ref[...] = wqkv_ref[...].T
    wp_t_ref[...] = emb_ref[0:128, :].T[:, 0:PATCH_IN]
    w1 = emb_ref[PATCH_IN : PATCH_IN + FREQ, :]
    w2_ref[...] = emb_ref[PATCH_IN + FREQ : PATCH_IN + FREQ + D, :]
    classes = emb_ref[PATCH_IN + FREQ + D : PATCH_IN + FREQ + D + CLASSES + 8, :]
    pre = mm(feats_ref[...], w1)
    pre_ref[...] = pre
    time_act = swish_parts(pre)[0].astype(BF)
    time_act_ref[...] = time_act
    hot = labels_ref[...] == lax.broadcasted_iota(jnp.int32, (labels_ref.shape[0], CLASSES + 8), 1)
    cond = mm(time_act, w2_ref[...]) + mm(jnp.where(hot, 1.0, 0.0).astype(BF), classes)
    cond_ref[...] = cond
    act = swish_parts(cond)[0]
    act_t_ref[...] = act.T.astype(BF)
    mods_ref[...] = mm(wa_ref[...].T, act_t_ref[...])


def second_kernel(masks, place, member, table_ref, shard_ref, act_t_ref, *refs):
    pieces, rest = refs[: len(masks)], refs[len(masks) :]
    wo_ref, wg_ref, wo_t_ref, wg_t_ref, wf_ref, wf_t_ref, wa_ref, mods_ref, full_ref = rest
    fill_full(full_ref, masks, place, member, table_ref, shard_ref, pieces)
    at = take_outer(full_ref, 0, wo_ref, wg_ref)
    at = take_blocks(full_ref, at, 4, wf_ref)
    take_blocks(full_ref, at, 3, wa_ref)
    wo_t_ref[...] = wo_ref[...].T
    wg_t_ref[...] = wg_ref[...].T
    wf_t_ref[...] = wf_ref[...].T
    mods_ref[...] = mm(wa_ref[...].T, act_t_ref[...])


def third_kernel(masks, place, member, table_ref, shard_ref, act_t_ref, *refs):
    pieces, rest = refs[: len(masks)], refs[len(masks) :]
    (wo_ref, wg_ref, wo_t_ref, wg_t_ref, wf_ref, wf_t_ref, wqkv_ref, wqkv_t_ref, wa_ref, wm_ref, wy_ref, wy_t_ref,
     mods_ref, modf_ref, full_ref, wide_ref) = rest
    fill_full(full_ref, masks, place, member, table_ref, shard_ref, pieces)
    at = take_outer(full_ref, 0, wo_ref, wg_ref)
    at = take_blocks(full_ref, at, 6, wa_ref)
    at = take_blocks(full_ref, at, 3, wqkv_ref)
    at = take_blocks(full_ref, at, 4, wf_ref)
    at = take_blocks(full_ref, at, 2, wm_ref)
    take_blocks(full_ref, at, 1, wide_ref)
    wo_t_ref[...] = wo_ref[...].T
    wg_t_ref[...] = wg_ref[...].T
    wf_t_ref[...] = wf_ref[...].T
    wqkv_t_ref[...] = wqkv_ref[...].T
    wy_ref[...] = wide_ref[:, 0:PATCH_IN]
    wy_t_ref[...] = wide_ref[...].T[0:PATCH_IN, :]
    mods_ref[...] = mm(wa_ref[...].T, act_t_ref[...])
    modf_ref[...] = mm(wm_ref[...].T, act_t_ref[...])


def assemble(kernel, table, offsets, shard, pieces, extra, outs, scratch):
    ng = lax.axis_size("grp")
    masks = tuple(m for m, v in pieces if v is not None)
    arrays = [v for _, v in pieces if v is not None]
    return small_kernel(
        functools.partial(kernel, masks, offsets["place"], offsets["member"]), outs,
        [((ng,) + shard.shape, BF)] + scratch, (table, shard, *extra, *arrays),
    )


def cond_back_kernel(n, table_ref, gma0_ref, gmb0_ref, gma1_ref, gmb1_ref, gmf_ref, wa0a_ref, wa0b_ref, wa1_ref, wm_ref,
                     w2_ref, cond_ref, pre_ref, time_act_ref, feats_ref, label_ref, squares_ref, rows_ref):
    low = lambda ref: ref[...].astype(BF)
    gact = mm(wm_ref[...], low(gmf_ref))
    gact += mm(wa1_ref[:, 0 : 2 * D], low(gma1_ref)) + mm(wa1_ref[:, 2 * D :], low(gmb1_ref))
    gact += mm(wa0a_ref[:, 0 : 2 * D], low(gma0_ref)) + mm(wa0a_ref[:, 2 * D :], gmb0_ref[0:D, :].astype(BF))
    gact += mm(wa0b_ref[...], gmb0_ref[D:, :].astype(BF))
    gcond = gact.T * swish_parts(cond_ref[...])[1]
    gpre = mm_nt(gcond.astype(BF), w2_ref[...]) * swish_parts(pre_ref[...])[1]
    total = jnp.sum(squares_ref[...]).reshape(1, 1)
    high = total.astype(BF).astype(F32)
    middle = (total - high).astype(BF).astype(F32)
    last = total - high - middle
    lane = lax.broadcasted_iota(jnp.int32, (n, 128), 1)
    row = lax.broadcasted_iota(jnp.int32, (n, 128), 0)
    loss = jnp.where(lane == 0, high, jnp.where(lane == 1, middle, jnp.where(lane == 2, last, 0.0)))
    loss = jnp.where(row == 0, loss, 0.0)
    loss = jnp.where(lane == 3, label_ref[:, 0:1], jnp.where(lane == 4, label_ref[:, 1:2], loss))
    top = jnp.concatenate([time_act_ref[...].astype(F32)[0:n], gpre[0:n]], axis=0)
    feats = jnp.concatenate([feats_ref[...].astype(F32)[0:n], loss], axis=1)
    rows_ref[0 : 2 * n, :] = top.astype(BF)
    rows_ref[2 * n : 4 * n, :] = jnp.concatenate([gcond[0:n], feats], axis=0).astype(BF)


def emb_grad_kernel(n, inv_entries, counts, extra, table_ref, *refs):
    pieces, (grad_ref, loss_ref, left_ref, right_ref) = refs[: len(counts)], refs[len(counts) :]
    at = 0
    for ref, count in zip(pieces, counts):
        each = ref.shape[0] // count
        for i in range(count):
            for base in range(each * (i + 1) - extra, each * (i + 1), 4 * n):
                left_ref[at : at + 2 * n, :] = ref[base : base + 2 * n, :]
                right_ref[at : at + 2 * n, :] = ref[base + 2 * n : base + 4 * n, :]
                at += 2 * n
    total = left_ref.shape[0]
    row = lax.broadcasted_iota(jnp.int32, (total, D), 0)
    top = (row % (2 * n)) < n
    zero = jnp.zeros((total, D), BF)
    act = jnp.where(top, left_ref[...], zero)
    gcond = jnp.where(top, right_ref[...], zero)
    gpre = jnp.where(top, zero, left_ref[...])
    feats = right_ref[:, 0:FREQ]
    tags = right_ref[:, FREQ:].astype(F32).T
    label = (tags[3:4, :] * 32.0 + tags[4:5, :]).astype(jnp.int32)
    label = pltpu.roll(jnp.broadcast_to(label, (8, total)), total - n, 1)[0:1, :]
    hot = label == lax.broadcasted_iota(jnp.int32, (CLASSES + 8, total), 0)
    grad_ref[0:PATCH_IN, :] = jnp.zeros((PATCH_IN, D), F32)
    grad_ref[PATCH_IN : PATCH_IN + FREQ, :] = mm(feats.T, gpre)
    grad_ref[PATCH_IN + FREQ : PATCH_IN + FREQ + D, :] = mm(act.T, gcond)
    grad_ref[PATCH_IN + FREQ + D :, :] = mm(jnp.where(hot, 1.0, 0.0).astype(BF), gcond)
    spot = lax.broadcasted_iota(jnp.int32, tags.shape, 1) % (2 * n) >= n
    spot &= lax.broadcasted_iota(jnp.int32, tags.shape, 0) < 3
    loss_ref[...] = jnp.sum(jnp.where(spot, tags, 0.0)).reshape(1, 1) * inv_entries


def update_kernel(masks, place, sizes, step_rows, layout, extra, n_chain, table_ref, *refs):
    pieces, refs = refs[: len(masks)], refs[len(masks) :]
    states, refs = refs[:6], refs[6 + n_chain :]
    news, rest_refs, shard_refs = refs[:6], refs[6 : 6 + len(sizes)], refs[6 + len(sizes) :]
    step = pl.program_id(0)

    @pl.when(step == 0)
    def _():
        for group, ref in zip(masks, pieces):
            each = ref.shape[0] // len(group)
            for i, mask in enumerate(group):
                start = each * i
                for rows, shard_ref in zip(sizes, shard_refs):
                    at = pl.ds(pl.multiple_of(table_ref[place + mask] * rows, rows), rows)
                    shard_ref[at, :] = ref[start : start + rows, :]
                    start += rows
        for rest_ref, shard_ref in zip(rest_refs, shard_refs):
            rest_ref[...] = shard_ref[shard_ref.shape[0] - rest_ref.shape[0] :, :].astype(F32)

    out_rows = states[0].shape[1]
    at = pl.multiple_of(step * out_rows, 16)
    grad = shard_refs[0][pl.ds(at, out_rows), :].astype(F32)
    for ref, value in zip(news[:3], advance(*(r[0] for r in states[:3]), grad)):
        ref[0] = value
    for group, row, block in layout:
        cols = slice(D * block, D * (block + 1))
        at = pl.multiple_of(row + step * step_rows, 16)
        grad = shard_refs[group][pl.ds(at, step_rows), :].astype(F32)
        for ref, value in zip(news[3:], advance(*(r[0, :, cols] for r in states[3:]), grad)):
            ref[0, :, cols] = value


def update(table, offsets, pieces, layer, packs, extra, outer, inner, chain):
    nr = lax.axis_size("rep")
    rows, wide = inner[0].shape[1], inner[0].shape[2]
    rows_out = outer[0].shape[1]
    step_rows = 16
    steps = rows // step_rows
    masks = tuple(m for m, _ in pieces)
    arrays = [v for _, v in pieces]
    sizes = tuple(p[1] // nr for p in packs)
    layout = [(0, rows_out + rows * i, 9 + i) for i in range(4)]
    layout += [(0, rows_out + rows * (4 + i), 2 + i) for i in range(4)]
    layout += [(1, rows * i, 6 + i) for i in range(3)] + [(1, rows * (3 + i), i) for i in range(2)]
    rests = [packs[0][1] - rows_out - 8 * rows, packs[1][1] - 5 * rows]
    in_spec = pl.BlockSpec((1, step_rows, wide), lambda i: (layer, i, 0))
    out_spec = pl.BlockSpec((1, rows_out // steps, D), lambda i: (layer, i, 0))
    states = list(outer) + list(inner)
    specs = [out_spec] * 3 + [in_spec] * 3
    chain = list(chain) if chain else []
    first = 1 + len(arrays) + len(states)
    return pl.pallas_call(
        functools.partial(
            update_kernel, masks, offsets["place"], sizes, step_rows, tuple(layout), extra, len(chain)
        ),
        grid=(steps,),
        in_specs=[SCALARS] + [whole(*a.shape) for a in arrays] + specs
        + [pl.BlockSpec(memory_space=pl.ANY)] * len(chain),
        out_specs=specs + [whole(r, D) for r in rests],
        out_shape=[sds(s.shape, F32) for s in states] + [sds((r, D), F32) for r in rests],
        scratch_shapes=[pltpu.VMEM((p[1], D), BF) for p in packs],
        input_output_aliases={first + i: i for i in range(len(chain))},
        compiler_params=pltpu.CompilerParams(vmem_limit_bytes=VMEM_LIMIT),
    )(table, *arrays, *states, *chain)


def local(
    latents, noise, timesteps, labels, emb_table, emb_mom, emb_ema, w_in, in_mom, in_ema,
    w_out, out_mom, out_ema, head, head_mom, head_ema,
):
    nr, ng = lax.axis_size("rep"), lax.axis_size("grp")
    member = lax.axis_index("grp")
    n = latents.shape[0]
    B = IMAGES_PER_STEP
    unit = 16 * nr
    digits = digit_list(nr)
    rows_d = D // ng
    rows_out = (D + FF) // ng
    emb_rows = emb_table.shape[0]
    seg = -(-(emb_rows + 15) // 16) * 16
    emb_full = emb_rows * (ng - 1) // 16 * 16 + seg
    full_rows = lambda rows: -(-rows // unit) * unit
    table, offsets = place_table(emb_rows)

    shard1, mine1 = pack_first(table, offsets, emb_table, w_in, seg, unit)
    got1 = gather_members(mine1)
    three, one = (1, rows_d, 3 * D), (1, rows_d, D)
    shard2, shard3, mine23 = pack_other(
        table, offsets,
        [
            (full_rows(rows_out + 7 * rows_d),
             [(w_out, (1, rows_out, D), (0, 0, 0), 1), (w_in, three, (0, 0, 3), 3), (w_in, one, (0, 0, 12), 1),
              (w_in, three, (0, 0, 1), 3)]),
            (full_rows(rows_out + 16 * rows_d),
             [(w_out, (1, rows_out, D), (1, 0, 0), 1), (w_in, (1, rows_d, 13 * D), (1, 0, 0), 13),
              (head, head.shape, (0, 0), 2)]),
        ],
    )
    around1 = spread_outer(after(got1, mine23), nr)
    cut2 = shard2.shape[0] // nr
    came1 = [v for m, v in around1 if m != (0,)]
    got2 = gather_members(after(mine23[:cut2], came1[0]))
    around2 = spread_outer(got2, nr)
    mine3 = after(mine23[cut2:], *came1, got2)
    got3 = [swap(mine3, "grp", k) for k in range(1, ng)]

    levels = plan(timesteps)
    noise_level = jnp.sqrt(jnp.maximum(1.0 - levels, 0.0))
    noisy = (
        jnp.sqrt(levels)[:, None, None] * latents.astype(F32)
        + noise_level[:, None, None] * noise.astype(F32)
    ).astype(BF)
    feats = jnp.pad(time_features(timesteps).astype(BF), ((0, 128 - n), (0, 0)))
    label_column = jnp.pad(labels, (0, 128 - n), constant_values=-1)[:, None]
    label_parts = jnp.pad(
        jnp.stack([labels >> 5, labels & 31], axis=1).astype(F32), ((0, 0), (0, 126))
    )
    pos = positions()

    pieces1 = spread_core(
        [(sum((m for m, _ in around1), ()), jnp.concatenate([v for _, v in around1], axis=0))], nr
    )
    wp_t, w2, wa0a, wqkv0, wqkv0_t, mods0a, time_act, pre_time, cond, act_t = assemble(
        functools.partial(first_kernel, emb_rows, seg), table, offsets, shard1, pieces1,
        (feats, label_column),
        [((D, PATCH_IN), BF), ((D, D), BF), ((D, 3 * D), BF), ((D, 3 * D), BF), ((3 * D, D), BF),
         ((3 * D, 128), F32), ((128, D), BF), ((128, D), F32), ((128, D), F32), ((D, 128), BF)],
        [((emb_full, D), BF)],
    )
    early = att_forward(noisy, wp_t, pos, after(mods0a, got2), wqkv0_t, B, 0, 2, ())
    got3 = [after(g, early[0]) for g in got3]
    got3 = jnp.concatenate(got3, axis=0)
    around3 = spread_outer(got3, nr)
    qkv0, lse0, att0 = att_forward(noisy, wp_t, pos, after(mods0a, got3), wqkv0_t, B, 1, 2, early)
    pieces2 = spread_core([(m, after(v, att0)) for m, v in around2], nr)
    wo0, wg0, wo0_t, wg0_t, wf0, wf0_t, wa0b, mods0b = assemble(
        second_kernel, table, offsets, shard2, pieces2, (act_t,),
        [((D, D), BF), ((FF, D), BF), ((D, D), BF), ((D, FF), BF), ((D, FF), BF), ((FF, D), BF),
         ((D, 3 * D), BF), ((3 * D, 128), F32)],
        [],
    )
    mid0, bra0, brb0, hid1 = ffn_forward(noisy, wp_t, pos, att0, mods0a, mods0b, wo0_t, wf0_t, wg0_t, B)
    pieces3 = spread_core([(m, after(v, hid1)) for m, v in around3], nr)
    (wo1, wg1, wo1_t, wg1_t, wf1, wf1_t, wqkv1, wqkv1_t, wa1, wm, wy, wy_t, mods1, modf) = assemble(
        third_kernel, table, offsets, shard3, pieces3, (act_t,),
        [((D, D), BF), ((FF, D), BF), ((D, D), BF), ((D, FF), BF), ((D, FF), BF), ((FF, D), BF),
         ((D, 3 * D), BF), ((3 * D, D), BF), ((D, 6 * D), BF), ((D, 2 * D), BF), ((D, PATCH_IN), BF),
         ((PATCH_IN, D), BF), ((6 * D, 128), F32), ((2 * D, 128), F32)],
        [((D, D), BF)],
    )
    entries = n * nr * ng * TOK * PATCH_IN
    outer_pack = (ng, full_rows(rows_out + 8 * rows_d + PATCH_IN), D)
    qkv_pack1 = (ng, full_rows(7 * rows_d), D)
    qkv_pack0 = (ng, full_rows(5 * rows_d + PATCH_IN), D)
    qkv1, lse1, go1, gmid1, gmb1, gmf, squares, keep_f1, send_f1 = block_step(
        table, hid1, noise, mods1, modf, wqkv1_t, wo1_t, wf1_t, wg1_t, wo1, wf1, wg1, wy_t, wy, act_t,
        float(entries), B, outer_pack,
    )
    parts_f1 = reduce_first(keep_f1, send_f1)
    ghid1, gma1, keep_a1, send_a1 = att_backward(
        table, (hid1,), qkv1, lse1, go1, gmid1, mods1, wqkv1, act_t, gmf, B, False, qkv_pack1
    )
    parts_a1 = reduce_first(keep_a1, send_a1)

    def outer_stage(parts):
        sends = []
        for number in range(1, len(digits)):
            own, sends, shift = reduce_outer(parts, table, offsets, number)
            parts = exchange(own, sends, "rep", shift)
        return parts, sends

    def member_stage(groups, extra):
        own, sends, shift = reduce_members(groups, extra, table, offsets)
        return exchange(own, sends, "grp", shift), sends

    def held(parts, *marks):
        return [parts[0]] + [after(p, *marks) for p in parts[1:]]

    parts_f1, sends_f1 = outer_stage(held(parts_f1, ghid1))
    go0, gmid0, gmb0, keep_f0, send_f0 = ffn_backward(
        table, after(ghid1, *sends_f1), mid0, att0, bra0, brb0, mods0a, mods0b, wf0_t, wo0, wf0, wg0, act_t,
        B, outer_pack,
    )
    parts_f0 = reduce_first(keep_f0, send_f0)
    parts_f1 = held(parts_f1, gmid0)
    parts_a1, sends_a1 = outer_stage(held(parts_a1, gmid0, *parts_f1[1:]))
    back0 = functools.partial(
        att_backward, table, (noisy, wp_t, pos), qkv0, lse0, go0, mods=mods0a, wqkv=wqkv0, cond=act_t, gmf=None,
        B=B, bottom=True, pack=qkv_pack0, parts=2,
    )
    half = back0(gmid=after(gmid0, *sends_a1), part=0)
    mark = half[0]
    parts_1, sends_1 = member_stage([parts_f1, held(parts_a1, mark)], None)
    parts_f0, sends_f0 = outer_stage([after(p, *sends_1) for p in held(parts_f0, mark)])
    gma0, keep_a0, send_a0 = back0(gmid=after(gmid0, *sends_f0), part=1, before=half)
    parts_a0 = reduce_first(keep_a0, send_a0)
    parts_f0 = held(parts_f0, gma0)
    piece_1 = reduce_last(held(parts_1, gma0), 0, table)
    rows0 = small_kernel(
        functools.partial(cond_back_kernel, n), [((4 * n, D), BF)], [],
        (table, after(gma0, piece_1), gmb0, gma1, gmb1, gmf, wa0a, wa0b, wa1, wm, w2, cond, pre_time,
         time_act, feats, label_parts, squares),
    )[0]
    parts_a0, sends_a0 = outer_stage(held(parts_a0, rows0, *parts_f0[1:]))
    pieces_1 = spread_core(spread_outer(piece_1, nr), nr)
    outer_state, inner_state = (w_out, out_mom, out_ema), (w_in, in_mom, in_ema)
    new_1 = update(table, offsets, pieces_1, 1, (outer_pack, qkv_pack1), 0, outer_state, inner_state, None)
    parts_0, sends_0 = member_stage([parts_f0, parts_a0], rows0)
    piece_0 = reduce_last(parts_0, 4 * n, table)
    pieces_0 = spread_core(spread_outer(piece_0, nr), nr)
    extra = ng * 4 * n
    new_0 = update(table, offsets, pieces_0, 0, (outer_pack, qkv_pack0), extra, outer_state, inner_state, new_1[:6])
    emb_grad, loss_value = small_kernel(
        functools.partial(emb_grad_kernel, n, 1.0 / entries, tuple(len(m) for m, _ in pieces_0), extra),
        [((emb_full, D), F32), ((1, 1), F32)], [((2 * n * nr * ng, D), BF)] * 2,
        (table, *[v for _, v in pieces_0]),
    )
    emb_grad = lax.dynamic_slice_in_dim(emb_grad, member * emb_rows, emb_rows, 0)
    patch_grad = jnp.where(member == 0, new_0[7][:PATCH_IN], 0.0)
    emb_new = advance(
        emb_table, emb_mom, emb_ema, emb_grad + jnp.pad(patch_grad, ((0, emb_rows - PATCH_IN), (0, 0)))
    )
    wm_grad = new_1[7][: 2 * rows_d].reshape(2, rows_d, D).transpose(1, 0, 2).reshape(rows_d, 2 * D)
    wy_grad = lax.dynamic_slice_in_dim(new_1[6][:PATCH_IN], member * rows_d, rows_d, 1).T
    head_new = advance(head, head_mom, head_ema, jnp.concatenate([wm_grad, wy_grad], axis=1))
    return (loss_value.reshape(()), *emb_new, *new_0[3:6], *new_0[:3], *head_new)


def solution(mesh):
    data = P(("rep", "grp"), None, None)
    vector = P(("rep", "grp"))
    flat = P("grp", None)
    deep = P(None, "grp", None)
    return jax.shard_map(
        local,
        mesh=mesh,
        in_specs=(data, data, vector, vector, flat, flat, flat, deep, deep, deep, deep, deep, deep,
                  flat, flat, flat),
        out_specs=(P(), flat, flat, flat, deep, deep, deep, deep, deep, deep, flat, flat, flat),
        check_vma=False,
    )
```

```python
import functools
import math

import jax
import jax.numpy as jnp
from jax import lax
from jax.experimental import pallas as pl
from jax.experimental.pallas import tpu as pltpu
from jax.sharding import PartitionSpec as P

D = 384
HEADS = 6
HEAD_DIM = 64
FF = 1536
TOK = 256
PATCH_IN = 16
EPSILON = 1e-06
BF = jnp.bfloat16
F32 = jnp.float32
VMEM_LIMIT = 58 * 1024 * 1024


def mm(left, right):
    return lax.dot_general(left, right, (((1,), (0,)), ((), ())), preferred_element_type=F32)


def mm_nt(left, right):
    return lax.dot_general(left, right, (((1,), (1,)), ((), ())), preferred_element_type=F32)


def norm_parts(x):
    centered = x - jnp.mean(x, axis=0, keepdims=True)
    variance = jnp.mean(centered * centered, axis=0, keepdims=True)
    inv = lax.rsqrt(variance + EPSILON)
    return centered * inv, inv


def norm_back(d, normed, inv, scale1):
    dn = d * scale1
    m1 = jnp.mean(dn, axis=0, keepdims=True)
    m2 = jnp.mean(dn * normed, axis=0, keepdims=True)
    return (dn - m1 - normed * m2) * inv


def column(mods_ref, index, image):
    block = mods_ref[pl.ds(index * D, D), :]
    lane = lax.broadcasted_iota(jnp.int32, block.shape, 1)
    return jnp.sum(jnp.where(lane == image, block, 0.0), axis=1, keepdims=True)


def put_column(out_ref, index, image, values):
    total = jnp.sum(values, axis=1, keepdims=True)
    rows = pl.ds(index * D, D)
    old = out_ref[rows, :]
    lane = lax.broadcasted_iota(jnp.int32, old.shape, 1)
    out_ref[rows, :] = jnp.where(lane == image, total, old)


def half_zero(x, half):
    row = lax.broadcasted_iota(jnp.int32, x.shape, 0)
    keep = row < HEAD_DIM if half == 0 else row >= HEAD_DIM
    return jnp.where(keep, x, jnp.zeros_like(x))


def head_groups(B):
    work = [(b, h) for b in range(B) for h in range(HEADS)]
    return [work[i : i + HEAD_GROUP] for i in range(0, len(work), HEAD_GROUP)]


def pair_rows(ref, b, h, base=0):
    lo = base + 2 * HEAD_DIM * (h // 2)
    return ref[b, lo : lo + 2 * HEAD_DIM, :]


def head_rows(ref, b, h, base=0):
    return ref[b, base + HEAD_DIM * h : base + HEAD_DIM * (h + 1), :]


def attention_forward(qkv_ref, B, lse_ref, att_ref):
    for work in head_groups(B):
        scores = [
            mm(pair_rows(qkv_ref, b, h, D).T, half_zero(pair_rows(qkv_ref, b, h), h % 2)) for b, h in work
        ]
        peaks = [jnp.max(x, axis=0, keepdims=True) for x in scores]
        exps = [jnp.exp(x - p) for x, p in zip(scores, peaks)]
        totals = [jnp.sum(x, axis=0, keepdims=True) for x in exps]
        outs = [mm(head_rows(qkv_ref, b, h, 2 * D), x.astype(BF)) for (b, h), x in zip(work, exps)]
        for (b, h), out, total, peak in zip(work, outs, totals, peaks):
            att_ref[HEAD_DIM * h : HEAD_DIM * (h + 1), lanes_of(b)] = (out * (1.0 / total)).astype(BF)
            lse_ref[b, h : h + 1, :] = peak + jnp.log(total)


def attention_backward(qkv_ref, B, lse_ref, go_ref, gqkv_ref):
    for work in head_groups(B):
        scores = [
            mm(pair_rows(qkv_ref, b, h, D).T, half_zero(pair_rows(qkv_ref, b, h), h % 2)) for b, h in work
        ]
        gprobs = [
            mm(pair_rows(qkv_ref, b, h, 2 * D).T, half_zero(pair_rows(go_ref, b, h), h % 2)) for b, h in work
        ]
        probs = [jnp.exp(x - lse_ref[b, h : h + 1, :]) for x, (b, h) in zip(scores, work)]
        inners = [jnp.sum(p * g, axis=0, keepdims=True) for p, g in zip(probs, gprobs)]
        gscores = [(p * (g - i)).astype(BF) for p, g, i in zip(probs, gprobs, inners)]
        gqs = [mm(head_rows(qkv_ref, b, h, D), g) for (b, h), g in zip(work, gscores)]
        gks = [mm_nt(head_rows(qkv_ref, b, h), g) for (b, h), g in zip(work, gscores)]
        gvs = [mm_nt(head_rows(go_ref, b, h), p.astype(BF)) for (b, h), p in zip(work, probs)]
        for (b, h), gq, gk, gv in zip(work, gqs, gks, gvs):
            row = HEAD_DIM * h
            for base, value in ((0, gq * (1.0 / math.sqrt(HEAD_DIM))), (D, gk), (2 * D, gv)):
                gqkv_ref[base + row : base + row + HEAD_DIM, lanes_of(b)] = value.astype(BF)


def project_qkv(wqkv_t_ref, normed_ref, qkv_ref, B):
    for part in range(3):
        qkv = mm(wqkv_t_ref[D * part : D * (part + 1), :], normed_ref[...])
        if part == 0:
            qkv = qkv * (1.0 / math.sqrt(HEAD_DIM))
        qkv = qkv.astype(BF)
        for b in range(B):
            qkv_ref[b, D * part : D * (part + 1), :] = qkv[:, TOK * b : TOK * (b + 1)]


def lanes_of(b):
    return slice(TOK * b, TOK * (b + 1))


def modulate_into(normed_ref, b, normed, scale1, shift):
    normed_ref[:, lanes_of(b)] = (normed * scale1 + shift).astype(BF)


def ffn_chunks():
    return [slice(f, f + FF_CHUNK) for f in range(0, FF, FF_CHUNK)]


def add_up(total, part):
    return part if total is None else total + part


GELU_C = 0.7978845608
GELU_A = 0.044715


def gelu_both(v):
    square = v * v
    t = jnp.tanh(v * (GELU_C + (GELU_C * GELU_A) * square))
    half = 0.5 + 0.5 * t
    slope = half + 0.5 * v * (1.0 - t * t) * (GELU_C + (3.0 * GELU_C * GELU_A) * square)
    return v * half, slope


def gelu_one(v):
    t = jnp.tanh(v * (GELU_C + (GELU_C * GELU_A) * (v * v)))
    return v * (0.5 + 0.5 * t)


def clear(*refs):
    for ref in refs:
        ref[...] = jnp.zeros_like(ref)


FF_CHUNK = 768
HEAD_GROUP = 12


def pack_blocks(pack_ref, start, value):
    members = pack_ref.shape[0]
    rows = D // members
    count = value.shape[1] // D
    for g in range(members):
        for c in range(count):
            pack_ref[g, start + rows * c : start + rows * (c + 1), :] = value[
                rows * g : rows * (g + 1), D * c : D * (c + 1)
            ].astype(BF)
    return start + rows * count


def pack_outer(pack_ref, awo_ref, awf_ref, awg_ref):
    members = pack_ref.shape[0]
    rows = (D + FF) // members
    for g in range(members):
        low, high = rows * g, rows * (g + 1)
        if low < D:
            cut = min(high, D)
            pack_ref[g, 0 : cut - low, :] = awo_ref[low:cut, :].astype(BF)
        if high > D:
            cut = max(low, D)
            pack_ref[g, cut - low : rows, :] = awg_ref[cut - D : high - D, :].astype(BF)
    return pack_blocks(pack_ref, rows, awf_ref)


def pack_rest(pack_ref, used, extra):
    if extra is not None:
        for g in range(pack_ref.shape[0]):
            pack_ref[g, used : used + PATCH_IN, :] = extra.astype(BF)
        used += PATCH_IN
    if used < pack_ref.shape[1]:
        pack_ref[:, used:, :] = jnp.zeros_like(pack_ref[:, used:, :])


def split_pack(pack_ref, table_ref, offset, outs):
    for j, out_ref in enumerate(outs):
        rows = out_ref.shape[1]
        at = pl.multiple_of(table_ref[offset + j] * rows, rows)
        out_ref[...] = pack_ref[:, pl.ds(at, rows), :]


def att_fwd_kernel(B, offset, held, noisy_ref, wp_t_ref, pos_ref, mods_ref, wqkv_t_ref, *refs):
    qkv_ref, lse_ref, att_out_ref, normed_ref, att_ref = refs[held:]
    step = pl.program_id(0)
    for b in range(B):
        image = (offset + step) * B + b
        hidden = mm(wp_t_ref[...], noisy_ref[b]) + pos_ref[...]
        normed, _ = norm_parts(hidden)
        modulate_into(normed_ref, b, normed, 1.0 + column(mods_ref, 1, image), column(mods_ref, 0, image))
    project_qkv(wqkv_t_ref, normed_ref, qkv_ref, B)
    attention_forward(qkv_ref, B, lse_ref, att_ref)
    for b in range(B):
        att_out_ref[b] = att_ref[:, lanes_of(b)]


def ffn_fwd_kernel(B, noisy_ref, wp_t_ref, pos_ref, att_ref, mods_a_ref, mods_b_ref, wo_t_ref, wf_t_ref,
                   wg_t_ref, mid_ref, bra_ref, brb_ref, hid_ref, normed_ref):
    step = pl.program_id(0)
    for b in range(B):
        image = step * B + b
        hidden = mm(wp_t_ref[...], noisy_ref[b]) + pos_ref[...]
        branch_a = mm(wo_t_ref[...], att_ref[b])
        bra_ref[b] = branch_a
        mid = hidden + column(mods_a_ref, 2, image) * branch_a
        mid_ref[b] = mid
        normed, _ = norm_parts(mid)
        modulate_into(normed_ref, b, normed, 1.0 + column(mods_b_ref, 1, image), column(mods_b_ref, 0, image))
    branch = None
    for rows in ffn_chunks():
        act = gelu_one(mm(wf_t_ref[rows, :], normed_ref[...])).astype(BF)
        branch = add_up(branch, mm(wg_t_ref[:, rows], act))
    for b in range(B):
        own = branch[:, lanes_of(b)]
        brb_ref[b] = own
        hid_ref[b] = mid_ref[b] + column(mods_b_ref, 2, step * B + b) * own


def block_kernel(B, entries, table_ref, hid_ref, noise_ref, mods_ref, modf_ref, wqkv_t_ref, wo_t_ref, wf_t_ref,
                 wg_t_ref, wo_ref, wf_ref, wg_ref, wy_t_ref, wy_ref, cond_ref,
                 qkv_ref, lse_ref, go_ref, gmid_ref, gm_ref, gmf_ref, loss_ref,
                 keep_ref, send_ref,
                 pack_ref, normed_ref, att_ref, slope_ref, act_ref, gpre_ref, gba_ref, gbb_ref, normf_ref, gout_ref,
                 awo_ref, awf_ref, awg_ref, awy_ref, bra_ref, ghid_ref):
    step = pl.program_id(0)
    first = step == 0

    @pl.when(first)
    def _():
        clear(gm_ref, gmf_ref, loss_ref, awo_ref, awf_ref, awg_ref, awy_ref)

    image = lambda b: step * B + b
    for b in range(B):
        normed, _ = norm_parts(hid_ref[b])
        modulate_into(normed_ref, b, normed, 1.0 + column(mods_ref, 1, image(b)), column(mods_ref, 0, image(b)))
    project_qkv(wqkv_t_ref, normed_ref, qkv_ref, B)
    attention_forward(qkv_ref, B, lse_ref, att_ref)
    branch_a = mm(wo_t_ref[...], att_ref[...])
    for b in range(B):
        own = branch_a[:, lanes_of(b)]
        bra_ref[b] = own
        mid = hid_ref[b] + column(mods_ref, 2, image(b)) * own
        gmid_ref[b] = mid
        normed, _ = norm_parts(mid)
        modulate_into(normed_ref, b, normed, 1.0 + column(mods_ref, 4, image(b)), column(mods_ref, 3, image(b)))
    branch_b = None
    for rows in ffn_chunks():
        act, slope = gelu_both(mm(wf_t_ref[rows, :], normed_ref[...]))
        slope_ref[rows, :] = slope
        act_ref[rows, :] = act.astype(BF)
        branch_b = add_up(branch_b, mm(wg_t_ref[:, rows], act_ref[rows, :]))
    for b in range(B):
        lanes = lanes_of(b)
        own = branch_b[:, lanes]
        gate_b = column(mods_ref, 5, image(b))
        normed_f, inv_f = norm_parts(gmid_ref[b] + gate_b * own)
        scale_f = 1.0 + column(modf_ref, 1, image(b))
        modulate_into(normf_ref, b, normed_f, scale_f, column(modf_ref, 0, image(b)))
        residue = mm(wy_t_ref[...], normf_ref[:, lanes]) - noise_ref[b].astype(F32)
        loss_ref[...] += residue * residue
        gout_ref[:, lanes] = ((2.0 / entries) * residue).astype(BF)
        gnf = mm(wy_ref[...], gout_ref[:, lanes])
        put_column(gmf_ref, 0, image(b), gnf)
        put_column(gmf_ref, 1, image(b), gnf * normed_f)
        ghid = norm_back(gnf, normed_f, inv_f, scale_f)
        ghid_ref[b] = ghid
        put_column(gm_ref, 3, image(b), ghid * own)
        gbb_ref[:, lanes] = (gate_b * ghid).astype(BF)
    gnb = None
    for rows in ffn_chunks():
        gact = mm(wg_ref[rows, :], gbb_ref[...])
        gpre_ref[rows, :] = (gact * slope_ref[rows, :]).astype(BF)
        gnb = add_up(gnb, mm(wf_ref[:, rows], gpre_ref[rows, :]))
        awf_ref[:, rows] += mm_nt(normed_ref[...], gpre_ref[rows, :])
        awg_ref[rows, :] += mm_nt(act_ref[rows, :], gbb_ref[...])
    for b in range(B):
        own = gnb[:, lanes_of(b)]
        normed, inv = norm_parts(gmid_ref[b])
        put_column(gm_ref, 1, image(b), own)
        put_column(gm_ref, 2, image(b), own * normed)
        gmid = ghid_ref[b] + norm_back(own, normed, inv, 1.0 + column(mods_ref, 4, image(b)))
        gmid_ref[b] = gmid
        put_column(gm_ref, 0, image(b), gmid * bra_ref[b])
        gba_ref[:, lanes_of(b)] = (column(mods_ref, 2, image(b)) * gmid).astype(BF)
    go = mm(wo_ref[...], gba_ref[...]).astype(BF)
    for b in range(B):
        go_ref[b] = go[:, lanes_of(b)]
    awo_ref[...] += mm_nt(att_ref[...], gba_ref[...])
    awy_ref[...] += mm_nt(gout_ref[...], normf_ref[...])

    @pl.when(step == pl.num_programs(0) - 1)
    def _():
        used = pack_outer(pack_ref, awo_ref, awf_ref, awg_ref)
        used = pack_blocks(pack_ref, used, mm_nt(cond_ref[...], gm_ref[...].astype(BF)))
        pack_rest(pack_ref, used, awy_ref[...])
        split_pack(pack_ref, table_ref, 0, (keep_ref, send_ref))


def ffn_bwd_kernel(B, table_ref, ghid_ref, mid_ref, att_ref, bra_ref, brb_ref, mods_a_ref, mods_b_ref, wf_t_ref, wo_ref, wf_ref,
                   wg_ref, cond_ref, go_ref, gmid_ref, gm_ref, keep_ref, send_ref, pack_ref,
                   normed_ref, act_ref, gpre_ref, gba_ref, gbb_ref, atts_ref, awo_ref, awf_ref, awg_ref):
    step = pl.program_id(0)
    first = step == 0

    @pl.when(first)
    def _():
        clear(gm_ref, awo_ref, awf_ref, awg_ref)

    image = lambda b: step * B + b
    for b in range(B):
        lanes = lanes_of(b)
        ghid = ghid_ref[b]
        put_column(gm_ref, 3, image(b), ghid * brb_ref[b])
        gbb_ref[:, lanes] = (column(mods_b_ref, 2, image(b)) * ghid).astype(BF)
        normed, _ = norm_parts(mid_ref[b])
        modulate_into(normed_ref, b, normed, 1.0 + column(mods_b_ref, 1, image(b)), column(mods_b_ref, 0, image(b)))
        atts_ref[:, lanes] = att_ref[b]
    gnb = None
    for rows in ffn_chunks():
        act, slope = gelu_both(mm(wf_t_ref[rows, :], normed_ref[...]))
        act_ref[rows, :] = act.astype(BF)
        gact = mm(wg_ref[rows, :], gbb_ref[...])
        gpre_ref[rows, :] = (gact * slope).astype(BF)
        gnb = add_up(gnb, mm(wf_ref[:, rows], gpre_ref[rows, :]))
        awf_ref[:, rows] += mm_nt(normed_ref[...], gpre_ref[rows, :])
        awg_ref[rows, :] += mm_nt(act_ref[rows, :], gbb_ref[...])
    for b in range(B):
        own = gnb[:, lanes_of(b)]
        normed, inv = norm_parts(mid_ref[b])
        put_column(gm_ref, 1, image(b), own)
        put_column(gm_ref, 2, image(b), own * normed)
        gmid = ghid_ref[b] + norm_back(own, normed, inv, 1.0 + column(mods_b_ref, 1, image(b)))
        gmid_ref[b] = gmid
        put_column(gm_ref, 0, image(b), gmid * bra_ref[b])
        gba_ref[:, lanes_of(b)] = (column(mods_a_ref, 2, image(b)) * gmid).astype(BF)
    go = mm(wo_ref[...], gba_ref[...]).astype(BF)
    for b in range(B):
        go_ref[b] = go[:, lanes_of(b)]
    awo_ref[...] += mm_nt(atts_ref[...], gba_ref[...])

    @pl.when(step == pl.num_programs(0) - 1)
    def _():
        used = pack_outer(pack_ref, awo_ref, awf_ref, awg_ref)
        used = pack_blocks(pack_ref, used, mm_nt(cond_ref[...], gm_ref[...].astype(BF)))
        pack_rest(pack_ref, used, None)
        split_pack(pack_ref, table_ref, 0, (keep_ref, send_ref))


def att_bwd_kernel(B, offset, bottom, opens, closes, *refs):
    refs = list(refs)
    take = lambda count: [refs.pop(0) for _ in range(count)]
    (table_ref,) = take(1)
    noisy_ref, wp_t_ref, pos_ref = take(3) if bottom else (None, None, None)
    (hid_ref,) = (None,) if bottom else take(1)
    qkv_ref, lse_ref, go_ref, gmid_ref, mods_ref, wqkv_ref, cond_ref = take(7)
    (gmf_ref,) = (None,) if bottom else take(1)
    before = take(3 if bottom else 2) if not opens else []
    (ghid_ref,) = (None,) if bottom else take(1)
    (gm_ref,) = take(1)
    sums = 2 if bottom else 1
    keep_ref, send_ref, pack_ref, accs = None, None, None, None
    if closes:
        keep_ref, send_ref = take(2)
    else:
        accs = take(sums)
    if closes:
        (pack_ref,) = take(1)
    normed_ref, gqkv_ref = take(2)
    tok_ref, noi_ref = take(2) if bottom else (None, None)
    if closes:
        accs = take(sums)
    step = pl.program_id(0)
    first = step == 0

    @pl.when(first)
    def _():
        if opens:
            gm_ref[...] = jnp.zeros_like(gm_ref)
            for acc_ref in accs:
                acc_ref[...] = jnp.zeros_like(acc_ref)
        else:
            for to_ref, from_ref in zip([gm_ref] + accs, before):
                to_ref[...] = from_ref[...]

    image = lambda b: (offset + step) * B + b
    source = lambda b: mm(wp_t_ref[...], noisy_ref[b]) + pos_ref[...] if bottom else hid_ref[b]
    for b in range(B):
        normed, _ = norm_parts(source(b))
        modulate_into(normed_ref, b, normed, 1.0 + column(mods_ref, 1, image(b)), column(mods_ref, 0, image(b)))
    attention_backward(qkv_ref, B, lse_ref, go_ref, gqkv_ref)
    gna = mm(wqkv_ref[...], gqkv_ref[...])
    for b in range(B):
        own = gna[:, lanes_of(b)]
        normed, inv = norm_parts(source(b))
        put_column(gm_ref, 0, image(b), own)
        put_column(gm_ref, 1, image(b), own * normed)
        ghid = gmid_ref[b] + norm_back(own, normed, inv, 1.0 + column(mods_ref, 1, image(b)))
        if bottom:
            tok_ref[:, lanes_of(b)] = ghid.astype(BF)
            noi_ref[:, lanes_of(b)] = noisy_ref[b]
        else:
            ghid_ref[b] = ghid
    accs[0][...] += mm_nt(normed_ref[...], gqkv_ref[...])
    if bottom:
        accs[1][...] += mm_nt(noi_ref[...], tok_ref[...])

    if closes:
        @pl.when(step == pl.num_programs(0) - 1)
        def _():
            used = pack_blocks(pack_ref, 0, accs[0])
            used = pack_blocks(pack_ref, used, mm_nt(cond_ref[...], gm_ref[...].astype(BF)))
            if not bottom:
                used = pack_blocks(pack_ref, used, mm_nt(cond_ref[...], gmf_ref[...].astype(BF)))
            pack_rest(pack_ref, used, accs[1][...] if bottom else None)
            split_pack(pack_ref, table_ref, 0, (keep_ref, send_ref))


def whole(*shape):
    return pl.BlockSpec(shape, lambda i: (0,) * len(shape))


def images(B, *shape, offset=0):
    return pl.BlockSpec((B,) + shape, lambda i: (i + offset,) + (0,) * len(shape))


def sds(shape, dtype):
    return jax.ShapeDtypeStruct(shape, dtype)


def run_kernel(kernel, steps, in_specs, outs, scratch, flops, args, aliases=None):
    out_specs = [spec for spec, _, _ in outs]
    out_shape = [sds(shape, dtype) for _, shape, dtype in outs]
    moved = sum(a.size * a.dtype.itemsize for a in args) + sum(
        math.prod(o.shape) * o.dtype.itemsize for o in out_shape
    )
    return pl.pallas_call(
        kernel,
        grid=(steps,),
        in_specs=in_specs,
        out_specs=out_specs,
        out_shape=out_shape,
        scratch_shapes=[pltpu.VMEM(shape, dtype) for shape, dtype in scratch],
        input_output_aliases=aliases or {},
        compiler_params=pltpu.CompilerParams(vmem_limit_bytes=VMEM_LIMIT),
        cost_estimate=pl.CostEstimate(flops=8 * flops, bytes_accessed=moved, transcendentals=0),
    )(*args)


MODS = whole(6 * D, 128)
HALF_MODS = whole(3 * D, 128)
COND = whole(D, 128)
SCALARS = pl.BlockSpec(memory_space=pltpu.SMEM)


def halves(pack):
    ng, rows, _ = pack
    half = (ng, rows // 2, D)
    return [(whole(*half), half, BF)] * 2


def att_forward(noisy, wp_t, pos, mods, wqkv_t, B, part, parts, before):
    n = noisy.shape[0]
    T = B * TOK
    steps = n // B // parts
    here = functools.partial(images, B, offset=part * steps)
    return run_kernel(
        functools.partial(att_fwd_kernel, B, part * steps, len(before)), steps,
        [here(PATCH_IN, TOK), whole(D, PATCH_IN), whole(D, TOK), HALF_MODS, whole(3 * D, D)]
        + [pl.BlockSpec(memory_space=pl.ANY)] * len(before),
        [(here(3 * D, TOK), (n, 3 * D, TOK), BF), (here(8, TOK), (n, 8, TOK), F32),
         (here(D, TOK), (n, D, TOK), BF)],
        [((D, T), BF), ((D, T), BF)],
        2 * n * TOK * (3 * D * D + 2 * D * TOK) // parts, (noisy, wp_t, pos, mods, wqkv_t) + tuple(before),
        aliases={5 + i: i for i in range(len(before))})


def ffn_forward(noisy, wp_t, pos, att, mods_a, mods_b, wo_t, wf_t, wg_t, B):
    n = noisy.shape[0]
    T = B * TOK
    full = images(B, D, TOK)
    return run_kernel(
        functools.partial(ffn_fwd_kernel, B), n // B,
        [images(B, PATCH_IN, TOK), whole(D, PATCH_IN), whole(D, TOK), full, HALF_MODS, HALF_MODS, whole(D, D),
         whole(FF, D), whole(D, FF)],
        [(full, (n, D, TOK), F32)] * 4,
        [((D, T), BF)],
        2 * n * TOK * (2 * D * FF + D * D), (noisy, wp_t, pos, att, mods_a, mods_b, wo_t, wf_t, wg_t))


def block_step(table, hid, noise, mods, modf, wqkv_t, wo_t, wf_t, wg_t, wo, wf, wg, wy_t, wy, cond, entries, B, pack):
    n = hid.shape[0]
    T = B * TOK
    full = images(B, D, TOK)
    return run_kernel(
        functools.partial(block_kernel, B, entries), n // B,
        [SCALARS, full, images(B, PATCH_IN, TOK), MODS, whole(2 * D, 128), whole(3 * D, D), whole(D, D),
         whole(FF, D), whole(D, FF), whole(D, D), whole(D, FF), whole(FF, D), whole(PATCH_IN, D),
         whole(D, PATCH_IN), COND],
        [(images(B, 3 * D, TOK), (n, 3 * D, TOK), BF), (images(B, 8, TOK), (n, 8, TOK), F32),
         (full, (n, D, TOK), BF), (full, (n, D, TOK), F32),
         (whole(4 * D, 128), (4 * D, 128), F32), (whole(2 * D, 128), (2 * D, 128), F32),
         (whole(PATCH_IN, TOK), (PATCH_IN, TOK), F32)] + halves(pack),
        [(pack, BF), ((D, T), BF), ((D, T), BF), ((FF, T), F32), ((FF, T), BF), ((FF, T), BF), ((D, T), BF),
         ((D, T), BF), ((D, T), BF), ((PATCH_IN, T), BF), ((D, D), F32), ((D, FF), F32), ((FF, D), F32),
         ((PATCH_IN, D), F32), ((B, D, TOK), F32), ((B, D, TOK), F32)],
        2 * n * TOK * (4 * D * D + 2 * D * TOK + 6 * D * FF + 2 * D * D),
        (table, hid, noise, mods, modf, wqkv_t, wo_t, wf_t, wg_t, wo, wf, wg, wy_t, wy, cond))


def ffn_backward(table, ghid, mid, att, bra, brb, mods_a, mods_b, wf_t, wo, wf, wg, cond, B, pack):
    n = mid.shape[0]
    T = B * TOK
    full = images(B, D, TOK)
    return run_kernel(
        functools.partial(ffn_bwd_kernel, B), n // B,
        [SCALARS, full, full, full, full, full, HALF_MODS, HALF_MODS, whole(FF, D), whole(D, D), whole(D, FF),
         whole(FF, D), COND],
        [(full, (n, D, TOK), BF), (full, (n, D, TOK), F32), (whole(4 * D, 128), (4 * D, 128), F32)] + halves(pack),
        [(pack, BF), ((D, T), BF), ((FF, T), BF), ((FF, T), BF), ((D, T), BF), ((D, T), BF), ((D, T), BF),
         ((D, D), F32), ((D, FF), F32), ((FF, D), F32)],
        2 * n * TOK * (5 * D * FF + 2 * D * D),
        (table, ghid, mid, att, bra, brb, mods_a, mods_b, wf_t, wo, wf, wg, cond))


def att_backward(table, source, qkv, lse, go, gmid, mods, wqkv, cond, gmf, B, bottom, pack, part=0, parts=1, before=()):
    n = qkv.shape[0]
    T = B * TOK
    steps = n // B // parts
    offset = part * steps
    opens, closes = part == 0, part == parts - 1
    here = functools.partial(images, B, offset=offset)
    full = here(D, TOK)
    gm = (whole(2 * D, 128), (2 * D, 128), F32)
    sums = [(whole(D, 3 * D), (D, 3 * D), F32)] + ([(whole(PATCH_IN, D), (PATCH_IN, D), F32)] if bottom else [])
    ins = [SCALARS] + ([here(PATCH_IN, TOK), whole(D, PATCH_IN), whole(D, TOK)] if bottom else [full])
    ins += [here(3 * D, TOK), here(8, TOK), full, full, HALF_MODS if bottom else MODS, whole(D, 3 * D), COND]
    ins += [] if bottom else [whole(2 * D, 128)]
    args = (table,) + tuple(source) + (qkv, lse, go, gmid, mods, wqkv, cond) + (() if bottom else (gmf,))
    if not opens:
        ins += [gm[0]] + [s[0] for s in sums]
        args += tuple(before)
    outs = ([] if bottom else [(full, (n, D, TOK), F32)]) + [gm] + (halves(pack) if closes else sums)
    scratch = ([(pack, BF)] if closes else []) + [((D, T), BF), ((3 * D, T), BF)]
    scratch += [((D, T), BF), ((PATCH_IN, T), BF)] if bottom else []
    scratch += [(s[1], F32) for s in sums] if closes else []
    return run_kernel(
        functools.partial(att_bwd_kernel, B, offset, bottom, opens, closes), steps, ins, outs, scratch,
        2 * n * TOK * (6 * D * D + 5 * D * TOK) // parts, args)


FREQ = 256
CLASSES = 1000
GRID = 16
LAYERS = 2
MOMENTUM = 0.9
LEARN = 30.0
DECAY = 0.7
IMAGES_PER_STEP = 2
SMALL_COST = 8 * 10**9


def plan(steps_in):
    anchor = math.cos(0.5 * math.pi * 0.008 / 1.008)
    fraction = (steps_in.astype(F32) / 1000.0 + 0.008) / 1.008
    levels = jnp.cos(0.5 * math.pi * fraction)
    return levels * levels / (anchor * anchor)


def time_features(steps_in):
    half_width = FREQ // 2
    frequencies = jnp.exp(-math.log(10000.0) * jnp.arange(half_width, dtype=F32) / half_width)
    angles = steps_in.astype(F32)[:, None] * frequencies[None, :]
    return jnp.concatenate([jnp.cos(angles), jnp.sin(angles)], axis=1)


def positions():
    quarter = D // 4
    omegas = jnp.exp(-math.log(10000.0) * jnp.arange(quarter, dtype=F32) / quarter)
    places = jnp.arange(GRID * GRID, dtype=jnp.int32)
    column = omegas[:, None] * (places % GRID).astype(F32)[None, :]
    row_pos = omegas[:, None] * (places // GRID).astype(F32)[None, :]
    return jnp.concatenate(
        [jnp.sin(column), jnp.cos(column), jnp.sin(row_pos), jnp.cos(row_pos)], axis=0
    )


def swish_parts(values):
    s = 1.0 / (1.0 + jnp.exp(-values))
    return values * s, s * (1.0 + values * (1.0 - s))


def advance(weight, moment, average, gradient):
    new_moment = MOMENTUM * moment + gradient
    new_weight = weight - LEARN * (gradient + MOMENTUM * new_moment)
    new_average = DECAY * average + (1.0 - DECAY) * new_weight
    return (new_weight, new_moment, new_average)


def after(x, *others):
    return lax.optimization_barrier((x,) + others)[0]


def swap(x, axis, mask):
    pairs = [(i, i ^ mask) for i in range(lax.axis_size(axis))]
    return lax.ppermute(x, axis, pairs)


def digit_list(n):
    found, shift = [], 0
    while (1 << shift) < n:
        left = n >> shift
        size = 2 if shift == 0 or left == 2 else 4
        found.append((shift, size))
        shift += size.bit_length() - 1
    return found


def place_of(index, n):
    place = 0
    for shift, size in digit_list(n):
        place = place * size + ((index >> shift) & (size - 1))
    return place


def place_table(emb_rows):
    nr, ng = lax.axis_size("rep"), lax.axis_size("grp")
    me, member = lax.axis_index("rep"), lax.axis_index("grp")
    entries, offsets = [], {}
    for shift, size in digit_list(nr):
        offsets[shift] = len(entries)
        entries += [((me >> shift) & (size - 1)) ^ j for j in range(size)]
    if not entries:
        entries = [0, 1]
    offsets["place"] = len(entries)
    entries += [place_of(me ^ mask, nr) for mask in range(nr)]
    offsets["member"] = len(entries)
    entries += [member ^ k for k in range(ng)]
    offsets["lead"] = len(entries)
    entries.append(emb_rows * member % 16)
    return jnp.stack([jnp.asarray(e, jnp.int32) for e in entries]), offsets


def in_vmem():
    return pl.BlockSpec(memory_space=pltpu.VMEM)


def small_kernel(kernel, outs, scratch, args, scalars=1):
    return pl.pallas_call(
        kernel,
        in_specs=[SCALARS] * scalars + [in_vmem()] * (len(args) - scalars),
        out_specs=[in_vmem()] * len(outs),
        out_shape=[sds(shape, dtype) for shape, dtype in outs],
        scratch_shapes=[pltpu.VMEM(shape, dtype) for shape, dtype in scratch],
        compiler_params=pltpu.CompilerParams(vmem_limit_bytes=VMEM_LIMIT),
        cost_estimate=pl.CostEstimate(flops=SMALL_COST, bytes_accessed=0, transcendentals=0),
    )(*args)


def spread_outer(piece, n):
    pieces = [((0,), piece)]
    digits = digit_list(n)[1:]
    for shift, size in digits:
        if len(pieces) > 1:
            pieces = [(sum((m for m, _ in pieces), ()), jnp.concatenate([v for _, v in pieces], axis=0))]
        masks, value = pieces[0]
        pieces = pieces + [
            (tuple(m ^ (j << shift) for m in masks), swap(value, "rep", j << shift)) for j in range(1, size)
        ]
    return pieces


def spread_core(pieces, n):
    if n == 1:
        return pieces
    return pieces + [(tuple(m ^ 1 for m in masks), swap(value, "rep", 1)) for masks, value in pieces]


def gather_members(mine):
    got = [swap(mine, "grp", k) for k in range(1, lax.axis_size("grp"))]
    return jnp.concatenate(got, axis=0) if got else None


def sum_parts(parts):
    total = parts[0][...].astype(F32)
    for part in parts[1:]:
        total = total + part[...].astype(F32)
    return total.astype(BF)


def rows_kernel(count, offset, table_ref, *refs):
    parts, outs, total_ref = refs[:count], refs[count:-1], refs[-1]
    total_ref[...] = sum_parts(parts)
    split_pack(total_ref, table_ref, offset, outs)


def members_kernel(counts, offset, has_extra, table_ref, *refs):
    refs = list(refs)
    groups = [[refs.pop(0) for _ in range(c)] for c in counts]
    extra_ref = refs.pop(0) if has_extra else None
    outs, totals = refs[: -len(counts)], refs[-len(counts) :]
    for parts, total_ref in zip(groups, totals):
        total_ref[...] = sum_parts(parts)
    for k, out_ref in enumerate(outs):
        at = 0
        for total_ref in totals:
            rows = total_ref.shape[1]
            out_ref[at : at + rows, :] = total_ref[table_ref[offset + k]]
            at += rows
        if has_extra:
            out_ref[at:, :] = extra_ref[...]


def last_kernel(count, extra, table_ref, *refs):
    parts, out_ref = refs[:count], refs[-1]
    rows = parts[0].shape[0] - extra
    total = parts[0][0:rows, :].astype(F32)
    for part in parts[1:]:
        total = total + part[0:rows, :].astype(F32)
    out_ref[0:rows, :] = total.astype(BF)
    if extra:
        for i, part in enumerate(parts):
            out_ref[rows + extra * i : rows + extra * (i + 1), :] = part[rows:, :]


def reduce_first(keep, send):
    return [keep, swap(send, "rep", 1)] if lax.axis_size("rep") > 1 else [keep]


def reduce_outer(parts, table, offsets, number):
    shift, size = digit_list(lax.axis_size("rep"))[number]
    ng, rows, _ = parts[0].shape
    one = lambda r: pl.BlockSpec((1, r, D), lambda i: (i, 0, 0))
    cut = pl.pallas_call(
        functools.partial(rows_kernel, len(parts), offsets[shift]),
        grid=(ng,),
        in_specs=[SCALARS] + [one(rows)] * len(parts),
        out_specs=[one(rows // size)] * size,
        out_shape=[sds((ng, rows // size, D), BF)] * size,
        scratch_shapes=[pltpu.VMEM((1, rows, D), BF)],
    )(table, *parts)
    return [cut[0]], cut[1:], shift


def exchange(own, sends, axis, shift):
    return own + [swap(x, axis, (j + 1) << shift) for j, x in enumerate(sends)]


def reduce_members(groups, extra, table, offsets):
    ng = groups[0][0].shape[0]
    rows = sum(g[0].shape[1] for g in groups) + (0 if extra is None else extra.shape[0])
    cut = small_kernel(
        functools.partial(members_kernel, tuple(len(g) for g in groups), offsets["member"], extra is not None),
        [((rows, D), BF)] * ng, [(g[0].shape, BF) for g in groups],
        (table, *sum(groups, []), *([] if extra is None else [extra])),
    )
    return [cut[0]], cut[1:], 0


def reduce_last(parts, extra, table):
    rows = parts[0].shape[0] + extra * (len(parts) - 1)
    return small_kernel(
        functools.partial(last_kernel, len(parts), extra), [((rows, D), BF)], [], (table, *parts)
    )[0]


def pack_first_kernel(lead_at, emb_real, shard_place, table_ref, emb_ref, wa_ref, wqkv_ref, shard_ref, mine_ref, wide_ref):
    wide_ref[...] = jnp.zeros_like(wide_ref)
    wide_ref[0:emb_real, :] = emb_ref[...]
    seg = wide_ref.shape[0]
    shard_ref[0:seg, :] = pltpu.roll(wide_ref[...], table_ref[lead_at], 0).astype(BF)
    at = seg
    for ref in (wa_ref, wqkv_ref):
        for c in range(3):
            rows = ref.shape[1]
            shard_ref[at : at + rows, :] = ref[0, :, D * c : D * (c + 1)].astype(BF)
            at += rows
    if at < shard_ref.shape[0]:
        shard_ref[at:, :] = jnp.zeros_like(shard_ref[at:, :])
    rows = mine_ref.shape[0]
    mine_ref[...] = shard_ref[pl.ds(pl.multiple_of(table_ref[shard_place] * rows, rows), rows), :]


def pack_first(table, offsets, emb_table, w_in, seg, unit):
    nr = lax.axis_size("rep")
    rows = w_in.shape[1]
    total = -(-(seg + 6 * rows) // unit) * unit
    part = lambda c: pl.BlockSpec((1, rows, 3 * D), lambda i: (0, 0, c))
    return pl.pallas_call(
        functools.partial(pack_first_kernel, offsets["lead"], emb_table.shape[0], offsets["place"]),
        grid=(1,),
        in_specs=[SCALARS, whole(*emb_table.shape), part(0), part(2)],
        out_specs=[whole(total, D), whole(total // nr, D)],
        out_shape=[sds((total, D), BF), sds((total // nr, D), BF)],
        scratch_shapes=[pltpu.VMEM((seg, D), F32)],
        compiler_params=pltpu.CompilerParams(vmem_limit_bytes=VMEM_LIMIT),
    )(table, emb_table, w_in, w_in)


def pack_other_kernel(layouts, shard_place, table_ref, *refs):
    refs = list(refs)
    inputs = [[refs.pop(0) for _ in layout] for layout in layouts]
    shard_refs, mine_ref = refs[:-1], refs[-1]
    put = 0
    for layout, ins, shard_ref in zip(layouts, inputs, shard_refs):
        at = 0
        for ref, count in zip(ins, layout):
            rows = ref.shape[-2]
            for c in range(count):
                cols = slice(D * c, D * (c + 1))
                value = ref[0, :, cols] if len(ref.shape) == 3 else ref[:, cols]
                shard_ref[at : at + rows, :] = value.astype(BF)
                at += rows
            if len(ref.shape) == 2:
                value = ref[:, D * count :]
                shard_ref[at : at + rows, :] = jnp.concatenate(
                    [value, jnp.zeros((rows, D - value.shape[1]), F32)], axis=1
                ).astype(BF)
                at += rows
        if at < shard_ref.shape[0]:
            shard_ref[at:, :] = jnp.zeros_like(shard_ref[at:, :])
        rows = shard_ref.shape[0] * mine_ref.shape[0] // sum(r.shape[0] for r in shard_refs)
        from_rows = pl.ds(pl.multiple_of(table_ref[shard_place] * rows, rows), rows)
        mine_ref[put : put + rows, :] = shard_ref[from_rows, :]
        put += rows


def pack_other(table, offsets, shards):
    nr = lax.axis_size("rep")
    spec = lambda shape, index: pl.BlockSpec(shape, lambda i: index)
    parts = sum((p for _, p in shards), [])
    shapes = [(rows, D) for rows, _ in shards] + [(sum(rows for rows, _ in shards) // nr, D)]
    return pl.pallas_call(
        functools.partial(
            pack_other_kernel, tuple(tuple(p[3] for p in ps) for _, ps in shards), offsets["place"]
        ),
        grid=(1,),
        in_specs=[SCALARS] + [spec(p[1], p[2]) for p in parts],
        out_specs=[whole(*shape) for shape in shapes],
        out_shape=[sds(shape, BF) for shape in shapes],
        compiler_params=pltpu.CompilerParams(vmem_limit_bytes=VMEM_LIMIT),
    )(table, *[p[0] for p in parts])


def fill_full(full_ref, masks, place, member, table_ref, shard_ref, pieces):
    ng = full_ref.shape[0]
    full_ref[table_ref[member]] = shard_ref[...]
    for group, ref in zip(masks, pieces):
        rows = ref.shape[0] // (len(group) * (ng - 1))
        for i, mask in enumerate(group):
            at = pl.ds(pl.multiple_of(table_ref[place + mask] * rows, rows), rows)
            for k in range(1, ng):
                start = (i * (ng - 1) + k - 1) * rows
                full_ref[table_ref[member + k], at, :] = ref[start : start + rows, :]


def take_blocks(full_ref, start, count, out_ref):
    ng = full_ref.shape[0]
    step = D // ng
    for g in range(ng):
        for c in range(count):
            out_ref[step * g : step * (g + 1), D * c : D * (c + 1)] = full_ref[
                g, start + step * c : start + step * (c + 1), :
            ]
    return start + step * count


def take_outer(full_ref, start, wo_ref, wg_ref):
    ng = full_ref.shape[0]
    wide = (D + FF) // ng
    for g in range(ng):
        low, high = wide * g, wide * (g + 1)
        if low < D:
            cut = min(high, D)
            wo_ref[low:cut, :] = full_ref[g, start : start + cut - low, :]
        if high > D:
            cut = max(low, D)
            wg_ref[cut - D : high - D, :] = full_ref[g, start + cut - low : start + wide, :]
    return start + wide


def first_kernel(emb_rows, seg, masks, place, member, table_ref, shard_ref, feats_ref, labels_ref, *refs):
    pieces, rest = refs[: len(masks)], refs[len(masks) :]
    (wp_t_ref, w2_ref, wa_ref, wqkv_ref, wqkv_t_ref, mods_ref, time_act_ref, pre_ref, cond_ref, act_t_ref,
     full_ref, emb_ref) = rest
    fill_full(full_ref, masks, place, member, table_ref, shard_ref, pieces)
    ng = full_ref.shape[0]
    emb_ref[...] = jnp.zeros_like(emb_ref)
    for g in range(ng):
        base = emb_rows * g // 16 * 16
        emb_ref[base : base + seg, :] = emb_ref[base : base + seg, :] + full_ref[g, 0:seg, :]
    at = take_blocks(full_ref, seg, 3, wa_ref)
    take_blocks(full_ref, at, 3, wqkv_ref)
    wqkv_t_ref[...] = wqkv_ref[...].T
    wp_t_ref[...] = emb_ref[0:128, :].T[:, 0:PATCH_IN]
    w1 = emb_ref[PATCH_IN : PATCH_IN + FREQ, :]
    w2_ref[...] = emb_ref[PATCH_IN + FREQ : PATCH_IN + FREQ + D, :]
    classes = emb_ref[PATCH_IN + FREQ + D : PATCH_IN + FREQ + D + CLASSES + 8, :]
    pre = mm(feats_ref[...], w1)
    pre_ref[...] = pre
    time_act = swish_parts(pre)[0].astype(BF)
    time_act_ref[...] = time_act
    hot = labels_ref[...] == lax.broadcasted_iota(jnp.int32, (labels_ref.shape[0], CLASSES + 8), 1)
    cond = mm(time_act, w2_ref[...]) + mm(jnp.where(hot, 1.0, 0.0).astype(BF), classes)
    cond_ref[...] = cond
    act = swish_parts(cond)[0]
    act_t_ref[...] = act.T.astype(BF)
    mods_ref[...] = mm(wa_ref[...].T, act_t_ref[...])


def second_kernel(masks, place, member, table_ref, shard_ref, act_t_ref, *refs):
    pieces, rest = refs[: len(masks)], refs[len(masks) :]
    wo_ref, wg_ref, wo_t_ref, wg_t_ref, wf_ref, wf_t_ref, wa_ref, mods_ref, full_ref = rest
    fill_full(full_ref, masks, place, member, table_ref, shard_ref, pieces)
    at = take_outer(full_ref, 0, wo_ref, wg_ref)
    at = take_blocks(full_ref, at, 4, wf_ref)
    take_blocks(full_ref, at, 3, wa_ref)
    wo_t_ref[...] = wo_ref[...].T
    wg_t_ref[...] = wg_ref[...].T
    wf_t_ref[...] = wf_ref[...].T
    mods_ref[...] = mm(wa_ref[...].T, act_t_ref[...])


def third_kernel(masks, place, member, table_ref, shard_ref, act_t_ref, *refs):
    pieces, rest = refs[: len(masks)], refs[len(masks) :]
    (wo_ref, wg_ref, wo_t_ref, wg_t_ref, wf_ref, wf_t_ref, wqkv_ref, wqkv_t_ref, wa_ref, wm_ref, wy_ref, wy_t_ref,
     mods_ref, modf_ref, full_ref, wide_ref) = rest
    fill_full(full_ref, masks, place, member, table_ref, shard_ref, pieces)
    at = take_outer(full_ref, 0, wo_ref, wg_ref)
    at = take_blocks(full_ref, at, 6, wa_ref)
    at = take_blocks(full_ref, at, 3, wqkv_ref)
    at = take_blocks(full_ref, at, 4, wf_ref)
    at = take_blocks(full_ref, at, 2, wm_ref)
    take_blocks(full_ref, at, 1, wide_ref)
    wo_t_ref[...] = wo_ref[...].T
    wg_t_ref[...] = wg_ref[...].T
    wf_t_ref[...] = wf_ref[...].T
    wqkv_t_ref[...] = wqkv_ref[...].T
    wy_ref[...] = wide_ref[:, 0:PATCH_IN]
    wy_t_ref[...] = wide_ref[...].T[0:PATCH_IN, :]
    mods_ref[...] = mm(wa_ref[...].T, act_t_ref[...])
    modf_ref[...] = mm(wm_ref[...].T, act_t_ref[...])


def assemble(kernel, table, offsets, shard, pieces, extra, outs, scratch):
    ng = lax.axis_size("grp")
    masks = tuple(m for m, v in pieces if v is not None)
    arrays = [v for _, v in pieces if v is not None]
    return small_kernel(
        functools.partial(kernel, masks, offsets["place"], offsets["member"]), outs,
        [((ng,) + shard.shape, BF)] + scratch, (table, shard, *extra, *arrays),
    )


def cond_back_kernel(n, table_ref, gma0_ref, gmb0_ref, gma1_ref, gmb1_ref, gmf_ref, wa0a_ref, wa0b_ref, wa1_ref, wm_ref,
                     w2_ref, cond_ref, pre_ref, time_act_ref, feats_ref, label_ref, squares_ref, rows_ref):
    low = lambda ref: ref[...].astype(BF)
    gact = mm(wm_ref[...], low(gmf_ref))
    gact += mm(wa1_ref[:, 0 : 2 * D], low(gma1_ref)) + mm(wa1_ref[:, 2 * D :], low(gmb1_ref))
    gact += mm(wa0a_ref[:, 0 : 2 * D], low(gma0_ref)) + mm(wa0a_ref[:, 2 * D :], gmb0_ref[0:D, :].astype(BF))
    gact += mm(wa0b_ref[...], gmb0_ref[D:, :].astype(BF))
    gcond = gact.T * swish_parts(cond_ref[...])[1]
    gpre = mm_nt(gcond.astype(BF), w2_ref[...]) * swish_parts(pre_ref[...])[1]
    total = jnp.sum(squares_ref[...]).reshape(1, 1)
    high = total.astype(BF).astype(F32)
    middle = (total - high).astype(BF).astype(F32)
    last = total - high - middle
    lane = lax.broadcasted_iota(jnp.int32, (n, 128), 1)
    row = lax.broadcasted_iota(jnp.int32, (n, 128), 0)
    loss = jnp.where(lane == 0, high, jnp.where(lane == 1, middle, jnp.where(lane == 2, last, 0.0)))
    loss = jnp.where(row == 0, loss, 0.0)
    loss = jnp.where(lane == 3, label_ref[:, 0:1], jnp.where(lane == 4, label_ref[:, 1:2], loss))
    top = jnp.concatenate([time_act_ref[...].astype(F32)[0:n], gpre[0:n]], axis=0)
    feats = jnp.concatenate([feats_ref[...].astype(F32)[0:n], loss], axis=1)
    rows_ref[0 : 2 * n, :] = top.astype(BF)
    rows_ref[2 * n : 4 * n, :] = jnp.concatenate([gcond[0:n], feats], axis=0).astype(BF)


def emb_grad_kernel(n, inv_entries, counts, extra, table_ref, *refs):
    pieces, (grad_ref, loss_ref, left_ref, right_ref) = refs[: len(counts)], refs[len(counts) :]
    at = 0
    for ref, count in zip(pieces, counts):
        each = ref.shape[0] // count
        for i in range(count):
            for base in range(each * (i + 1) - extra, each * (i + 1), 4 * n):
                left_ref[at : at + 2 * n, :] = ref[base : base + 2 * n, :]
                right_ref[at : at + 2 * n, :] = ref[base + 2 * n : base + 4 * n, :]
                at += 2 * n
    total = left_ref.shape[0]
    row = lax.broadcasted_iota(jnp.int32, (total, D), 0)
    top = (row % (2 * n)) < n
    zero = jnp.zeros((total, D), BF)
    act = jnp.where(top, left_ref[...], zero)
    gcond = jnp.where(top, right_ref[...], zero)
    gpre = jnp.where(top, zero, left_ref[...])
    feats = right_ref[:, 0:FREQ]
    tags = right_ref[:, FREQ:].astype(F32).T
    label = (tags[3:4, :] * 32.0 + tags[4:5, :]).astype(jnp.int32)
    label = pltpu.roll(jnp.broadcast_to(label, (8, total)), total - n, 1)[0:1, :]
    hot = label == lax.broadcasted_iota(jnp.int32, (CLASSES + 8, total), 0)
    grad_ref[0:PATCH_IN, :] = jnp.zeros((PATCH_IN, D), F32)
    grad_ref[PATCH_IN : PATCH_IN + FREQ, :] = mm(feats.T, gpre)
    grad_ref[PATCH_IN + FREQ : PATCH_IN + FREQ + D, :] = mm(act.T, gcond)
    grad_ref[PATCH_IN + FREQ + D :, :] = mm(jnp.where(hot, 1.0, 0.0).astype(BF), gcond)
    spot = lax.broadcasted_iota(jnp.int32, tags.shape, 1) % (2 * n) >= n
    spot &= lax.broadcasted_iota(jnp.int32, tags.shape, 0) < 3
    loss_ref[...] = jnp.sum(jnp.where(spot, tags, 0.0)).reshape(1, 1) * inv_entries


def update_kernel(masks, place, sizes, step_rows, layout, extra, n_chain, table_ref, *refs):
    pieces, refs = refs[: len(masks)], refs[len(masks) :]
    states, refs = refs[:6], refs[6 + n_chain :]
    news, rest_refs, shard_refs = refs[:6], refs[6 : 6 + len(sizes)], refs[6 + len(sizes) :]
    step = pl.program_id(0)

    @pl.when(step == 0)
    def _():
        for group, ref in zip(masks, pieces):
            each = ref.shape[0] // len(group)
            for i, mask in enumerate(group):
                start = each * i
                for rows, shard_ref in zip(sizes, shard_refs):
                    at = pl.ds(pl.multiple_of(table_ref[place + mask] * rows, rows), rows)
                    shard_ref[at, :] = ref[start : start + rows, :]
                    start += rows
        for rest_ref, shard_ref in zip(rest_refs, shard_refs):
            rest_ref[...] = shard_ref[shard_ref.shape[0] - rest_ref.shape[0] :, :].astype(F32)

    out_rows = states[0].shape[1]
    at = pl.multiple_of(step * out_rows, 16)
    grad = shard_refs[0][pl.ds(at, out_rows), :].astype(F32)
    for ref, value in zip(news[:3], advance(*(r[0] for r in states[:3]), grad)):
        ref[0] = value
    for group, row, block in layout:
        cols = slice(D * block, D * (block + 1))
        at = pl.multiple_of(row + step * step_rows, 16)
        grad = shard_refs[group][pl.ds(at, step_rows), :].astype(F32)
        for ref, value in zip(news[3:], advance(*(r[0, :, cols] for r in states[3:]), grad)):
            ref[0, :, cols] = value


def update(table, offsets, pieces, layer, packs, extra, outer, inner, chain):
    nr = lax.axis_size("rep")
    rows, wide = inner[0].shape[1], inner[0].shape[2]
    rows_out = outer[0].shape[1]
    step_rows = 16
    steps = rows // step_rows
    masks = tuple(m for m, _ in pieces)
    arrays = [v for _, v in pieces]
    sizes = tuple(p[1] // nr for p in packs)
    layout = [(0, rows_out + rows * i, 9 + i) for i in range(4)]
    layout += [(0, rows_out + rows * (4 + i), 2 + i) for i in range(4)]
    layout += [(1, rows * i, 6 + i) for i in range(3)] + [(1, rows * (3 + i), i) for i in range(2)]
    rests = [packs[0][1] - rows_out - 8 * rows, packs[1][1] - 5 * rows]
    in_spec = pl.BlockSpec((1, step_rows, wide), lambda i: (layer, i, 0))
    out_spec = pl.BlockSpec((1, rows_out // steps, D), lambda i: (layer, i, 0))
    states = list(outer) + list(inner)
    specs = [out_spec] * 3 + [in_spec] * 3
    chain = list(chain) if chain else []
    first = 1 + len(arrays) + len(states)
    return pl.pallas_call(
        functools.partial(
            update_kernel, masks, offsets["place"], sizes, step_rows, tuple(layout), extra, len(chain)
        ),
        grid=(steps,),
        in_specs=[SCALARS] + [whole(*a.shape) for a in arrays] + specs
        + [pl.BlockSpec(memory_space=pl.ANY)] * len(chain),
        out_specs=specs + [whole(r, D) for r in rests],
        out_shape=[sds(s.shape, F32) for s in states] + [sds((r, D), F32) for r in rests],
        scratch_shapes=[pltpu.VMEM((p[1], D), BF) for p in packs],
        input_output_aliases={first + i: i for i in range(len(chain))},
        compiler_params=pltpu.CompilerParams(vmem_limit_bytes=VMEM_LIMIT),
    )(table, *arrays, *states, *chain)


def local(
    latents, noise, timesteps, labels, emb_table, emb_mom, emb_ema, w_in, in_mom, in_ema,
    w_out, out_mom, out_ema, head, head_mom, head_ema,
):
    nr, ng = lax.axis_size("rep"), lax.axis_size("grp")
    member = lax.axis_index("grp")
    n = latents.shape[0]
    B = IMAGES_PER_STEP
    unit = 16 * nr
    digits = digit_list(nr)
    rows_d = D // ng
    rows_out = (D + FF) // ng
    emb_rows = emb_table.shape[0]
    seg = -(-(emb_rows + 15) // 16) * 16
    emb_full = emb_rows * (ng - 1) // 16 * 16 + seg
    full_rows = lambda rows: -(-rows // unit) * unit
    table, offsets = place_table(emb_rows)

    shard1, mine1 = pack_first(table, offsets, emb_table, w_in, seg, unit)
    got1 = gather_members(mine1)
    three, one = (1, rows_d, 3 * D), (1, rows_d, D)
    shard2, shard3, mine23 = pack_other(
        table, offsets,
        [
            (full_rows(rows_out + 7 * rows_d),
             [(w_out, (1, rows_out, D), (0, 0, 0), 1), (w_in, three, (0, 0, 3), 3), (w_in, one, (0, 0, 12), 1),
              (w_in, three, (0, 0, 1), 3)]),
            (full_rows(rows_out + 16 * rows_d),
             [(w_out, (1, rows_out, D), (1, 0, 0), 1), (w_in, (1, rows_d, 13 * D), (1, 0, 0), 13),
              (head, head.shape, (0, 0), 2)]),
        ],
    )
    around1 = spread_outer(after(got1, mine23), nr)
    cut2 = shard2.shape[0] // nr
    came1 = [v for m, v in around1 if m != (0,)]
    got2 = gather_members(after(mine23[:cut2], came1[0]))
    around2 = spread_outer(got2, nr)
    mine3 = after(mine23[cut2:], *came1, got2)
    got3 = [swap(mine3, "grp", k) for k in range(1, ng)]

    levels = plan(timesteps)
    noise_level = jnp.sqrt(jnp.maximum(1.0 - levels, 0.0))
    noisy = (
        jnp.sqrt(levels)[:, None, None] * latents.astype(F32)
        + noise_level[:, None, None] * noise.astype(F32)
    ).astype(BF)
    feats = jnp.pad(time_features(timesteps).astype(BF), ((0, 128 - n), (0, 0)))
    label_column = jnp.pad(labels, (0, 128 - n), constant_values=-1)[:, None]
    label_parts = jnp.pad(
        jnp.stack([labels >> 5, labels & 31], axis=1).astype(F32), ((0, 0), (0, 126))
    )
    pos = positions()

    pieces1 = spread_core(
        [(sum((m for m, _ in around1), ()), jnp.concatenate([v for _, v in around1], axis=0))], nr
    )
    wp_t, w2, wa0a, wqkv0, wqkv0_t, mods0a, time_act, pre_time, cond, act_t = assemble(
        functools.partial(first_kernel, emb_rows, seg), table, offsets, shard1, pieces1,
        (feats, label_column),
        [((D, PATCH_IN), BF), ((D, D), BF), ((D, 3 * D), BF), ((D, 3 * D), BF), ((3 * D, D), BF),
         ((3 * D, 128), F32), ((128, D), BF), ((128, D), F32), ((128, D), F32), ((D, 128), BF)],
        [((emb_full, D), BF)],
    )
    early = att_forward(noisy, wp_t, pos, after(mods0a, got2), wqkv0_t, B, 0, 2, ())
    got3 = [after(g, early[0]) for g in got3]
    got3 = jnp.concatenate(got3, axis=0)
    around3 = spread_outer(got3, nr)
    qkv0, lse0, att0 = att_forward(noisy, wp_t, pos, after(mods0a, got3), wqkv0_t, B, 1, 2, early)
    pieces2 = spread_core([(m, after(v, att0)) for m, v in around2], nr)
    wo0, wg0, wo0_t, wg0_t, wf0, wf0_t, wa0b, mods0b = assemble(
        second_kernel, table, offsets, shard2, pieces2, (act_t,),
        [((D, D), BF), ((FF, D), BF), ((D, D), BF), ((D, FF), BF), ((D, FF), BF), ((FF, D), BF),
         ((D, 3 * D), BF), ((3 * D, 128), F32)],
        [],
    )
    mid0, bra0, brb0, hid1 = ffn_forward(noisy, wp_t, pos, att0, mods0a, mods0b, wo0_t, wf0_t, wg0_t, B)
    pieces3 = spread_core([(m, after(v, hid1)) for m, v in around3], nr)
    (wo1, wg1, wo1_t, wg1_t, wf1, wf1_t, wqkv1, wqkv1_t, wa1, wm, wy, wy_t, mods1, modf) = assemble(
        third_kernel, table, offsets, shard3, pieces3, (act_t,),
        [((D, D), BF), ((FF, D), BF), ((D, D), BF), ((D, FF), BF), ((D, FF), BF), ((FF, D), BF),
         ((D, 3 * D), BF), ((3 * D, D), BF), ((D, 6 * D), BF), ((D, 2 * D), BF), ((D, PATCH_IN), BF),
         ((PATCH_IN, D), BF), ((6 * D, 128), F32), ((2 * D, 128), F32)],
        [((D, D), BF)],
    )
    entries = n * nr * ng * TOK * PATCH_IN
    outer_pack = (ng, full_rows(rows_out + 8 * rows_d + PATCH_IN), D)
    qkv_pack1 = (ng, full_rows(7 * rows_d), D)
    qkv_pack0 = (ng, full_rows(5 * rows_d + PATCH_IN), D)
    qkv1, lse1, go1, gmid1, gmb1, gmf, squares, keep_f1, send_f1 = block_step(
        table, hid1, noise, mods1, modf, wqkv1_t, wo1_t, wf1_t, wg1_t, wo1, wf1, wg1, wy_t, wy, act_t,
        float(entries), B, outer_pack,
    )
    parts_f1 = reduce_first(keep_f1, send_f1)
    ghid1, gma1, keep_a1, send_a1 = att_backward(
        table, (hid1,), qkv1, lse1, go1, gmid1, mods1, wqkv1, act_t, gmf, B, False, qkv_pack1
    )
    parts_a1 = reduce_first(keep_a1, send_a1)

    def outer_stage(parts):
        sends = []
        for number in range(1, len(digits)):
            own, sends, shift = reduce_outer(parts, table, offsets, number)
            parts = exchange(own, sends, "rep", shift)
        return parts, sends

    def member_stage(groups, extra):
        own, sends, shift = reduce_members(groups, extra, table, offsets)
        return exchange(own, sends, "grp", shift), sends

    def held(parts, *marks):
        return [parts[0]] + [after(p, *marks) for p in parts[1:]]

    parts_f1, sends_f1 = outer_stage(held(parts_f1, ghid1))
    go0, gmid0, gmb0, keep_f0, send_f0 = ffn_backward(
        table, after(ghid1, *sends_f1), mid0, att0, bra0, brb0, mods0a, mods0b, wf0_t, wo0, wf0, wg0, act_t,
        B, outer_pack,
    )
    parts_f0 = reduce_first(keep_f0, send_f0)
    parts_f1 = held(parts_f1, gmid0)
    parts_a1, sends_a1 = outer_stage(held(parts_a1, gmid0, *parts_f1[1:]))
    back0 = functools.partial(
        att_backward, table, (noisy, wp_t, pos), qkv0, lse0, go0, mods=mods0a, wqkv=wqkv0, cond=act_t, gmf=None,
        B=B, bottom=True, pack=qkv_pack0, parts=2,
    )
    half = back0(gmid=after(gmid0, *sends_a1), part=0)
    mark = half[0]
    parts_1, sends_1 = member_stage([parts_f1, held(parts_a1, mark)], None)
    parts_f0, sends_f0 = outer_stage([after(p, *sends_1) for p in held(parts_f0, mark)])
    gma0, keep_a0, send_a0 = back0(gmid=after(gmid0, *sends_f0), part=1, before=half)
    parts_a0 = reduce_first(keep_a0, send_a0)
    parts_f0 = held(parts_f0, gma0)
    piece_1 = reduce_last(held(parts_1, gma0), 0, table)
    rows0 = small_kernel(
        functools.partial(cond_back_kernel, n), [((4 * n, D), BF)], [],
        (table, after(gma0, piece_1), gmb0, gma1, gmb1, gmf, wa0a, wa0b, wa1, wm, w2, cond, pre_time,
         time_act, feats, label_parts, squares),
    )[0]
    parts_a0, sends_a0 = outer_stage(held(parts_a0, rows0, *parts_f0[1:]))
    pieces_1 = spread_core(spread_outer(piece_1, nr), nr)
    outer_state, inner_state = (w_out, out_mom, out_ema), (w_in, in_mom, in_ema)
    new_1 = update(table, offsets, pieces_1, 1, (outer_pack, qkv_pack1), 0, outer_state, inner_state, None)
    parts_0, sends_0 = member_stage([parts_f0, parts_a0], rows0)
    piece_0 = reduce_last(parts_0, 4 * n, table)
    pieces_0 = spread_core(spread_outer(piece_0, nr), nr)
    extra = ng * 4 * n
    new_0 = update(table, offsets, pieces_0, 0, (outer_pack, qkv_pack0), extra, outer_state, inner_state, new_1[:6])
    emb_grad, loss_value = small_kernel(
        functools.partial(emb_grad_kernel, n, 1.0 / entries, tuple(len(m) for m, _ in pieces_0), extra),
        [((emb_full, D), F32), ((1, 1), F32)], [((2 * n * nr * ng, D), BF)] * 2,
        (table, *[v for _, v in pieces_0]),
    )
    emb_grad = lax.dynamic_slice_in_dim(emb_grad, member * emb_rows, emb_rows, 0)
    patch_grad = jnp.where(member == 0, new_0[7][:PATCH_IN], 0.0)
    emb_new = advance(
        emb_table, emb_mom, emb_ema, emb_grad + jnp.pad(patch_grad, ((0, emb_rows - PATCH_IN), (0, 0)))
    )
    wm_grad = new_1[7][: 2 * rows_d].reshape(2, rows_d, D).transpose(1, 0, 2).reshape(rows_d, 2 * D)
    wy_grad = lax.dynamic_slice_in_dim(new_1[6][:PATCH_IN], member * rows_d, rows_d, 1).T
    head_new = advance(head, head_mom, head_ema, jnp.concatenate([wm_grad, wy_grad], axis=1))
    return (loss_value.reshape(()), *emb_new, *new_0[3:6], *new_0[:3], *head_new)


def solution(mesh):
    data = P(("rep", "grp"), None, None)
    vector = P(("rep", "grp"))
    flat = P("grp", None)
    deep = P(None, "grp", None)
    return jax.shard_map(
        local,
        mesh=mesh,
        in_specs=(data, data, vector, vector, flat, flat, flat, deep, deep, deep, deep, deep, deep,
                  flat, flat, flat),
        out_specs=(P(), flat, flat, flat, deep, deep, deep, deep, deep, deep, flat, flat, flat),
        check_vma=False,
    )
```

```python
import functools
import math

import jax
import jax.numpy as jnp
from jax import lax
from jax.experimental import pallas as pl
from jax.experimental.pallas import tpu as pltpu
from jax.sharding import PartitionSpec as P

D = 384
HEADS = 6
HEAD_DIM = 64
FF = 1536
TOK = 256
PATCH_IN = 16
EPSILON = 1e-06
BF = jnp.bfloat16
F32 = jnp.float32
VMEM_LIMIT = 58 * 1024 * 1024


def mm(left, right):
    return lax.dot_general(left, right, (((1,), (0,)), ((), ())), preferred_element_type=F32)


def mm_nt(left, right):
    return lax.dot_general(left, right, (((1,), (1,)), ((), ())), preferred_element_type=F32)


def norm_parts(x):
    centered = x - jnp.mean(x, axis=0, keepdims=True)
    variance = jnp.mean(centered * centered, axis=0, keepdims=True)
    inv = lax.rsqrt(variance + EPSILON)
    return centered * inv, inv


def norm_back(d, normed, inv, scale1):
    dn = d * scale1
    m1 = jnp.mean(dn, axis=0, keepdims=True)
    m2 = jnp.mean(dn * normed, axis=0, keepdims=True)
    return (dn - m1 - normed * m2) * inv


def column(mods_ref, index, image):
    block = mods_ref[pl.ds(index * D, D), :]
    lane = lax.broadcasted_iota(jnp.int32, block.shape, 1)
    return jnp.sum(jnp.where(lane == image, block, 0.0), axis=1, keepdims=True)


def put_column(out_ref, index, image, values):
    total = jnp.sum(values, axis=1, keepdims=True)
    rows = pl.ds(index * D, D)
    old = out_ref[rows, :]
    lane = lax.broadcasted_iota(jnp.int32, old.shape, 1)
    out_ref[rows, :] = jnp.where(lane == image, total, old)


def half_zero(x, half):
    row = lax.broadcasted_iota(jnp.int32, x.shape, 0)
    keep = row < HEAD_DIM if half == 0 else row >= HEAD_DIM
    return jnp.where(keep, x, jnp.zeros_like(x))


def head_groups(B):
    work = [(b, h) for b in range(B) for h in range(HEADS)]
    return [work[i : i + HEAD_GROUP] for i in range(0, len(work), HEAD_GROUP)]


def pair_rows(ref, b, h, base=0):
    lo = base + 2 * HEAD_DIM * (h // 2)
    return ref[b, lo : lo + 2 * HEAD_DIM, :]


def head_rows(ref, b, h, base=0):
    return ref[b, base + HEAD_DIM * h : base + HEAD_DIM * (h + 1), :]


def attention_forward(qkv_ref, B, lse_ref, att_ref):
    for work in head_groups(B):
        scores = [
            mm(pair_rows(qkv_ref, b, h, D).T, half_zero(pair_rows(qkv_ref, b, h), h % 2)) for b, h in work
        ]
        peaks = [jnp.max(x, axis=0, keepdims=True) for x in scores]
        exps = [jnp.exp(x - p) for x, p in zip(scores, peaks)]
        totals = [jnp.sum(x, axis=0, keepdims=True) for x in exps]
        outs = [mm(head_rows(qkv_ref, b, h, 2 * D), x.astype(BF)) for (b, h), x in zip(work, exps)]
        for (b, h), out, total, peak in zip(work, outs, totals, peaks):
            att_ref[HEAD_DIM * h : HEAD_DIM * (h + 1), lanes_of(b)] = (out * (1.0 / total)).astype(BF)
            lse_ref[b, h : h + 1, :] = peak + jnp.log(total)


def attention_backward(qkv_ref, B, lse_ref, go_ref, gqkv_ref):
    for work in head_groups(B):
        scores = [
            mm(pair_rows(qkv_ref, b, h, D).T, half_zero(pair_rows(qkv_ref, b, h), h % 2)) for b, h in work
        ]
        gprobs = [
            mm(pair_rows(qkv_ref, b, h, 2 * D).T, half_zero(pair_rows(go_ref, b, h), h % 2)) for b, h in work
        ]
        probs = [jnp.exp(x - lse_ref[b, h : h + 1, :]) for x, (b, h) in zip(scores, work)]
        inners = [jnp.sum(p * g, axis=0, keepdims=True) for p, g in zip(probs, gprobs)]
        gscores = [(p * (g - i)).astype(BF) for p, g, i in zip(probs, gprobs, inners)]
        gqs = [mm(head_rows(qkv_ref, b, h, D), g) for (b, h), g in zip(work, gscores)]
        gks = [mm_nt(head_rows(qkv_ref, b, h), g) for (b, h), g in zip(work, gscores)]
        gvs = [mm_nt(head_rows(go_ref, b, h), p.astype(BF)) for (b, h), p in zip(work, probs)]
        for (b, h), gq, gk, gv in zip(work, gqs, gks, gvs):
            row = HEAD_DIM * h
            for base, value in ((0, gq * (1.0 / math.sqrt(HEAD_DIM))), (D, gk), (2 * D, gv)):
                gqkv_ref[base + row : base + row + HEAD_DIM, lanes_of(b)] = value.astype(BF)


def project_qkv(wqkv_t_ref, normed_ref, qkv_ref, B):
    for part in range(3):
        qkv = mm(wqkv_t_ref[D * part : D * (part + 1), :], normed_ref[...])
        if part == 0:
            qkv = qkv * (1.0 / math.sqrt(HEAD_DIM))
        qkv = qkv.astype(BF)
        for b in range(B):
            qkv_ref[b, D * part : D * (part + 1), :] = qkv[:, TOK * b : TOK * (b + 1)]


def lanes_of(b):
    return slice(TOK * b, TOK * (b + 1))


def modulate_into(normed_ref, b, normed, scale1, shift):
    normed_ref[:, lanes_of(b)] = (normed * scale1 + shift).astype(BF)


def ffn_chunks():
    return [slice(f, f + FF_CHUNK) for f in range(0, FF, FF_CHUNK)]


def add_up(total, part):
    return part if total is None else total + part


GELU_C = 0.7978845608
GELU_A = 0.044715


def gelu_both(v):
    square = v * v
    t = jnp.tanh(v * (GELU_C + (GELU_C * GELU_A) * square))
    half = 0.5 + 0.5 * t
    slope = half + 0.5 * v * (1.0 - t * t) * (GELU_C + (3.0 * GELU_C * GELU_A) * square)
    return v * half, slope


def gelu_one(v):
    t = jnp.tanh(v * (GELU_C + (GELU_C * GELU_A) * (v * v)))
    return v * (0.5 + 0.5 * t)


def clear(*refs):
    for ref in refs:
        ref[...] = jnp.zeros_like(ref)


FF_CHUNK = 768
HEAD_GROUP = 12


def pack_blocks(pack_ref, start, value):
    members = pack_ref.shape[0]
    rows = D // members
    count = value.shape[1] // D
    for g in range(members):
        for c in range(count):
            pack_ref[g, start + rows * c : start + rows * (c + 1), :] = value[
                rows * g : rows * (g + 1), D * c : D * (c + 1)
            ].astype(BF)
    return start + rows * count


def pack_outer(pack_ref, awo_ref, awf_ref, awg_ref):
    members = pack_ref.shape[0]
    rows = (D + FF) // members
    for g in range(members):
        low, high = rows * g, rows * (g + 1)
        if low < D:
            cut = min(high, D)
            pack_ref[g, 0 : cut - low, :] = awo_ref[low:cut, :].astype(BF)
        if high > D:
            cut = max(low, D)
            pack_ref[g, cut - low : rows, :] = awg_ref[cut - D : high - D, :].astype(BF)
    return pack_blocks(pack_ref, rows, awf_ref)


def pack_rest(pack_ref, used, extra):
    if extra is not None:
        for g in range(pack_ref.shape[0]):
            pack_ref[g, used : used + PATCH_IN, :] = extra.astype(BF)
        used += PATCH_IN
    if used < pack_ref.shape[1]:
        pack_ref[:, used:, :] = jnp.zeros_like(pack_ref[:, used:, :])


def split_pack(pack_ref, table_ref, offset, outs):
    for j, out_ref in enumerate(outs):
        rows = out_ref.shape[1]
        at = pl.multiple_of(table_ref[offset + j] * rows, rows)
        out_ref[...] = pack_ref[:, pl.ds(at, rows), :]


def att_fwd_kernel(B, offset, held, noisy_ref, wp_t_ref, pos_ref, mods_ref, wqkv_t_ref, *refs):
    qkv_ref, lse_ref, att_out_ref, normed_ref, att_ref = refs[held:]
    step = pl.program_id(0)
    for b in range(B):
        image = (offset + step) * B + b
        hidden = mm(wp_t_ref[...], noisy_ref[b]) + pos_ref[...]
        normed, _ = norm_parts(hidden)
        modulate_into(normed_ref, b, normed, 1.0 + column(mods_ref, 1, image), column(mods_ref, 0, image))
    project_qkv(wqkv_t_ref, normed_ref, qkv_ref, B)
    attention_forward(qkv_ref, B, lse_ref, att_ref)
    for b in range(B):
        att_out_ref[b] = att_ref[:, lanes_of(b)]


def ffn_fwd_kernel(B, noisy_ref, wp_t_ref, pos_ref, att_ref, mods_a_ref, mods_b_ref, wo_t_ref, wf_t_ref,
                   wg_t_ref, mid_ref, bra_ref, brb_ref, hid_ref, normed_ref):
    step = pl.program_id(0)
    for b in range(B):
        image = step * B + b
        hidden = mm(wp_t_ref[...], noisy_ref[b]) + pos_ref[...]
        branch_a = mm(wo_t_ref[...], att_ref[b])
        bra_ref[b] = branch_a
        mid = hidden + column(mods_a_ref, 2, image) * branch_a
        mid_ref[b] = mid
        normed, _ = norm_parts(mid)
        modulate_into(normed_ref, b, normed, 1.0 + column(mods_b_ref, 1, image), column(mods_b_ref, 0, image))
    branch = None
    for rows in ffn_chunks():
        act = gelu_one(mm(wf_t_ref[rows, :], normed_ref[...])).astype(BF)
        branch = add_up(branch, mm(wg_t_ref[:, rows], act))
    for b in range(B):
        own = branch[:, lanes_of(b)]
        brb_ref[b] = own
        hid_ref[b] = mid_ref[b] + column(mods_b_ref, 2, step * B + b) * own


def block_kernel(B, entries, table_ref, hid_ref, noise_ref, mods_ref, modf_ref, wqkv_t_ref, wo_t_ref, wf_t_ref,
                 wg_t_ref, wo_ref, wf_ref, wg_ref, wy_t_ref, wy_ref, cond_ref,
                 qkv_ref, lse_ref, go_ref, gmid_ref, gm_ref, gmf_ref, loss_ref,
                 keep_ref, send_ref,
                 pack_ref, normed_ref, att_ref, slope_ref, act_ref, gpre_ref, gba_ref, gbb_ref, normf_ref, gout_ref,
                 awo_ref, awf_ref, awg_ref, awy_ref, bra_ref, ghid_ref):
    step = pl.program_id(0)
    first = step == 0

    @pl.when(first)
    def _():
        clear(gm_ref, gmf_ref, loss_ref, awo_ref, awf_ref, awg_ref, awy_ref)

    image = lambda b: step * B + b
    for b in range(B):
        normed, _ = norm_parts(hid_ref[b])
        modulate_into(normed_ref, b, normed, 1.0 + column(mods_ref, 1, image(b)), column(mods_ref, 0, image(b)))
    project_qkv(wqkv_t_ref, normed_ref, qkv_ref, B)
    attention_forward(qkv_ref, B, lse_ref, att_ref)
    branch_a = mm(wo_t_ref[...], att_ref[...])
    for b in range(B):
        own = branch_a[:, lanes_of(b)]
        bra_ref[b] = own
        mid = hid_ref[b] + column(mods_ref, 2, image(b)) * own
        gmid_ref[b] = mid
        normed, _ = norm_parts(mid)
        modulate_into(normed_ref, b, normed, 1.0 + column(mods_ref, 4, image(b)), column(mods_ref, 3, image(b)))
    branch_b = None
    for rows in ffn_chunks():
        act, slope = gelu_both(mm(wf_t_ref[rows, :], normed_ref[...]))
        slope_ref[rows, :] = slope
        act_ref[rows, :] = act.astype(BF)
        branch_b = add_up(branch_b, mm(wg_t_ref[:, rows], act_ref[rows, :]))
    for b in range(B):
        lanes = lanes_of(b)
        own = branch_b[:, lanes]
        gate_b = column(mods_ref, 5, image(b))
        normed_f, inv_f = norm_parts(gmid_ref[b] + gate_b * own)
        scale_f = 1.0 + column(modf_ref, 1, image(b))
        modulate_into(normf_ref, b, normed_f, scale_f, column(modf_ref, 0, image(b)))
        residue = mm(wy_t_ref[...], normf_ref[:, lanes]) - noise_ref[b].astype(F32)
        loss_ref[...] += residue * residue
        gout_ref[:, lanes] = ((2.0 / entries) * residue).astype(BF)
        gnf = mm(wy_ref[...], gout_ref[:, lanes])
        put_column(gmf_ref, 0, image(b), gnf)
        put_column(gmf_ref, 1, image(b), gnf * normed_f)
        ghid = norm_back(gnf, normed_f, inv_f, scale_f)
        ghid_ref[b] = ghid
        put_column(gm_ref, 3, image(b), ghid * own)
        gbb_ref[:, lanes] = (gate_b * ghid).astype(BF)
    gnb = None
    for rows in ffn_chunks():
        gact = mm(wg_ref[rows, :], gbb_ref[...])
        gpre_ref[rows, :] = (gact * slope_ref[rows, :]).astype(BF)
        gnb = add_up(gnb, mm(wf_ref[:, rows], gpre_ref[rows, :]))
        awf_ref[:, rows] += mm_nt(normed_ref[...], gpre_ref[rows, :])
        awg_ref[rows, :] += mm_nt(act_ref[rows, :], gbb_ref[...])
    for b in range(B):
        own = gnb[:, lanes_of(b)]
        normed, inv = norm_parts(gmid_ref[b])
        put_column(gm_ref, 1, image(b), own)
        put_column(gm_ref, 2, image(b), own * normed)
        gmid = ghid_ref[b] + norm_back(own, normed, inv, 1.0 + column(mods_ref, 4, image(b)))
        gmid_ref[b] = gmid
        put_column(gm_ref, 0, image(b), gmid * bra_ref[b])
        gba_ref[:, lanes_of(b)] = (column(mods_ref, 2, image(b)) * gmid).astype(BF)
    go = mm(wo_ref[...], gba_ref[...]).astype(BF)
    for b in range(B):
        go_ref[b] = go[:, lanes_of(b)]
    awo_ref[...] += mm_nt(att_ref[...], gba_ref[...])
    awy_ref[...] += mm_nt(gout_ref[...], normf_ref[...])

    @pl.when(step == pl.num_programs(0) - 1)
    def _():
        used = pack_outer(pack_ref, awo_ref, awf_ref, awg_ref)
        used = pack_blocks(pack_ref, used, mm_nt(cond_ref[...], gm_ref[...].astype(BF)))
        pack_rest(pack_ref, used, awy_ref[...])
        split_pack(pack_ref, table_ref, 0, (keep_ref, send_ref))


def ffn_bwd_kernel(B, table_ref, ghid_ref, mid_ref, att_ref, bra_ref, brb_ref, mods_a_ref, mods_b_ref, wf_t_ref, wo_ref, wf_ref,
                   wg_ref, cond_ref, go_ref, gmid_ref, gm_ref, keep_ref, send_ref, pack_ref,
                   normed_ref, act_ref, gpre_ref, gba_ref, gbb_ref, atts_ref, awo_ref, awf_ref, awg_ref):
    step = pl.program_id(0)
    first = step == 0

    @pl.when(first)
    def _():
        clear(gm_ref, awo_ref, awf_ref, awg_ref)

    image = lambda b: step * B + b
    for b in range(B):
        lanes = lanes_of(b)
        ghid = ghid_ref[b]
        put_column(gm_ref, 3, image(b), ghid * brb_ref[b])
        gbb_ref[:, lanes] = (column(mods_b_ref, 2, image(b)) * ghid).astype(BF)
        normed, _ = norm_parts(mid_ref[b])
        modulate_into(normed_ref, b, normed, 1.0 + column(mods_b_ref, 1, image(b)), column(mods_b_ref, 0, image(b)))
        atts_ref[:, lanes] = att_ref[b]
    gnb = None
    for rows in ffn_chunks():
        act, slope = gelu_both(mm(wf_t_ref[rows, :], normed_ref[...]))
        act_ref[rows, :] = act.astype(BF)
        gact = mm(wg_ref[rows, :], gbb_ref[...])
        gpre_ref[rows, :] = (gact * slope).astype(BF)
        gnb = add_up(gnb, mm(wf_ref[:, rows], gpre_ref[rows, :]))
        awf_ref[:, rows] += mm_nt(normed_ref[...], gpre_ref[rows, :])
        awg_ref[rows, :] += mm_nt(act_ref[rows, :], gbb_ref[...])
    for b in range(B):
        own = gnb[:, lanes_of(b)]
        normed, inv = norm_parts(mid_ref[b])
        put_column(gm_ref, 1, image(b), own)
        put_column(gm_ref, 2, image(b), own * normed)
        gmid = ghid_ref[b] + norm_back(own, normed, inv, 1.0 + column(mods_b_ref, 1, image(b)))
        gmid_ref[b] = gmid
        put_column(gm_ref, 0, image(b), gmid * bra_ref[b])
        gba_ref[:, lanes_of(b)] = (column(mods_a_ref, 2, image(b)) * gmid).astype(BF)
    go = mm(wo_ref[...], gba_ref[...]).astype(BF)
    for b in range(B):
        go_ref[b] = go[:, lanes_of(b)]
    awo_ref[...] += mm_nt(atts_ref[...], gba_ref[...])

    @pl.when(step == pl.num_programs(0) - 1)
    def _():
        used = pack_outer(pack_ref, awo_ref, awf_ref, awg_ref)
        used = pack_blocks(pack_ref, used, mm_nt(cond_ref[...], gm_ref[...].astype(BF)))
        pack_rest(pack_ref, used, None)
        split_pack(pack_ref, table_ref, 0, (keep_ref, send_ref))


def att_bwd_kernel(B, offset, bottom, opens, closes, *refs):
    refs = list(refs)
    take = lambda count: [refs.pop(0) for _ in range(count)]
    (table_ref,) = take(1)
    noisy_ref, wp_t_ref, pos_ref = take(3) if bottom else (None, None, None)
    (hid_ref,) = (None,) if bottom else take(1)
    qkv_ref, lse_ref, go_ref, gmid_ref, mods_ref, wqkv_ref, cond_ref = take(7)
    (gmf_ref,) = (None,) if bottom else take(1)
    before = take(3 if bottom else 2) if not opens else []
    (ghid_ref,) = (None,) if bottom else take(1)
    (gm_ref,) = take(1)
    sums = 2 if bottom else 1
    keep_ref, send_ref, pack_ref, accs = None, None, None, None
    if closes:
        keep_ref, send_ref = take(2)
    else:
        accs = take(sums)
    if closes:
        (pack_ref,) = take(1)
    normed_ref, gqkv_ref = take(2)
    tok_ref, noi_ref = take(2) if bottom else (None, None)
    if closes:
        accs = take(sums)
    step = pl.program_id(0)
    first = step == 0

    @pl.when(first)
    def _():
        if opens:
            gm_ref[...] = jnp.zeros_like(gm_ref)
            for acc_ref in accs:
                acc_ref[...] = jnp.zeros_like(acc_ref)
        else:
            for to_ref, from_ref in zip([gm_ref] + accs, before):
                to_ref[...] = from_ref[...]

    image = lambda b: (offset + step) * B + b
    source = lambda b: mm(wp_t_ref[...], noisy_ref[b]) + pos_ref[...] if bottom else hid_ref[b]
    for b in range(B):
        normed, _ = norm_parts(source(b))
        modulate_into(normed_ref, b, normed, 1.0 + column(mods_ref, 1, image(b)), column(mods_ref, 0, image(b)))
    attention_backward(qkv_ref, B, lse_ref, go_ref, gqkv_ref)
    gna = mm(wqkv_ref[...], gqkv_ref[...])
    for b in range(B):
        own = gna[:, lanes_of(b)]
        normed, inv = norm_parts(source(b))
        put_column(gm_ref, 0, image(b), own)
        put_column(gm_ref, 1, image(b), own * normed)
        ghid = gmid_ref[b] + norm_back(own, normed, inv, 1.0 + column(mods_ref, 1, image(b)))
        if bottom:
            tok_ref[:, lanes_of(b)] = ghid.astype(BF)
            noi_ref[:, lanes_of(b)] = noisy_ref[b]
        else:
            ghid_ref[b] = ghid
    accs[0][...] += mm_nt(normed_ref[...], gqkv_ref[...])
    if bottom:
        accs[1][...] += mm_nt(noi_ref[...], tok_ref[...])

    if closes:
        @pl.when(step == pl.num_programs(0) - 1)
        def _():
            used = pack_blocks(pack_ref, 0, accs[0])
            used = pack_blocks(pack_ref, used, mm_nt(cond_ref[...], gm_ref[...].astype(BF)))
            if not bottom:
                used = pack_blocks(pack_ref, used, mm_nt(cond_ref[...], gmf_ref[...].astype(BF)))
            pack_rest(pack_ref, used, accs[1][...] if bottom else None)
            split_pack(pack_ref, table_ref, 0, (keep_ref, send_ref))


def whole(*shape):
    return pl.BlockSpec(shape, lambda i: (0,) * len(shape))


def images(B, *shape, offset=0):
    return pl.BlockSpec((B,) + shape, lambda i: (i + offset,) + (0,) * len(shape))


def sds(shape, dtype):
    return jax.ShapeDtypeStruct(shape, dtype)


def run_kernel(kernel, steps, in_specs, outs, scratch, flops, args, aliases=None):
    out_specs = [spec for spec, _, _ in outs]
    out_shape = [sds(shape, dtype) for _, shape, dtype in outs]
    moved = sum(a.size * a.dtype.itemsize for a in args) + sum(
        math.prod(o.shape) * o.dtype.itemsize for o in out_shape
    )
    return pl.pallas_call(
        kernel,
        grid=(steps,),
        in_specs=in_specs,
        out_specs=out_specs,
        out_shape=out_shape,
        scratch_shapes=[pltpu.VMEM(shape, dtype) for shape, dtype in scratch],
        input_output_aliases=aliases or {},
        compiler_params=pltpu.CompilerParams(vmem_limit_bytes=VMEM_LIMIT),
        cost_estimate=pl.CostEstimate(flops=8 * flops, bytes_accessed=moved, transcendentals=0),
    )(*args)


MODS = whole(6 * D, 128)
HALF_MODS = whole(3 * D, 128)
COND = whole(D, 128)
SCALARS = pl.BlockSpec(memory_space=pltpu.SMEM)


def halves(pack):
    ng, rows, _ = pack
    half = (ng, rows // 2, D)
    return [(whole(*half), half, BF)] * 2


def att_forward(noisy, wp_t, pos, mods, wqkv_t, B, part, parts, before):
    n = noisy.shape[0]
    T = B * TOK
    steps = n // B // parts
    here = functools.partial(images, B, offset=part * steps)
    return run_kernel(
        functools.partial(att_fwd_kernel, B, part * steps, len(before)), steps,
        [here(PATCH_IN, TOK), whole(D, PATCH_IN), whole(D, TOK), HALF_MODS, whole(3 * D, D)]
        + [pl.BlockSpec(memory_space=pl.ANY)] * len(before),
        [(here(3 * D, TOK), (n, 3 * D, TOK), BF), (here(8, TOK), (n, 8, TOK), F32),
         (here(D, TOK), (n, D, TOK), BF)],
        [((D, T), BF), ((D, T), BF)],
        2 * n * TOK * (3 * D * D + 2 * D * TOK) // parts, (noisy, wp_t, pos, mods, wqkv_t) + tuple(before),
        aliases={5 + i: i for i in range(len(before))})


def ffn_forward(noisy, wp_t, pos, att, mods_a, mods_b, wo_t, wf_t, wg_t, B):
    n = noisy.shape[0]
    T = B * TOK
    full = images(B, D, TOK)
    return run_kernel(
        functools.partial(ffn_fwd_kernel, B), n // B,
        [images(B, PATCH_IN, TOK), whole(D, PATCH_IN), whole(D, TOK), full, HALF_MODS, HALF_MODS, whole(D, D),
         whole(FF, D), whole(D, FF)],
        [(full, (n, D, TOK), F32)] * 4,
        [((D, T), BF)],
        2 * n * TOK * (2 * D * FF + D * D), (noisy, wp_t, pos, att, mods_a, mods_b, wo_t, wf_t, wg_t))


def block_step(table, hid, noise, mods, modf, wqkv_t, wo_t, wf_t, wg_t, wo, wf, wg, wy_t, wy, cond, entries, B, pack):
    n = hid.shape[0]
    T = B * TOK
    full = images(B, D, TOK)
    return run_kernel(
        functools.partial(block_kernel, B, entries), n // B,
        [SCALARS, full, images(B, PATCH_IN, TOK), MODS, whole(2 * D, 128), whole(3 * D, D), whole(D, D),
         whole(FF, D), whole(D, FF), whole(D, D), whole(D, FF), whole(FF, D), whole(PATCH_IN, D),
         whole(D, PATCH_IN), COND],
        [(images(B, 3 * D, TOK), (n, 3 * D, TOK), BF), (images(B, 8, TOK), (n, 8, TOK), F32),
         (full, (n, D, TOK), BF), (full, (n, D, TOK), F32),
         (whole(4 * D, 128), (4 * D, 128), F32), (whole(2 * D, 128), (2 * D, 128), F32),
         (whole(PATCH_IN, TOK), (PATCH_IN, TOK), F32)] + halves(pack),
        [(pack, BF), ((D, T), BF), ((D, T), BF), ((FF, T), F32), ((FF, T), BF), ((FF, T), BF), ((D, T), BF),
         ((D, T), BF), ((D, T), BF), ((PATCH_IN, T), BF), ((D, D), F32), ((D, FF), F32), ((FF, D), F32),
         ((PATCH_IN, D), F32), ((B, D, TOK), F32), ((B, D, TOK), F32)],
        2 * n * TOK * (4 * D * D + 2 * D * TOK + 6 * D * FF + 2 * D * D),
        (table, hid, noise, mods, modf, wqkv_t, wo_t, wf_t, wg_t, wo, wf, wg, wy_t, wy, cond))


def ffn_backward(table, ghid, mid, att, bra, brb, mods_a, mods_b, wf_t, wo, wf, wg, cond, B, pack):
    n = mid.shape[0]
    T = B * TOK
    full = images(B, D, TOK)
    return run_kernel(
        functools.partial(ffn_bwd_kernel, B), n // B,
        [SCALARS, full, full, full, full, full, HALF_MODS, HALF_MODS, whole(FF, D), whole(D, D), whole(D, FF),
         whole(FF, D), COND],
        [(full, (n, D, TOK), BF), (full, (n, D, TOK), F32), (whole(4 * D, 128), (4 * D, 128), F32)] + halves(pack),
        [(pack, BF), ((D, T), BF), ((FF, T), BF), ((FF, T), BF), ((D, T), BF), ((D, T), BF), ((D, T), BF),
         ((D, D), F32), ((D, FF), F32), ((FF, D), F32)],
        2 * n * TOK * (5 * D * FF + 2 * D * D),
        (table, ghid, mid, att, bra, brb, mods_a, mods_b, wf_t, wo, wf, wg, cond))


def att_backward(table, source, qkv, lse, go, gmid, mods, wqkv, cond, gmf, B, bottom, pack, part=0, parts=1, before=()):
    n = qkv.shape[0]
    T = B * TOK
    steps = n // B // parts
    offset = part * steps
    opens, closes = part == 0, part == parts - 1
    here = functools.partial(images, B, offset=offset)
    full = here(D, TOK)
    gm = (whole(2 * D, 128), (2 * D, 128), F32)
    sums = [(whole(D, 3 * D), (D, 3 * D), F32)] + ([(whole(PATCH_IN, D), (PATCH_IN, D), F32)] if bottom else [])
    ins = [SCALARS] + ([here(PATCH_IN, TOK), whole(D, PATCH_IN), whole(D, TOK)] if bottom else [full])
    ins += [here(3 * D, TOK), here(8, TOK), full, full, HALF_MODS if bottom else MODS, whole(D, 3 * D), COND]
    ins += [] if bottom else [whole(2 * D, 128)]
    args = (table,) + tuple(source) + (qkv, lse, go, gmid, mods, wqkv, cond) + (() if bottom else (gmf,))
    if not opens:
        ins += [gm[0]] + [s[0] for s in sums]
        args += tuple(before)
    outs = ([] if bottom else [(full, (n, D, TOK), F32)]) + [gm] + (halves(pack) if closes else sums)
    scratch = ([(pack, BF)] if closes else []) + [((D, T), BF), ((3 * D, T), BF)]
    scratch += [((D, T), BF), ((PATCH_IN, T), BF)] if bottom else []
    scratch += [(s[1], F32) for s in sums] if closes else []
    return run_kernel(
        functools.partial(att_bwd_kernel, B, offset, bottom, opens, closes), steps, ins, outs, scratch,
        2 * n * TOK * (6 * D * D + 5 * D * TOK) // parts, args)


FREQ = 256
CLASSES = 1000
GRID = 16
LAYERS = 2
MOMENTUM = 0.9
LEARN = 30.0
DECAY = 0.7
IMAGES_PER_STEP = 2
SMALL_COST = 8 * 10**9


def plan(steps_in):
    anchor = math.cos(0.5 * math.pi * 0.008 / 1.008)
    fraction = (steps_in.astype(F32) / 1000.0 + 0.008) / 1.008
    levels = jnp.cos(0.5 * math.pi * fraction)
    return levels * levels / (anchor * anchor)


def time_features(steps_in):
    half_width = FREQ // 2
    frequencies = jnp.exp(-math.log(10000.0) * jnp.arange(half_width, dtype=F32) / half_width)
    angles = steps_in.astype(F32)[:, None] * frequencies[None, :]
    return jnp.concatenate([jnp.cos(angles), jnp.sin(angles)], axis=1)


def positions():
    quarter = D // 4
    omegas = jnp.exp(-math.log(10000.0) * jnp.arange(quarter, dtype=F32) / quarter)
    places = jnp.arange(GRID * GRID, dtype=jnp.int32)
    column = omegas[:, None] * (places % GRID).astype(F32)[None, :]
    row_pos = omegas[:, None] * (places // GRID).astype(F32)[None, :]
    return jnp.concatenate(
        [jnp.sin(column), jnp.cos(column), jnp.sin(row_pos), jnp.cos(row_pos)], axis=0
    )


def swish_parts(values):
    s = 1.0 / (1.0 + jnp.exp(-values))
    return values * s, s * (1.0 + values * (1.0 - s))


def advance(weight, moment, average, gradient):
    new_moment = MOMENTUM * moment + gradient
    new_weight = weight - LEARN * (gradient + MOMENTUM * new_moment)
    new_average = DECAY * average + (1.0 - DECAY) * new_weight
    return (new_weight, new_moment, new_average)


def after(x, *others):
    return lax.optimization_barrier((x,) + others)[0]


def swap(x, axis, mask):
    pairs = [(i, i ^ mask) for i in range(lax.axis_size(axis))]
    return lax.ppermute(x, axis, pairs)


def digit_list(n):
    found, shift = [], 0
    while (1 << shift) < n:
        left = n >> shift
        size = 2 if shift == 0 or left == 2 else 4
        found.append((shift, size))
        shift += size.bit_length() - 1
    return found


def place_of(index, n):
    place = 0
    for shift, size in digit_list(n):
        place = place * size + ((index >> shift) & (size - 1))
    return place


def place_table(emb_rows):
    nr, ng = lax.axis_size("rep"), lax.axis_size("grp")
    me, member = lax.axis_index("rep"), lax.axis_index("grp")
    entries, offsets = [], {}
    for shift, size in digit_list(nr):
        offsets[shift] = len(entries)
        entries += [((me >> shift) & (size - 1)) ^ j for j in range(size)]
    if not entries:
        entries = [0, 1]
    offsets["place"] = len(entries)
    entries += [place_of(me ^ mask, nr) for mask in range(nr)]
    offsets["member"] = len(entries)
    entries += [member ^ k for k in range(ng)]
    offsets["lead"] = len(entries)
    entries.append(emb_rows * member % 16)
    return jnp.stack([jnp.asarray(e, jnp.int32) for e in entries]), offsets


def in_vmem():
    return pl.BlockSpec(memory_space=pltpu.VMEM)


def small_kernel(kernel, outs, scratch, args, scalars=1):
    return pl.pallas_call(
        kernel,
        in_specs=[SCALARS] * scalars + [in_vmem()] * (len(args) - scalars),
        out_specs=[in_vmem()] * len(outs),
        out_shape=[sds(shape, dtype) for shape, dtype in outs],
        scratch_shapes=[pltpu.VMEM(shape, dtype) for shape, dtype in scratch],
        compiler_params=pltpu.CompilerParams(vmem_limit_bytes=VMEM_LIMIT),
        cost_estimate=pl.CostEstimate(flops=SMALL_COST, bytes_accessed=0, transcendentals=0),
    )(*args)


def spread_outer(piece, n):
    pieces = [((0,), piece)]
    digits = digit_list(n)[1:]
    for shift, size in digits:
        if len(pieces) > 1:
            pieces = [(sum((m for m, _ in pieces), ()), jnp.concatenate([v for _, v in pieces], axis=0))]
        masks, value = pieces[0]
        pieces = pieces + [
            (tuple(m ^ (j << shift) for m in masks), swap(value, "rep", j << shift)) for j in range(1, size)
        ]
    return pieces


def spread_core(pieces, n, marks=()):
    if n == 1:
        return pieces
    return pieces + [
        (tuple(m ^ 1 for m in masks), swap(after(value, *marks) if marks else value, "rep", 1))
        for masks, value in pieces
    ]


def gather_members(mine):
    got = [swap(mine, "grp", k) for k in range(1, lax.axis_size("grp"))]
    return jnp.concatenate(got, axis=0) if got else None


def sum_parts(parts):
    total = parts[0][...].astype(F32)
    for part in parts[1:]:
        total = total + part[...].astype(F32)
    return total.astype(BF)


def rows_kernel(count, offset, table_ref, *refs):
    parts, outs, total_ref = refs[:count], refs[count:-1], refs[-1]
    total_ref[...] = sum_parts(parts)
    split_pack(total_ref, table_ref, offset, outs)


def members_kernel(counts, offset, has_extra, table_ref, *refs):
    refs = list(refs)
    groups = [[refs.pop(0) for _ in range(c)] for c in counts]
    extra_ref = refs.pop(0) if has_extra else None
    outs, totals = refs[: -len(counts)], refs[-len(counts) :]
    for parts, total_ref in zip(groups, totals):
        total_ref[...] = sum_parts(parts)
    for k, out_ref in enumerate(outs):
        at = 0
        for total_ref in totals:
            rows = total_ref.shape[1]
            out_ref[at : at + rows, :] = total_ref[table_ref[offset + k]]
            at += rows
        if has_extra:
            out_ref[at:, :] = extra_ref[...]


def last_kernel(count, extra, table_ref, *refs):
    parts, out_ref = refs[:count], refs[-1]
    rows = parts[0].shape[0] - extra
    total = parts[0][0:rows, :].astype(F32)
    for part in parts[1:]:
        total = total + part[0:rows, :].astype(F32)
    out_ref[0:rows, :] = total.astype(BF)
    if extra:
        for i, part in enumerate(parts):
            out_ref[rows + extra * i : rows + extra * (i + 1), :] = part[rows:, :]


def reduce_first(keep, send):
    return [keep, swap(send, "rep", 1)] if lax.axis_size("rep") > 1 else [keep]


def reduce_outer(parts, table, offsets, number):
    shift, size = digit_list(lax.axis_size("rep"))[number]
    ng, rows, _ = parts[0].shape
    one = lambda r: pl.BlockSpec((1, r, D), lambda i: (i, 0, 0))
    cut = pl.pallas_call(
        functools.partial(rows_kernel, len(parts), offsets[shift]),
        grid=(ng,),
        in_specs=[SCALARS] + [one(rows)] * len(parts),
        out_specs=[one(rows // size)] * size,
        out_shape=[sds((ng, rows // size, D), BF)] * size,
        scratch_shapes=[pltpu.VMEM((1, rows, D), BF)],
    )(table, *parts)
    return [cut[0]], cut[1:], shift


def exchange(own, sends, axis, shift):
    return own + [swap(x, axis, (j + 1) << shift) for j, x in enumerate(sends)]


def reduce_members(groups, extra, table, offsets):
    ng = groups[0][0].shape[0]
    rows = sum(g[0].shape[1] for g in groups) + (0 if extra is None else extra.shape[0])
    cut = small_kernel(
        functools.partial(members_kernel, tuple(len(g) for g in groups), offsets["member"], extra is not None),
        [((rows, D), BF)] * ng, [(g[0].shape, BF) for g in groups],
        (table, *sum(groups, []), *([] if extra is None else [extra])),
    )
    return [cut[0]], cut[1:], 0


def reduce_last(parts, extra, table):
    rows = parts[0].shape[0] + extra * (len(parts) - 1)
    return small_kernel(
        functools.partial(last_kernel, len(parts), extra), [((rows, D), BF)], [], (table, *parts)
    )[0]


def pack_first_kernel(lead_at, emb_real, shard_place, table_ref, emb_ref, wa_ref, wqkv_ref, shard_ref, mine_ref, wide_ref):
    wide_ref[...] = jnp.zeros_like(wide_ref)
    wide_ref[0:emb_real, :] = emb_ref[...]
    seg = wide_ref.shape[0]
    shard_ref[0:seg, :] = pltpu.roll(wide_ref[...], table_ref[lead_at], 0).astype(BF)
    at = seg
    for ref in (wa_ref, wqkv_ref):
        for c in range(3):
            rows = ref.shape[1]
            shard_ref[at : at + rows, :] = ref[0, :, D * c : D * (c + 1)].astype(BF)
            at += rows
    if at < shard_ref.shape[0]:
        shard_ref[at:, :] = jnp.zeros_like(shard_ref[at:, :])
    rows = mine_ref.shape[0]
    mine_ref[...] = shard_ref[pl.ds(pl.multiple_of(table_ref[shard_place] * rows, rows), rows), :]


def pack_first(table, offsets, emb_table, w_in, seg, unit):
    nr = lax.axis_size("rep")
    rows = w_in.shape[1]
    total = -(-(seg + 6 * rows) // unit) * unit
    part = lambda c: pl.BlockSpec((1, rows, 3 * D), lambda i: (0, 0, c))
    return pl.pallas_call(
        functools.partial(pack_first_kernel, offsets["lead"], emb_table.shape[0], offsets["place"]),
        grid=(1,),
        in_specs=[SCALARS, whole(*emb_table.shape), part(0), part(2)],
        out_specs=[whole(total, D), whole(total // nr, D)],
        out_shape=[sds((total, D), BF), sds((total // nr, D), BF)],
        scratch_shapes=[pltpu.VMEM((seg, D), F32)],
        compiler_params=pltpu.CompilerParams(vmem_limit_bytes=VMEM_LIMIT),
    )(table, emb_table, w_in, w_in)


def pack_other_kernel(layouts, shard_place, table_ref, *refs):
    refs = list(refs)
    inputs = [[refs.pop(0) for _ in layout] for layout in layouts]
    shard_refs, mine_ref = refs[:-1], refs[-1]
    put = 0
    for layout, ins, shard_ref in zip(layouts, inputs, shard_refs):
        at = 0
        for ref, count in zip(ins, layout):
            rows = ref.shape[-2]
            for c in range(count):
                cols = slice(D * c, D * (c + 1))
                value = ref[0, :, cols] if len(ref.shape) == 3 else ref[:, cols]
                shard_ref[at : at + rows, :] = value.astype(BF)
                at += rows
            if len(ref.shape) == 2:
                value = ref[:, D * count :]
                shard_ref[at : at + rows, :] = jnp.concatenate(
                    [value, jnp.zeros((rows, D - value.shape[1]), F32)], axis=1
                ).astype(BF)
                at += rows
        if at < shard_ref.shape[0]:
            shard_ref[at:, :] = jnp.zeros_like(shard_ref[at:, :])
        rows = shard_ref.shape[0] * mine_ref.shape[0] // sum(r.shape[0] for r in shard_refs)
        from_rows = pl.ds(pl.multiple_of(table_ref[shard_place] * rows, rows), rows)
        mine_ref[put : put + rows, :] = shard_ref[from_rows, :]
        put += rows


def pack_other(table, offsets, shards):
    nr = lax.axis_size("rep")
    spec = lambda shape, index: pl.BlockSpec(shape, lambda i: index)
    parts = sum((p for _, p in shards), [])
    shapes = [(rows, D) for rows, _ in shards] + [(sum(rows for rows, _ in shards) // nr, D)]
    return pl.pallas_call(
        functools.partial(
            pack_other_kernel, tuple(tuple(p[3] for p in ps) for _, ps in shards), offsets["place"]
        ),
        grid=(1,),
        in_specs=[SCALARS] + [spec(p[1], p[2]) for p in parts],
        out_specs=[whole(*shape) for shape in shapes],
        out_shape=[sds(shape, BF) for shape in shapes],
        compiler_params=pltpu.CompilerParams(vmem_limit_bytes=VMEM_LIMIT),
    )(table, *[p[0] for p in parts])


def fill_full(full_ref, masks, place, member, table_ref, shard_ref, pieces):
    ng = full_ref.shape[0]
    full_ref[table_ref[member]] = shard_ref[...]
    for group, ref in zip(masks, pieces):
        rows = ref.shape[0] // (len(group) * (ng - 1))
        for i, mask in enumerate(group):
            at = pl.ds(pl.multiple_of(table_ref[place + mask] * rows, rows), rows)
            for k in range(1, ng):
                start = (i * (ng - 1) + k - 1) * rows
                full_ref[table_ref[member + k], at, :] = ref[start : start + rows, :]


def take_blocks(full_ref, start, count, out_ref):
    ng = full_ref.shape[0]
    step = D // ng
    for g in range(ng):
        for c in range(count):
            out_ref[step * g : step * (g + 1), D * c : D * (c + 1)] = full_ref[
                g, start + step * c : start + step * (c + 1), :
            ]
    return start + step * count


def take_outer(full_ref, start, wo_ref, wg_ref):
    ng = full_ref.shape[0]
    wide = (D + FF) // ng
    for g in range(ng):
        low, high = wide * g, wide * (g + 1)
        if low < D:
            cut = min(high, D)
            wo_ref[low:cut, :] = full_ref[g, start : start + cut - low, :]
        if high > D:
            cut = max(low, D)
            wg_ref[cut - D : high - D, :] = full_ref[g, start + cut - low : start + wide, :]
    return start + wide


def first_kernel(emb_rows, seg, masks, place, member, table_ref, shard_ref, feats_ref, labels_ref, *refs):
    pieces, rest = refs[: len(masks)], refs[len(masks) :]
    (wp_t_ref, w2_ref, wa_ref, wqkv_ref, wqkv_t_ref, mods_ref, time_act_ref, pre_ref, cond_ref, act_t_ref,
     full_ref, emb_ref) = rest
    fill_full(full_ref, masks, place, member, table_ref, shard_ref, pieces)
    ng = full_ref.shape[0]
    emb_ref[...] = jnp.zeros_like(emb_ref)
    for g in range(ng):
        base = emb_rows * g // 16 * 16
        emb_ref[base : base + seg, :] = emb_ref[base : base + seg, :] + full_ref[g, 0:seg, :]
    at = take_blocks(full_ref, seg, 3, wa_ref)
    take_blocks(full_ref, at, 3, wqkv_ref)
    wqkv_t_ref[...] = wqkv_ref[...].T
    wp_t_ref[...] = emb_ref[0:128, :].T[:, 0:PATCH_IN]
    w1 = emb_ref[PATCH_IN : PATCH_IN + FREQ, :]
    w2_ref[...] = emb_ref[PATCH_IN + FREQ : PATCH_IN + FREQ + D, :]
    classes = emb_ref[PATCH_IN + FREQ + D : PATCH_IN + FREQ + D + CLASSES + 8, :]
    pre = mm(feats_ref[...], w1)
    pre_ref[...] = pre
    time_act = swish_parts(pre)[0].astype(BF)
    time_act_ref[...] = time_act
    hot = labels_ref[...] == lax.broadcasted_iota(jnp.int32, (labels_ref.shape[0], CLASSES + 8), 1)
    cond = mm(time_act, w2_ref[...]) + mm(jnp.where(hot, 1.0, 0.0).astype(BF), classes)
    cond_ref[...] = cond
    act = swish_parts(cond)[0]
    act_t_ref[...] = act.T.astype(BF)
    mods_ref[...] = mm(wa_ref[...].T, act_t_ref[...])


def second_kernel(masks, place, member, table_ref, shard_ref, act_t_ref, *refs):
    pieces, rest = refs[: len(masks)], refs[len(masks) :]
    wo_ref, wg_ref, wo_t_ref, wg_t_ref, wf_ref, wf_t_ref, wa_ref, mods_ref, full_ref = rest
    fill_full(full_ref, masks, place, member, table_ref, shard_ref, pieces)
    at = take_outer(full_ref, 0, wo_ref, wg_ref)
    at = take_blocks(full_ref, at, 4, wf_ref)
    take_blocks(full_ref, at, 3, wa_ref)
    wo_t_ref[...] = wo_ref[...].T
    wg_t_ref[...] = wg_ref[...].T
    wf_t_ref[...] = wf_ref[...].T
    mods_ref[...] = mm(wa_ref[...].T, act_t_ref[...])


def third_kernel(masks, place, member, table_ref, shard_ref, act_t_ref, *refs):
    pieces, rest = refs[: len(masks)], refs[len(masks) :]
    (wo_ref, wg_ref, wo_t_ref, wg_t_ref, wf_ref, wf_t_ref, wqkv_ref, wqkv_t_ref, wa_ref, wm_ref, wy_ref, wy_t_ref,
     mods_ref, modf_ref, full_ref, wide_ref) = rest
    fill_full(full_ref, masks, place, member, table_ref, shard_ref, pieces)
    at = take_outer(full_ref, 0, wo_ref, wg_ref)
    at = take_blocks(full_ref, at, 6, wa_ref)
    at = take_blocks(full_ref, at, 3, wqkv_ref)
    at = take_blocks(full_ref, at, 4, wf_ref)
    at = take_blocks(full_ref, at, 2, wm_ref)
    take_blocks(full_ref, at, 1, wide_ref)
    wo_t_ref[...] = wo_ref[...].T
    wg_t_ref[...] = wg_ref[...].T
    wf_t_ref[...] = wf_ref[...].T
    wqkv_t_ref[...] = wqkv_ref[...].T
    wy_ref[...] = wide_ref[:, 0:PATCH_IN]
    wy_t_ref[...] = wide_ref[...].T[0:PATCH_IN, :]
    mods_ref[...] = mm(wa_ref[...].T, act_t_ref[...])
    modf_ref[...] = mm(wm_ref[...].T, act_t_ref[...])


def assemble(kernel, table, offsets, shard, pieces, extra, outs, scratch):
    ng = lax.axis_size("grp")
    masks = tuple(m for m, v in pieces if v is not None)
    arrays = [v for _, v in pieces if v is not None]
    return small_kernel(
        functools.partial(kernel, masks, offsets["place"], offsets["member"]), outs,
        [((ng,) + shard.shape, BF)] + scratch, (table, shard, *extra, *arrays),
    )


def cond_back_kernel(n, table_ref, gma0_ref, gmb0_ref, gma1_ref, gmb1_ref, gmf_ref, wa0a_ref, wa0b_ref, wa1_ref, wm_ref,
                     w2_ref, cond_ref, pre_ref, time_act_ref, feats_ref, label_ref, squares_ref, rows_ref):
    low = lambda ref: ref[...].astype(BF)
    gact = mm(wm_ref[...], low(gmf_ref))
    gact += mm(wa1_ref[:, 0 : 2 * D], low(gma1_ref)) + mm(wa1_ref[:, 2 * D :], low(gmb1_ref))
    gact += mm(wa0a_ref[:, 0 : 2 * D], low(gma0_ref)) + mm(wa0a_ref[:, 2 * D :], gmb0_ref[0:D, :].astype(BF))
    gact += mm(wa0b_ref[...], gmb0_ref[D:, :].astype(BF))
    gcond = gact.T * swish_parts(cond_ref[...])[1]
    gpre = mm_nt(gcond.astype(BF), w2_ref[...]) * swish_parts(pre_ref[...])[1]
    total = jnp.sum(squares_ref[...]).reshape(1, 1)
    high = total.astype(BF).astype(F32)
    middle = (total - high).astype(BF).astype(F32)
    last = total - high - middle
    lane = lax.broadcasted_iota(jnp.int32, (n, 128), 1)
    row = lax.broadcasted_iota(jnp.int32, (n, 128), 0)
    loss = jnp.where(lane == 0, high, jnp.where(lane == 1, middle, jnp.where(lane == 2, last, 0.0)))
    loss = jnp.where(row == 0, loss, 0.0)
    loss = jnp.where(lane == 3, label_ref[:, 0:1], jnp.where(lane == 4, label_ref[:, 1:2], loss))
    top = jnp.concatenate([time_act_ref[...].astype(F32)[0:n], gpre[0:n]], axis=0)
    feats = jnp.concatenate([feats_ref[...].astype(F32)[0:n], loss], axis=1)
    rows_ref[0 : 2 * n, :] = top.astype(BF)
    rows_ref[2 * n : 4 * n, :] = jnp.concatenate([gcond[0:n], feats], axis=0).astype(BF)


def emb_kernel(n, inv_entries, counts, extra, member, emb_rows, table_ref, patch_ref, w_ref, m_ref, e_ref, *refs):
    pieces, refs = refs[: len(counts)], refs[len(counts) :]
    new_w_ref, new_m_ref, new_e_ref, loss_ref, left_ref, right_ref, grad_ref, own_ref = refs
    at = 0
    for ref, count in zip(pieces, counts):
        each = ref.shape[0] // count
        for i in range(count):
            for base in range(each * (i + 1) - extra, each * (i + 1), 4 * n):
                left_ref[at : at + 2 * n, :] = ref[base : base + 2 * n, :]
                right_ref[at : at + 2 * n, :] = ref[base + 2 * n : base + 4 * n, :]
                at += 2 * n
    total = left_ref.shape[0]
    row = lax.broadcasted_iota(jnp.int32, (total, D), 0)
    top = (row % (2 * n)) < n
    zero = jnp.zeros((total, D), BF)
    act = jnp.where(top, left_ref[...], zero)
    gcond = jnp.where(top, right_ref[...], zero)
    gpre = jnp.where(top, zero, left_ref[...])
    feats = right_ref[:, 0:FREQ]
    tags = right_ref[:, FREQ:].astype(F32).T
    label = (tags[3:4, :] * 32.0 + tags[4:5, :]).astype(jnp.int32)
    label = pltpu.roll(jnp.broadcast_to(label, (8, total)), total - n, 1)[0:1, :]
    hot = label == lax.broadcasted_iota(jnp.int32, (CLASSES + 8, total), 0)
    grad_ref[0:PATCH_IN, :] = patch_ref[0:PATCH_IN, :]
    grad_ref[PATCH_IN : PATCH_IN + FREQ, :] = mm(feats.T, gpre)
    grad_ref[PATCH_IN + FREQ : PATCH_IN + FREQ + D, :] = mm(act.T, gcond)
    grad_ref[PATCH_IN + FREQ + D : PATCH_IN + FREQ + D + CLASSES + 8, :] = mm(jnp.where(hot, 1.0, 0.0).astype(BF), gcond)
    rows = own_ref.shape[0]
    start = emb_rows * table_ref[member]
    low = start // 8 * 8
    block = grad_ref[pl.ds(pl.multiple_of(low, 8), rows), :]
    own_ref[...] = pltpu.roll(block, lax.rem(rows - (start - low), rows), 0)
    new = advance(w_ref[...], m_ref[...], e_ref[...], own_ref[0:emb_rows, :])
    new_w_ref[...], new_m_ref[...], new_e_ref[...] = new
    spot = lax.broadcasted_iota(jnp.int32, tags.shape, 1) % (2 * n) >= n
    spot &= lax.broadcasted_iota(jnp.int32, tags.shape, 0) < 3
    loss_ref[...] = jnp.sum(jnp.where(spot, tags, 0.0)).reshape(1, 1) * inv_entries


def update_kernel(masks, place, member, sizes, step_rows, layout, has_head, n_chain, table_ref, *refs):
    pieces, refs = refs[: len(masks)], refs[len(masks) :]
    count = 9 if has_head else 6
    states, refs = refs[:count], refs[count + n_chain :]
    news, refs = refs[:count], refs[count:]
    rest_ref, shard_refs = (None, refs) if has_head else (refs[0], refs[1:])
    step = pl.program_id(0)

    @pl.when(step == 0)
    def _():
        for group, ref in zip(masks, pieces):
            each = ref.shape[0] // len(group)
            for i, mask in enumerate(group):
                start = each * i
                for rows, shard_ref in zip(sizes, shard_refs):
                    at = pl.ds(pl.multiple_of(table_ref[place + mask] * rows, rows), rows)
                    shard_ref[at, :] = ref[start : start + rows, :]
                    start += rows
        if not has_head:
            shard_ref = shard_refs[1]
            rest_ref[...] = shard_ref[shard_ref.shape[0] - rest_ref.shape[0] :, :].astype(F32)
        else:
            rows = states[6].shape[0]
            state = [r[...] for r in states[6:]]
            start = layout[-1][1] + rows
            for c in range(2):
                cols = slice(D * c, D * (c + 1))
                grad = shard_refs[1][start + rows * c : start + rows * (c + 1), :].astype(F32)
                for ref, value in zip(news[6:], advance(*(x[:, cols] for x in state), grad)):
                    ref[:, cols] = value
            start = layout[7][1] + rows
            flat = shard_refs[0][start : start + PATCH_IN, :].astype(F32)
            turn = jnp.where(table_ref[member] == 0, 0, D - rows * table_ref[member])
            grad = pltpu.roll(flat, turn, 1)[:, 0:128].T[0:rows, :]
            for ref, value in zip(news[6:], advance(*(x[:, 2 * D :] for x in state), grad)):
                ref[:, 2 * D :] = value

    out_rows = states[0].shape[1]
    at = pl.multiple_of(step * out_rows, 16)
    grad = shard_refs[0][pl.ds(at, out_rows), :].astype(F32)
    for ref, value in zip(news[:3], advance(*(r[0] for r in states[:3]), grad)):
        ref[0] = value
    for group, row, block in layout:
        cols = slice(D * block, D * (block + 1))
        at = pl.multiple_of(row + step * step_rows, 16)
        grad = shard_refs[group][pl.ds(at, step_rows), :].astype(F32)
        for ref, value in zip(news[3:6], advance(*(r[0, :, cols] for r in states[3:6]), grad)):
            ref[0, :, cols] = value


def update(table, offsets, pieces, layer, packs, outer, inner, head, chain):
    nr = lax.axis_size("rep")
    rows, wide = inner[0].shape[1], inner[0].shape[2]
    rows_out = outer[0].shape[1]
    step_rows = 16
    steps = rows // step_rows
    masks = tuple(m for m, _ in pieces)
    arrays = [v for _, v in pieces]
    sizes = tuple(p[1] // nr for p in packs)
    layout = [(0, rows_out + rows * i, 9 + i) for i in range(4)]
    layout += [(0, rows_out + rows * (4 + i), 2 + i) for i in range(4)]
    layout += [(1, rows * i, 6 + i) for i in range(3)] + [(1, rows * (3 + i), i) for i in range(2)]
    rests = [] if head else [packs[1][1] - 5 * rows]
    in_spec = pl.BlockSpec((1, step_rows, wide), lambda i: (layer, i, 0))
    out_spec = pl.BlockSpec((1, rows_out // steps, D), lambda i: (layer, i, 0))
    states = list(outer) + list(inner) + list(head or ())
    specs = [out_spec] * 3 + [in_spec] * 3 + [whole(*h.shape) for h in head or ()]
    chain = list(chain) if chain else []
    first = 1 + len(arrays) + len(states)
    return pl.pallas_call(
        functools.partial(
            update_kernel, masks, offsets["place"], offsets["member"], sizes, step_rows, tuple(layout), bool(head),
            len(chain),
        ),
        grid=(steps,),
        in_specs=[SCALARS] + [whole(*a.shape) for a in arrays] + specs
        + [pl.BlockSpec(memory_space=pl.ANY)] * len(chain),
        out_specs=specs + [whole(r, D) for r in rests],
        out_shape=[sds(s.shape, F32) for s in states] + [sds((r, D), F32) for r in rests],
        scratch_shapes=[pltpu.VMEM((p[1], D), BF) for p in packs],
        input_output_aliases={first + i: i for i in range(len(chain))},
        compiler_params=pltpu.CompilerParams(vmem_limit_bytes=VMEM_LIMIT),
    )(table, *arrays, *states, *chain)


def local(
    latents, noise, timesteps, labels, emb_table, emb_mom, emb_ema, w_in, in_mom, in_ema,
    w_out, out_mom, out_ema, head, head_mom, head_ema,
):
    nr, ng = lax.axis_size("rep"), lax.axis_size("grp")
    member = lax.axis_index("grp")
    n = latents.shape[0]
    B = IMAGES_PER_STEP
    unit = 16 * nr
    digits = digit_list(nr)
    rows_d = D // ng
    rows_out = (D + FF) // ng
    emb_rows = emb_table.shape[0]
    seg = -(-(emb_rows + 15) // 16) * 16
    emb_full = emb_rows * (ng - 1) // 16 * 16 + seg
    full_rows = lambda rows: -(-rows // unit) * unit
    table, offsets = place_table(emb_rows)

    shard1, mine1 = pack_first(table, offsets, emb_table, w_in, seg, unit)
    got1 = gather_members(mine1)
    three, one = (1, rows_d, 3 * D), (1, rows_d, D)
    shard2, shard3, mine23 = pack_other(
        table, offsets,
        [
            (full_rows(rows_out + 7 * rows_d),
             [(w_out, (1, rows_out, D), (0, 0, 0), 1), (w_in, three, (0, 0, 3), 3), (w_in, one, (0, 0, 12), 1),
              (w_in, three, (0, 0, 1), 3)]),
            (full_rows(rows_out + 16 * rows_d),
             [(w_out, (1, rows_out, D), (1, 0, 0), 1), (w_in, (1, rows_d, 13 * D), (1, 0, 0), 13),
              (head, head.shape, (0, 0), 2)]),
        ],
    )
    around1 = spread_outer(after(got1, mine23), nr)
    cut2 = shard2.shape[0] // nr
    came1 = [v for m, v in around1 if m != (0,)]
    mine2 = after(mine23[:cut2], got1)
    parts2 = [swap(after(mine2, came1[0]) if k == 3 else mine2, "grp", k) for k in range(1, ng)]
    got2 = jnp.concatenate(parts2, axis=0)
    around2 = spread_outer(got2, nr)
    mine3 = mine23[cut2:]
    got3 = [swap(after(mine3, *parts2, *came1), "grp", k) for k in range(1, ng)]

    levels = plan(timesteps)
    noise_level = jnp.sqrt(jnp.maximum(1.0 - levels, 0.0))
    noisy = (
        jnp.sqrt(levels)[:, None, None] * latents.astype(F32)
        + noise_level[:, None, None] * noise.astype(F32)
    ).astype(BF)
    feats = jnp.pad(time_features(timesteps).astype(BF), ((0, 128 - n), (0, 0)))
    label_column = jnp.pad(labels, (0, 128 - n), constant_values=-1)[:, None]
    label_parts = jnp.pad(
        jnp.stack([labels >> 5, labels & 31], axis=1).astype(F32), ((0, 0), (0, 126))
    )
    pos = positions()

    pieces1 = spread_core(
        [(sum((m for m, _ in around1), ()), jnp.concatenate([v for _, v in around1], axis=0))], nr, parts2[:2]
    )
    wp_t, w2, wa0a, wqkv0, wqkv0_t, mods0a, time_act, pre_time, cond, act_t = assemble(
        functools.partial(first_kernel, emb_rows, seg), table, offsets, shard1, pieces1,
        (feats, label_column),
        [((D, PATCH_IN), BF), ((D, D), BF), ((D, 3 * D), BF), ((D, 3 * D), BF), ((3 * D, D), BF),
         ((3 * D, 128), F32), ((128, D), BF), ((128, D), F32), ((128, D), F32), ((D, 128), BF)],
        [((emb_full, D), BF)],
    )
    early = att_forward(noisy, wp_t, pos, after(mods0a, got2), wqkv0_t, B, 0, 2, ())
    got3 = [after(g, early[0]) for g in got3]
    got3 = jnp.concatenate(got3, axis=0)
    around3 = spread_outer(got3, nr)
    qkv0, lse0, att0 = att_forward(noisy, wp_t, pos, after(mods0a, got3), wqkv0_t, B, 1, 2, early)
    pieces2 = spread_core([(m, after(v, att0)) for m, v in around2], nr)
    wo0, wg0, wo0_t, wg0_t, wf0, wf0_t, wa0b, mods0b = assemble(
        second_kernel, table, offsets, shard2, pieces2, (act_t,),
        [((D, D), BF), ((FF, D), BF), ((D, D), BF), ((D, FF), BF), ((D, FF), BF), ((FF, D), BF),
         ((D, 3 * D), BF), ((3 * D, 128), F32)],
        [],
    )
    mid0, bra0, brb0, hid1 = ffn_forward(noisy, wp_t, pos, att0, mods0a, mods0b, wo0_t, wf0_t, wg0_t, B)
    pieces3 = spread_core([(m, after(v, hid1)) for m, v in around3], nr)
    (wo1, wg1, wo1_t, wg1_t, wf1, wf1_t, wqkv1, wqkv1_t, wa1, wm, wy, wy_t, mods1, modf) = assemble(
        third_kernel, table, offsets, shard3, pieces3, (act_t,),
        [((D, D), BF), ((FF, D), BF), ((D, D), BF), ((D, FF), BF), ((D, FF), BF), ((FF, D), BF),
         ((D, 3 * D), BF), ((3 * D, D), BF), ((D, 6 * D), BF), ((D, 2 * D), BF), ((D, PATCH_IN), BF),
         ((PATCH_IN, D), BF), ((6 * D, 128), F32), ((2 * D, 128), F32)],
        [((D, D), BF)],
    )
    entries = n * nr * ng * TOK * PATCH_IN
    outer_pack = (ng, full_rows(rows_out + 8 * rows_d + PATCH_IN), D)
    qkv_pack1 = (ng, full_rows(7 * rows_d), D)
    qkv_pack0 = (ng, full_rows(5 * rows_d + PATCH_IN), D)
    qkv1, lse1, go1, gmid1, gmb1, gmf, squares, keep_f1, send_f1 = block_step(
        table, hid1, noise, mods1, modf, wqkv1_t, wo1_t, wf1_t, wg1_t, wo1, wf1, wg1, wy_t, wy, act_t,
        float(entries), B, outer_pack,
    )
    parts_f1 = reduce_first(keep_f1, send_f1)
    ghid1, gma1, keep_a1, send_a1 = att_backward(
        table, (hid1,), qkv1, lse1, go1, gmid1, mods1, wqkv1, act_t, gmf, B, False, qkv_pack1
    )
    parts_a1 = reduce_first(keep_a1, send_a1)

    def outer_stage(parts):
        sends = []
        for number in range(1, len(digits)):
            own, sends, shift = reduce_outer(parts, table, offsets, number)
            parts = exchange(own, sends, "rep", shift)
        return parts, sends

    def member_stage(groups, extra):
        own, sends, shift = reduce_members(groups, extra, table, offsets)
        return exchange(own, sends, "grp", shift), sends

    def held(parts, *marks):
        return [parts[0]] + [after(p, *marks) for p in parts[1:]]

    parts_f1, sends_f1 = outer_stage(held(parts_f1, ghid1))
    go0, gmid0, gmb0, keep_f0, send_f0 = ffn_backward(
        table, after(ghid1, *sends_f1), mid0, att0, bra0, brb0, mods0a, mods0b, wf0_t, wo0, wf0, wg0, act_t,
        B, outer_pack,
    )
    parts_f0 = reduce_first(keep_f0, send_f0)
    parts_f1 = held(parts_f1, gmid0)
    parts_a1, sends_a1 = outer_stage(held(parts_a1, gmid0, *parts_f1[1:]))
    back0 = functools.partial(
        att_backward, table, (noisy, wp_t, pos), qkv0, lse0, go0, mods=mods0a, wqkv=wqkv0, cond=act_t, gmf=None,
        B=B, bottom=True, pack=qkv_pack0, parts=2,
    )
    half = back0(gmid=after(gmid0, *sends_a1), part=0)
    mark = half[0]
    parts_1, sends_1 = member_stage([parts_f1, held(parts_a1, mark)], None)
    parts_f0, sends_f0 = outer_stage([after(p, *sends_1) for p in held(parts_f0, mark)])
    gma0, keep_a0, send_a0 = back0(gmid=after(gmid0, *sends_f0), part=1, before=half)
    parts_a0 = reduce_first(keep_a0, send_a0)
    parts_f0 = held(parts_f0, gma0)
    piece_1 = reduce_last(held(parts_1, gma0), 0, table)
    rows0 = small_kernel(
        functools.partial(cond_back_kernel, n), [((4 * n, D), BF)], [],
        (table, after(gma0, piece_1), gmb0, gma1, gmb1, gmf, wa0a, wa0b, wa1, wm, w2, cond, pre_time,
         time_act, feats, label_parts, squares),
    )[0]
    parts_a0, sends_a0 = outer_stage(held(parts_a0, rows0, *parts_f0[1:]))
    pieces_1 = spread_core(spread_outer(piece_1, nr), nr)
    outer_state, inner_state = (w_out, out_mom, out_ema), (w_in, in_mom, in_ema)
    new_1 = update(table, offsets, pieces_1, 1, (outer_pack, qkv_pack1), outer_state, inner_state, (head, head_mom, head_ema), None)
    parts_0, sends_0 = member_stage([parts_f0, parts_a0], rows0)
    piece_0 = reduce_last(parts_0, 4 * n, table)
    pieces_0 = spread_core([(m, after(v, new_1[0])) for m, v in spread_outer(piece_0, nr)], nr)
    extra = ng * 4 * n
    new_0 = update(table, offsets, pieces_0, 0, (outer_pack, qkv_pack0), outer_state, inner_state, None, new_1[:6])
    own_rows = -(-(emb_rows + 7) // 8) * 8
    grad_rows = max(emb_full, emb_rows * (ng - 1) // 8 * 8 + own_rows)
    new_emb = small_kernel(
        functools.partial(
            emb_kernel, n, 1.0 / entries, tuple(len(m) for m, _ in pieces_0), extra, offsets["member"], emb_rows
        ),
        [(emb_table.shape, F32)] * 3 + [((1, 1), F32)],
        [((2 * n * nr * ng, D), BF)] * 2 + [((grad_rows, D), F32), ((own_rows, D), F32)],
        (table, new_0[6], emb_table, emb_mom, emb_ema, *[v for _, v in pieces_0]),
    )
    return (new_emb[3].reshape(()), *new_emb[:3], *new_0[3:6], *new_0[:3], *new_1[6:9])


def solution(mesh):
    data = P(("rep", "grp"), None, None)
    vector = P(("rep", "grp"))
    flat = P("grp", None)
    deep = P(None, "grp", None)
    return jax.shard_map(
        local,
        mesh=mesh,
        in_specs=(data, data, vector, vector, flat, flat, flat, deep, deep, deep, deep, deep, deep,
                  flat, flat, flat),
        out_specs=(P(), flat, flat, flat, deep, deep, deep, deep, deep, deep, flat, flat, flat),
        check_vma=False,
    )
```

```python
import functools
import math

import jax
import jax.numpy as jnp
from jax import lax
from jax.experimental import pallas as pl
from jax.experimental.pallas import tpu as pltpu
from jax.sharding import PartitionSpec as P

D = 384
HEADS = 6
HEAD_DIM = 64
FF = 1536
TOK = 256
PATCH_IN = 16
EPSILON = 1e-06
BF = jnp.bfloat16
F32 = jnp.float32
VMEM_LIMIT = 58 * 1024 * 1024


def mm(left, right):
    return lax.dot_general(left, right, (((1,), (0,)), ((), ())), preferred_element_type=F32)


def mm_nt(left, right):
    return lax.dot_general(left, right, (((1,), (1,)), ((), ())), preferred_element_type=F32)


def norm_parts(x):
    centered = x - jnp.mean(x, axis=0, keepdims=True)
    variance = jnp.mean(centered * centered, axis=0, keepdims=True)
    inv = lax.rsqrt(variance + EPSILON)
    return centered * inv, inv


def norm_back(d, normed, inv, scale1):
    dn = d * scale1
    m1 = jnp.mean(dn, axis=0, keepdims=True)
    m2 = jnp.mean(dn * normed, axis=0, keepdims=True)
    return (dn - m1 - normed * m2) * inv


def column(mods_ref, index, image):
    block = mods_ref[pl.ds(index * D, D), :]
    lane = lax.broadcasted_iota(jnp.int32, block.shape, 1)
    return jnp.sum(jnp.where(lane == image, block, 0.0), axis=1, keepdims=True)


def put_column(out_ref, index, image, values):
    total = jnp.sum(values, axis=1, keepdims=True)
    rows = pl.ds(index * D, D)
    old = out_ref[rows, :]
    lane = lax.broadcasted_iota(jnp.int32, old.shape, 1)
    out_ref[rows, :] = jnp.where(lane == image, total, old)


def half_zero(x, half):
    row = lax.broadcasted_iota(jnp.int32, x.shape, 0)
    keep = row < HEAD_DIM if half == 0 else row >= HEAD_DIM
    return jnp.where(keep, x, jnp.zeros_like(x))


def head_groups(B):
    work = [(b, h) for b in range(B) for h in range(HEADS)]
    return [work[i : i + HEAD_GROUP] for i in range(0, len(work), HEAD_GROUP)]


def pair_rows(ref, b, h, base=0):
    lo = base + 2 * HEAD_DIM * (h // 2)
    return ref[b, lo : lo + 2 * HEAD_DIM, :]


def head_rows(ref, b, h, base=0):
    return ref[b, base + HEAD_DIM * h : base + HEAD_DIM * (h + 1), :]


def attention_forward(qkv_ref, B, lse_ref, att_ref):
    for work in head_groups(B):
        scores = [
            mm(pair_rows(qkv_ref, b, h, D).T, half_zero(pair_rows(qkv_ref, b, h), h % 2)) for b, h in work
        ]
        peaks = [jnp.max(x, axis=0, keepdims=True) for x in scores]
        exps = [jnp.exp(x - p) for x, p in zip(scores, peaks)]
        totals = [jnp.sum(x, axis=0, keepdims=True) for x in exps]
        outs = [mm(head_rows(qkv_ref, b, h, 2 * D), x.astype(BF)) for (b, h), x in zip(work, exps)]
        for (b, h), out, total, peak in zip(work, outs, totals, peaks):
            att_ref[HEAD_DIM * h : HEAD_DIM * (h + 1), lanes_of(b)] = (out * (1.0 / total)).astype(BF)
            lse_ref[b, h : h + 1, :] = peak + jnp.log(total)


def attention_backward(qkv_ref, B, lse_ref, go_ref, gqkv_ref):
    for work in head_groups(B):
        scores = [
            mm(pair_rows(qkv_ref, b, h, D).T, half_zero(pair_rows(qkv_ref, b, h), h % 2)) for b, h in work
        ]
        gprobs = [
            mm(pair_rows(qkv_ref, b, h, 2 * D).T, half_zero(pair_rows(go_ref, b, h), h % 2)) for b, h in work
        ]
        probs = [jnp.exp(x - lse_ref[b, h : h + 1, :]) for x, (b, h) in zip(scores, work)]
        inners = [jnp.sum(p * g, axis=0, keepdims=True) for p, g in zip(probs, gprobs)]
        gscores = [(p * (g - i)).astype(BF) for p, g, i in zip(probs, gprobs, inners)]
        gqs = [mm(head_rows(qkv_ref, b, h, D), g) for (b, h), g in zip(work, gscores)]
        gks = [mm_nt(head_rows(qkv_ref, b, h), g) for (b, h), g in zip(work, gscores)]
        gvs = [mm_nt(head_rows(go_ref, b, h), p.astype(BF)) for (b, h), p in zip(work, probs)]
        for (b, h), gq, gk, gv in zip(work, gqs, gks, gvs):
            row = HEAD_DIM * h
            for base, value in ((0, gq * (1.0 / math.sqrt(HEAD_DIM))), (D, gk), (2 * D, gv)):
                gqkv_ref[base + row : base + row + HEAD_DIM, lanes_of(b)] = value.astype(BF)


def project_qkv(wqkv_t_ref, normed_ref, qkv_ref, B):
    for part in range(3):
        qkv = mm(wqkv_t_ref[D * part : D * (part + 1), :], normed_ref[...])
        if part == 0:
            qkv = qkv * (1.0 / math.sqrt(HEAD_DIM))
        qkv = qkv.astype(BF)
        for b in range(B):
            qkv_ref[b, D * part : D * (part + 1), :] = qkv[:, TOK * b : TOK * (b + 1)]


def lanes_of(b):
    return slice(TOK * b, TOK * (b + 1))


def modulate_into(normed_ref, b, normed, scale1, shift):
    normed_ref[:, lanes_of(b)] = (normed * scale1 + shift).astype(BF)


def ffn_chunks():
    return [slice(f, f + FF_CHUNK) for f in range(0, FF, FF_CHUNK)]


def add_up(total, part):
    return part if total is None else total + part


GELU_C = 0.7978845608
GELU_A = 0.044715


def gelu_both(v):
    square = v * v
    t = jnp.tanh(v * (GELU_C + (GELU_C * GELU_A) * square))
    half = 0.5 + 0.5 * t
    slope = half + 0.5 * v * (1.0 - t * t) * (GELU_C + (3.0 * GELU_C * GELU_A) * square)
    return v * half, slope


def gelu_one(v):
    t = jnp.tanh(v * (GELU_C + (GELU_C * GELU_A) * (v * v)))
    return v * (0.5 + 0.5 * t)


def clear(*refs):
    for ref in refs:
        ref[...] = jnp.zeros_like(ref)


FF_CHUNK = 768
HEAD_GROUP = 12


def pack_blocks(pack_ref, start, value):
    members = pack_ref.shape[0]
    rows = D // members
    count = value.shape[1] // D
    for g in range(members):
        for c in range(count):
            pack_ref[g, start + rows * c : start + rows * (c + 1), :] = value[
                rows * g : rows * (g + 1), D * c : D * (c + 1)
            ].astype(BF)
    return start + rows * count


def pack_outer(pack_ref, awo_ref, awf_ref, awg_ref):
    members = pack_ref.shape[0]
    rows = (D + FF) // members
    for g in range(members):
        low, high = rows * g, rows * (g + 1)
        if low < D:
            cut = min(high, D)
            pack_ref[g, 0 : cut - low, :] = awo_ref[low:cut, :].astype(BF)
        if high > D:
            cut = max(low, D)
            pack_ref[g, cut - low : rows, :] = awg_ref[cut - D : high - D, :].astype(BF)
    return pack_blocks(pack_ref, rows, awf_ref)


def pack_rest(pack_ref, used, extra):
    if extra is not None:
        for g in range(pack_ref.shape[0]):
            pack_ref[g, used : used + PATCH_IN, :] = extra.astype(BF)
        used += PATCH_IN
    if used < pack_ref.shape[1]:
        pack_ref[:, used:, :] = jnp.zeros_like(pack_ref[:, used:, :])


def split_pack(pack_ref, table_ref, offset, outs):
    for j, out_ref in enumerate(outs):
        rows = out_ref.shape[1]
        at = pl.multiple_of(table_ref[offset + j] * rows, rows)
        out_ref[...] = pack_ref[:, pl.ds(at, rows), :]


def att_fwd_kernel(B, offset, held, noisy_ref, wp_t_ref, pos_ref, mods_ref, wqkv_t_ref, *refs):
    qkv_ref, lse_ref, att_out_ref, normed_ref, att_ref = refs[held:]
    step = pl.program_id(0)
    for b in range(B):
        image = (offset + step) * B + b
        hidden = mm(wp_t_ref[...], noisy_ref[b]) + pos_ref[...]
        normed, _ = norm_parts(hidden)
        modulate_into(normed_ref, b, normed, 1.0 + column(mods_ref, 1, image), column(mods_ref, 0, image))
    project_qkv(wqkv_t_ref, normed_ref, qkv_ref, B)
    attention_forward(qkv_ref, B, lse_ref, att_ref)
    for b in range(B):
        att_out_ref[b] = att_ref[:, lanes_of(b)]


def ffn_fwd_kernel(B, noisy_ref, wp_t_ref, pos_ref, att_ref, mods_a_ref, mods_b_ref, wo_t_ref, wf_t_ref,
                   wg_t_ref, mid_ref, bra_ref, brb_ref, hid_ref, normed_ref):
    step = pl.program_id(0)
    for b in range(B):
        image = step * B + b
        hidden = mm(wp_t_ref[...], noisy_ref[b]) + pos_ref[...]
        branch_a = mm(wo_t_ref[...], att_ref[b])
        bra_ref[b] = branch_a.astype(BF)
        mid = hidden + column(mods_a_ref, 2, image) * branch_a
        mid_ref[b] = mid
        normed, _ = norm_parts(mid)
        modulate_into(normed_ref, b, normed, 1.0 + column(mods_b_ref, 1, image), column(mods_b_ref, 0, image))
    branch = None
    for rows in ffn_chunks():
        act = gelu_one(mm(wf_t_ref[rows, :], normed_ref[...])).astype(BF)
        branch = add_up(branch, mm(wg_t_ref[:, rows], act))
    for b in range(B):
        own = branch[:, lanes_of(b)]
        brb_ref[b] = own.astype(BF)
        hid_ref[b] = mid_ref[b] + column(mods_b_ref, 2, step * B + b) * own


def block_kernel(B, entries, table_ref, hid_ref, noise_ref, mods_ref, modf_ref, wqkv_t_ref, wo_t_ref, wf_t_ref,
                 wg_t_ref, wo_ref, wf_ref, wg_ref, wy_t_ref, wy_ref, cond_ref,
                 qkv_ref, lse_ref, go_ref, gmid_ref, gm_ref, gmf_ref, loss_ref,
                 keep_ref, send_ref,
                 pack_ref, normed_ref, att_ref, slope_ref, act_ref, gpre_ref, gba_ref, gbb_ref, normf_ref, gout_ref,
                 awo_ref, awf_ref, awg_ref, awy_ref, bra_ref, ghid_ref):
    step = pl.program_id(0)
    first = step == 0

    @pl.when(first)
    def _():
        clear(gm_ref, gmf_ref, loss_ref, awo_ref, awf_ref, awg_ref, awy_ref)

    image = lambda b: step * B + b
    for b in range(B):
        normed, _ = norm_parts(hid_ref[b])
        modulate_into(normed_ref, b, normed, 1.0 + column(mods_ref, 1, image(b)), column(mods_ref, 0, image(b)))
    project_qkv(wqkv_t_ref, normed_ref, qkv_ref, B)
    attention_forward(qkv_ref, B, lse_ref, att_ref)
    branch_a = mm(wo_t_ref[...], att_ref[...])
    for b in range(B):
        own = branch_a[:, lanes_of(b)]
        bra_ref[b] = own
        mid = hid_ref[b] + column(mods_ref, 2, image(b)) * own
        gmid_ref[b] = mid
        normed, _ = norm_parts(mid)
        modulate_into(normed_ref, b, normed, 1.0 + column(mods_ref, 4, image(b)), column(mods_ref, 3, image(b)))
    branch_b = None
    for rows in ffn_chunks():
        act, slope = gelu_both(mm(wf_t_ref[rows, :], normed_ref[...]))
        slope_ref[rows, :] = slope
        act_ref[rows, :] = act.astype(BF)
        branch_b = add_up(branch_b, mm(wg_t_ref[:, rows], act_ref[rows, :]))
    for b in range(B):
        lanes = lanes_of(b)
        own = branch_b[:, lanes]
        gate_b = column(mods_ref, 5, image(b))
        normed_f, inv_f = norm_parts(gmid_ref[b] + gate_b * own)
        scale_f = 1.0 + column(modf_ref, 1, image(b))
        modulate_into(normf_ref, b, normed_f, scale_f, column(modf_ref, 0, image(b)))
        residue = mm(wy_t_ref[...], normf_ref[:, lanes]) - noise_ref[b].astype(F32)
        loss_ref[...] += residue * residue
        gout_ref[:, lanes] = ((2.0 / entries) * residue).astype(BF)
        gnf = mm(wy_ref[...], gout_ref[:, lanes])
        put_column(gmf_ref, 0, image(b), gnf)
        put_column(gmf_ref, 1, image(b), gnf * normed_f)
        ghid = norm_back(gnf, normed_f, inv_f, scale_f)
        ghid_ref[b] = ghid
        put_column(gm_ref, 3, image(b), ghid * own)
        gbb_ref[:, lanes] = (gate_b * ghid).astype(BF)
    gnb = None
    for rows in ffn_chunks():
        gact = mm(wg_ref[rows, :], gbb_ref[...])
        gpre_ref[rows, :] = (gact * slope_ref[rows, :]).astype(BF)
        gnb = add_up(gnb, mm(wf_ref[:, rows], gpre_ref[rows, :]))
        awf_ref[:, rows] += mm_nt(normed_ref[...], gpre_ref[rows, :])
        awg_ref[rows, :] += mm_nt(act_ref[rows, :], gbb_ref[...])
    for b in range(B):
        own = gnb[:, lanes_of(b)]
        normed, inv = norm_parts(gmid_ref[b])
        put_column(gm_ref, 1, image(b), own)
        put_column(gm_ref, 2, image(b), own * normed)
        gmid = ghid_ref[b] + norm_back(own, normed, inv, 1.0 + column(mods_ref, 4, image(b)))
        gmid_ref[b] = gmid
        put_column(gm_ref, 0, image(b), gmid * bra_ref[b])
        gba_ref[:, lanes_of(b)] = (column(mods_ref, 2, image(b)) * gmid).astype(BF)
    go = mm(wo_ref[...], gba_ref[...]).astype(BF)
    for b in range(B):
        go_ref[b] = go[:, lanes_of(b)]
    awo_ref[...] += mm_nt(att_ref[...], gba_ref[...])
    awy_ref[...] += mm_nt(gout_ref[...], normf_ref[...])

    @pl.when(step == pl.num_programs(0) - 1)
    def _():
        used = pack_outer(pack_ref, awo_ref, awf_ref, awg_ref)
        used = pack_blocks(pack_ref, used, mm_nt(cond_ref[...], gm_ref[...].astype(BF)))
        pack_rest(pack_ref, used, awy_ref[...])
        split_pack(pack_ref, table_ref, 0, (keep_ref, send_ref))


def ffn_bwd_kernel(B, table_ref, ghid_ref, mid_ref, att_ref, bra_ref, brb_ref, mods_a_ref, mods_b_ref, wf_t_ref, wo_ref, wf_ref,
                   wg_ref, cond_ref, go_ref, gmid_ref, gm_ref, keep_ref, send_ref, pack_ref,
                   normed_ref, act_ref, gpre_ref, gba_ref, gbb_ref, atts_ref, awo_ref, awf_ref, awg_ref):
    step = pl.program_id(0)
    first = step == 0

    @pl.when(first)
    def _():
        clear(gm_ref, awo_ref, awf_ref, awg_ref)

    image = lambda b: step * B + b
    for b in range(B):
        lanes = lanes_of(b)
        ghid = ghid_ref[b]
        put_column(gm_ref, 3, image(b), ghid * brb_ref[b])
        gbb_ref[:, lanes] = (column(mods_b_ref, 2, image(b)) * ghid).astype(BF)
        normed, _ = norm_parts(mid_ref[b])
        modulate_into(normed_ref, b, normed, 1.0 + column(mods_b_ref, 1, image(b)), column(mods_b_ref, 0, image(b)))
        atts_ref[:, lanes] = att_ref[b]
    gnb = None
    for rows in ffn_chunks():
        act, slope = gelu_both(mm(wf_t_ref[rows, :], normed_ref[...]))
        act_ref[rows, :] = act.astype(BF)
        gact = mm(wg_ref[rows, :], gbb_ref[...])
        gpre_ref[rows, :] = (gact * slope).astype(BF)
        gnb = add_up(gnb, mm(wf_ref[:, rows], gpre_ref[rows, :]))
        awf_ref[:, rows] += mm_nt(normed_ref[...], gpre_ref[rows, :])
        awg_ref[rows, :] += mm_nt(act_ref[rows, :], gbb_ref[...])
    for b in range(B):
        own = gnb[:, lanes_of(b)]
        normed, inv = norm_parts(mid_ref[b])
        put_column(gm_ref, 1, image(b), own)
        put_column(gm_ref, 2, image(b), own * normed)
        gmid = ghid_ref[b] + norm_back(own, normed, inv, 1.0 + column(mods_b_ref, 1, image(b)))
        gmid_ref[b] = gmid
        put_column(gm_ref, 0, image(b), gmid * bra_ref[b])
        gba_ref[:, lanes_of(b)] = (column(mods_a_ref, 2, image(b)) * gmid).astype(BF)
    go = mm(wo_ref[...], gba_ref[...]).astype(BF)
    for b in range(B):
        go_ref[b] = go[:, lanes_of(b)]
    awo_ref[...] += mm_nt(atts_ref[...], gba_ref[...])

    @pl.when(step == pl.num_programs(0) - 1)
    def _():
        used = pack_outer(pack_ref, awo_ref, awf_ref, awg_ref)
        used = pack_blocks(pack_ref, used, mm_nt(cond_ref[...], gm_ref[...].astype(BF)))
        pack_rest(pack_ref, used, None)
        split_pack(pack_ref, table_ref, 0, (keep_ref, send_ref))


def att_bwd_kernel(B, offset, bottom, opens, closes, *refs):
    refs = list(refs)
    take = lambda count: [refs.pop(0) for _ in range(count)]
    (table_ref,) = take(1)
    noisy_ref, wp_t_ref, pos_ref = take(3) if bottom else (None, None, None)
    (hid_ref,) = (None,) if bottom else take(1)
    qkv_ref, lse_ref, go_ref, gmid_ref, mods_ref, wqkv_ref, cond_ref = take(7)
    (gmf_ref,) = (None,) if bottom else take(1)
    before = take(3 if bottom else 2) if not opens else []
    (ghid_ref,) = (None,) if bottom else take(1)
    (gm_ref,) = take(1)
    sums = 2 if bottom else 1
    keep_ref, send_ref, pack_ref, accs = None, None, None, None
    if closes:
        keep_ref, send_ref = take(2)
    else:
        accs = take(sums)
    if closes:
        (pack_ref,) = take(1)
    normed_ref, gqkv_ref = take(2)
    tok_ref, noi_ref = take(2) if bottom else (None, None)
    if closes:
        accs = take(sums)
    step = pl.program_id(0)
    first = step == 0

    @pl.when(first)
    def _():
        if opens:
            gm_ref[...] = jnp.zeros_like(gm_ref)
            for acc_ref in accs:
                acc_ref[...] = jnp.zeros_like(acc_ref)
        else:
            for to_ref, from_ref in zip([gm_ref] + accs, before):
                to_ref[...] = from_ref[...]

    image = lambda b: (offset + step) * B + b
    source = lambda b: mm(wp_t_ref[...], noisy_ref[b]) + pos_ref[...] if bottom else hid_ref[b]
    for b in range(B):
        normed, _ = norm_parts(source(b))
        modulate_into(normed_ref, b, normed, 1.0 + column(mods_ref, 1, image(b)), column(mods_ref, 0, image(b)))
    attention_backward(qkv_ref, B, lse_ref, go_ref, gqkv_ref)
    gna = mm(wqkv_ref[...], gqkv_ref[...])
    for b in range(B):
        own = gna[:, lanes_of(b)]
        normed, inv = norm_parts(source(b))
        put_column(gm_ref, 0, image(b), own)
        put_column(gm_ref, 1, image(b), own * normed)
        ghid = gmid_ref[b] + norm_back(own, normed, inv, 1.0 + column(mods_ref, 1, image(b)))
        if bottom:
            tok_ref[:, lanes_of(b)] = ghid.astype(BF)
            noi_ref[:, lanes_of(b)] = noisy_ref[b]
        else:
            ghid_ref[b] = ghid
    accs[0][...] += mm_nt(normed_ref[...], gqkv_ref[...])
    if bottom:
        accs[1][...] += mm_nt(noi_ref[...], tok_ref[...])

    if closes:
        @pl.when(step == pl.num_programs(0) - 1)
        def _():
            used = pack_blocks(pack_ref, 0, accs[0])
            used = pack_blocks(pack_ref, used, mm_nt(cond_ref[...], gm_ref[...].astype(BF)))
            if not bottom:
                used = pack_blocks(pack_ref, used, mm_nt(cond_ref[...], gmf_ref[...].astype(BF)))
            pack_rest(pack_ref, used, accs[1][...] if bottom else None)
            split_pack(pack_ref, table_ref, 0, (keep_ref, send_ref))


def whole(*shape):
    return pl.BlockSpec(shape, lambda i: (0,) * len(shape))


def images(B, *shape, offset=0):
    return pl.BlockSpec((B,) + shape, lambda i: (i + offset,) + (0,) * len(shape))


def sds(shape, dtype):
    return jax.ShapeDtypeStruct(shape, dtype)


def run_kernel(kernel, steps, in_specs, outs, scratch, flops, args, aliases=None):
    out_specs = [spec for spec, _, _ in outs]
    out_shape = [sds(shape, dtype) for _, shape, dtype in outs]
    moved = sum(a.size * a.dtype.itemsize for a in args) + sum(
        math.prod(o.shape) * o.dtype.itemsize for o in out_shape
    )
    return pl.pallas_call(
        kernel,
        grid=(steps,),
        in_specs=in_specs,
        out_specs=out_specs,
        out_shape=out_shape,
        scratch_shapes=[pltpu.VMEM(shape, dtype) for shape, dtype in scratch],
        input_output_aliases=aliases or {},
        compiler_params=pltpu.CompilerParams(vmem_limit_bytes=VMEM_LIMIT),
        cost_estimate=pl.CostEstimate(flops=8 * flops, bytes_accessed=moved, transcendentals=0),
    )(*args)


MODS = whole(6 * D, 128)
HALF_MODS = whole(3 * D, 128)
COND = whole(D, 128)
SCALARS = pl.BlockSpec(memory_space=pltpu.SMEM)


def halves(pack):
    ng, rows, _ = pack
    half = (ng, rows // 2, D)
    return [(whole(*half), half, BF)] * 2


def att_forward(noisy, wp_t, pos, mods, wqkv_t, B, part, parts, before):
    n = noisy.shape[0]
    T = B * TOK
    steps = n // B // parts
    here = functools.partial(images, B, offset=part * steps)
    return run_kernel(
        functools.partial(att_fwd_kernel, B, part * steps, len(before)), steps,
        [here(PATCH_IN, TOK), whole(D, PATCH_IN), whole(D, TOK), HALF_MODS, whole(3 * D, D)]
        + [pl.BlockSpec(memory_space=pl.ANY)] * len(before),
        [(here(3 * D, TOK), (n, 3 * D, TOK), BF), (here(8, TOK), (n, 8, TOK), F32),
         (here(D, TOK), (n, D, TOK), BF)],
        [((D, T), BF), ((D, T), BF)],
        2 * n * TOK * (3 * D * D + 2 * D * TOK) // parts, (noisy, wp_t, pos, mods, wqkv_t) + tuple(before),
        aliases={5 + i: i for i in range(len(before))})


def ffn_forward(noisy, wp_t, pos, att, mods_a, mods_b, wo_t, wf_t, wg_t, B):
    n = noisy.shape[0]
    T = B * TOK
    full = images(B, D, TOK)
    return run_kernel(
        functools.partial(ffn_fwd_kernel, B), n // B,
        [images(B, PATCH_IN, TOK), whole(D, PATCH_IN), whole(D, TOK), full, HALF_MODS, HALF_MODS, whole(D, D),
         whole(FF, D), whole(D, FF)],
        [(full, (n, D, TOK), F32), (full, (n, D, TOK), BF), (full, (n, D, TOK), BF), (full, (n, D, TOK), F32)],
        [((D, T), BF)],
        2 * n * TOK * (2 * D * FF + D * D), (noisy, wp_t, pos, att, mods_a, mods_b, wo_t, wf_t, wg_t))


def block_step(table, hid, noise, mods, modf, wqkv_t, wo_t, wf_t, wg_t, wo, wf, wg, wy_t, wy, cond, entries, B, pack):
    n = hid.shape[0]
    T = B * TOK
    full = images(B, D, TOK)
    return run_kernel(
        functools.partial(block_kernel, B, entries), n // B,
        [SCALARS, full, images(B, PATCH_IN, TOK), MODS, whole(2 * D, 128), whole(3 * D, D), whole(D, D),
         whole(FF, D), whole(D, FF), whole(D, D), whole(D, FF), whole(FF, D), whole(PATCH_IN, D),
         whole(D, PATCH_IN), COND],
        [(images(B, 3 * D, TOK), (n, 3 * D, TOK), BF), (images(B, 8, TOK), (n, 8, TOK), F32),
         (full, (n, D, TOK), BF), (full, (n, D, TOK), F32),
         (whole(4 * D, 128), (4 * D, 128), F32), (whole(2 * D, 128), (2 * D, 128), F32),
         (whole(PATCH_IN, TOK), (PATCH_IN, TOK), F32)] + halves(pack),
        [(pack, BF), ((D, T), BF), ((D, T), BF), ((FF, T), F32), ((FF, T), BF), ((FF, T), BF), ((D, T), BF),
         ((D, T), BF), ((D, T), BF), ((PATCH_IN, T), BF), ((D, D), F32), ((D, FF), F32), ((FF, D), F32),
         ((PATCH_IN, D), F32), ((B, D, TOK), F32), ((B, D, TOK), F32)],
        2 * n * TOK * (4 * D * D + 2 * D * TOK + 6 * D * FF + 2 * D * D),
        (table, hid, noise, mods, modf, wqkv_t, wo_t, wf_t, wg_t, wo, wf, wg, wy_t, wy, cond))


def ffn_backward(table, ghid, mid, att, bra, brb, mods_a, mods_b, wf_t, wo, wf, wg, cond, B, pack):
    n = mid.shape[0]
    T = B * TOK
    full = images(B, D, TOK)
    return run_kernel(
        functools.partial(ffn_bwd_kernel, B), n // B,
        [SCALARS, full, full, full, full, full, HALF_MODS, HALF_MODS, whole(FF, D), whole(D, D), whole(D, FF),
         whole(FF, D), COND],
        [(full, (n, D, TOK), BF), (full, (n, D, TOK), F32), (whole(4 * D, 128), (4 * D, 128), F32)] + halves(pack),
        [(pack, BF), ((D, T), BF), ((FF, T), BF), ((FF, T), BF), ((D, T), BF), ((D, T), BF), ((D, T), BF),
         ((D, D), F32), ((D, FF), F32), ((FF, D), F32)],
        2 * n * TOK * (5 * D * FF + 2 * D * D),
        (table, ghid, mid, att, bra, brb, mods_a, mods_b, wf_t, wo, wf, wg, cond))


def att_backward(table, source, qkv, lse, go, gmid, mods, wqkv, cond, gmf, B, bottom, pack, part=0, parts=1, before=()):
    n = qkv.shape[0]
    T = B * TOK
    steps = n // B // parts
    offset = part * steps
    opens, closes = part == 0, part == parts - 1
    here = functools.partial(images, B, offset=offset)
    full = here(D, TOK)
    gm = (whole(2 * D, 128), (2 * D, 128), F32)
    sums = [(whole(D, 3 * D), (D, 3 * D), F32)] + ([(whole(PATCH_IN, D), (PATCH_IN, D), F32)] if bottom else [])
    ins = [SCALARS] + ([here(PATCH_IN, TOK), whole(D, PATCH_IN), whole(D, TOK)] if bottom else [full])
    ins += [here(3 * D, TOK), here(8, TOK), full, full, HALF_MODS if bottom else MODS, whole(D, 3 * D), COND]
    ins += [] if bottom else [whole(2 * D, 128)]
    args = (table,) + tuple(source) + (qkv, lse, go, gmid, mods, wqkv, cond) + (() if bottom else (gmf,))
    if not opens:
        ins += [gm[0]] + [s[0] for s in sums]
        args += tuple(before)
    outs = ([] if bottom else [(full, (n, D, TOK), F32)]) + [gm] + (halves(pack) if closes else sums)
    scratch = ([(pack, BF)] if closes else []) + [((D, T), BF), ((3 * D, T), BF)]
    scratch += [((D, T), BF), ((PATCH_IN, T), BF)] if bottom else []
    scratch += [(s[1], F32) for s in sums] if closes else []
    return run_kernel(
        functools.partial(att_bwd_kernel, B, offset, bottom, opens, closes), steps, ins, outs, scratch,
        2 * n * TOK * (6 * D * D + 5 * D * TOK) // parts, args)


FREQ = 256
CLASSES = 1000
GRID = 16
LAYERS = 2
MOMENTUM = 0.9
LEARN = 30.0
DECAY = 0.7
IMAGES_PER_STEP = 2
SMALL_COST = 8 * 10**9


def plan(steps_in):
    anchor = math.cos(0.5 * math.pi * 0.008 / 1.008)
    fraction = (steps_in.astype(F32) / 1000.0 + 0.008) / 1.008
    levels = jnp.cos(0.5 * math.pi * fraction)
    return levels * levels / (anchor * anchor)


def time_features(steps_in):
    half_width = FREQ // 2
    frequencies = jnp.exp(-math.log(10000.0) * jnp.arange(half_width, dtype=F32) / half_width)
    angles = steps_in.astype(F32)[:, None] * frequencies[None, :]
    return jnp.concatenate([jnp.cos(angles), jnp.sin(angles)], axis=1)


def positions():
    quarter = D // 4
    omegas = jnp.exp(-math.log(10000.0) * jnp.arange(quarter, dtype=F32) / quarter)
    places = jnp.arange(GRID * GRID, dtype=jnp.int32)
    column = omegas[:, None] * (places % GRID).astype(F32)[None, :]
    row_pos = omegas[:, None] * (places // GRID).astype(F32)[None, :]
    return jnp.concatenate(
        [jnp.sin(column), jnp.cos(column), jnp.sin(row_pos), jnp.cos(row_pos)], axis=0
    )


def swish_parts(values):
    s = 1.0 / (1.0 + jnp.exp(-values))
    return values * s, s * (1.0 + values * (1.0 - s))


def advance(weight, moment, average, gradient):
    new_moment = MOMENTUM * moment + gradient
    new_weight = weight - LEARN * (gradient + MOMENTUM * new_moment)
    new_average = DECAY * average + (1.0 - DECAY) * new_weight
    return (new_weight, new_moment, new_average)


def after(x, *others):
    return lax.optimization_barrier((x,) + others)[0]


def swap(x, axis, mask):
    pairs = [(i, i ^ mask) for i in range(lax.axis_size(axis))]
    return lax.ppermute(x, axis, pairs)


def digit_list(n):
    found, shift = [], 0
    while (1 << shift) < n:
        left = n >> shift
        size = 2 if shift == 0 or left == 2 else 4
        found.append((shift, size))
        shift += size.bit_length() - 1
    return found


def place_of(index, n):
    place = 0
    for shift, size in digit_list(n):
        place = place * size + ((index >> shift) & (size - 1))
    return place


def place_table(emb_rows):
    nr, ng = lax.axis_size("rep"), lax.axis_size("grp")
    me, member = lax.axis_index("rep"), lax.axis_index("grp")
    entries, offsets = [], {}
    for shift, size in digit_list(nr):
        offsets[shift] = len(entries)
        entries += [((me >> shift) & (size - 1)) ^ j for j in range(size)]
    if not entries:
        entries = [0, 1]
    offsets["place"] = len(entries)
    entries += [place_of(me ^ mask, nr) for mask in range(nr)]
    offsets["member"] = len(entries)
    entries += [member ^ k for k in range(ng)]
    offsets["lead"] = len(entries)
    entries.append(emb_rows * member % 16)
    return jnp.stack([jnp.asarray(e, jnp.int32) for e in entries]), offsets


def in_vmem():
    return pl.BlockSpec(memory_space=pltpu.VMEM)


def small_kernel(kernel, outs, scratch, args, scalars=1):
    return pl.pallas_call(
        kernel,
        in_specs=[SCALARS] * scalars + [in_vmem()] * (len(args) - scalars),
        out_specs=[in_vmem()] * len(outs),
        out_shape=[sds(shape, dtype) for shape, dtype in outs],
        scratch_shapes=[pltpu.VMEM(shape, dtype) for shape, dtype in scratch],
        compiler_params=pltpu.CompilerParams(vmem_limit_bytes=VMEM_LIMIT),
        cost_estimate=pl.CostEstimate(flops=SMALL_COST, bytes_accessed=0, transcendentals=0),
    )(*args)


def spread_outer(piece, n):
    pieces = [((0,), piece)]
    digits = digit_list(n)[1:]
    for shift, size in digits:
        if len(pieces) > 1:
            pieces = [(sum((m for m, _ in pieces), ()), jnp.concatenate([v for _, v in pieces], axis=0))]
        masks, value = pieces[0]
        pieces = pieces + [
            (tuple(m ^ (j << shift) for m in masks), swap(value, "rep", j << shift)) for j in range(1, size)
        ]
    return pieces


def spread_core(pieces, n, marks=()):
    if n == 1:
        return pieces
    return pieces + [
        (tuple(m ^ 1 for m in masks), swap(after(value, *marks) if marks else value, "rep", 1))
        for masks, value in pieces
    ]


def gather_members(mine):
    got = [swap(mine, "grp", k) for k in range(1, lax.axis_size("grp"))]
    return jnp.concatenate(got, axis=0) if got else None


def sum_parts(parts):
    total = parts[0][...].astype(F32)
    for part in parts[1:]:
        total = total + part[...].astype(F32)
    return total.astype(BF)


def rows_kernel(count, offset, table_ref, *refs):
    parts, outs, total_ref = refs[:count], refs[count:-1], refs[-1]
    total_ref[...] = sum_parts(parts)
    split_pack(total_ref, table_ref, offset, outs)


def members_kernel(counts, offset, has_extra, table_ref, *refs):
    refs = list(refs)
    groups = [[refs.pop(0) for _ in range(c)] for c in counts]
    extra_ref = refs.pop(0) if has_extra else None
    outs, totals = refs[: -len(counts)], refs[-len(counts) :]
    for parts, total_ref in zip(groups, totals):
        total_ref[...] = sum_parts(parts)
    for k, out_ref in enumerate(outs):
        at = 0
        for total_ref in totals:
            rows = total_ref.shape[1]
            out_ref[at : at + rows, :] = total_ref[table_ref[offset + k]]
            at += rows
        if has_extra:
            out_ref[at:, :] = extra_ref[...]


def last_kernel(count, extra, table_ref, *refs):
    parts, out_ref = refs[:count], refs[-1]
    rows = parts[0].shape[0] - extra
    total = parts[0][0:rows, :].astype(F32)
    for part in parts[1:]:
        total = total + part[0:rows, :].astype(F32)
    out_ref[0:rows, :] = total.astype(BF)
    if extra:
        for i, part in enumerate(parts):
            out_ref[rows + extra * i : rows + extra * (i + 1), :] = part[rows:, :]


def reduce_first(keep, send):
    return [keep, swap(send, "rep", 1)] if lax.axis_size("rep") > 1 else [keep]


def reduce_outer(parts, table, offsets, number):
    shift, size = digit_list(lax.axis_size("rep"))[number]
    ng, rows, _ = parts[0].shape
    one = lambda r: pl.BlockSpec((1, r, D), lambda i: (i, 0, 0))
    cut = pl.pallas_call(
        functools.partial(rows_kernel, len(parts), offsets[shift]),
        grid=(ng,),
        in_specs=[SCALARS] + [one(rows)] * len(parts),
        out_specs=[one(rows // size)] * size,
        out_shape=[sds((ng, rows // size, D), BF)] * size,
        scratch_shapes=[pltpu.VMEM((1, rows, D), BF)],
    )(table, *parts)
    return [cut[0]], cut[1:], shift


def exchange(own, sends, axis, shift):
    return own + [swap(x, axis, (j + 1) << shift) for j, x in enumerate(sends)]


def reduce_members(groups, extra, table, offsets):
    ng = groups[0][0].shape[0]
    rows = sum(g[0].shape[1] for g in groups) + (0 if extra is None else extra.shape[0])
    cut = small_kernel(
        functools.partial(members_kernel, tuple(len(g) for g in groups), offsets["member"], extra is not None),
        [((rows, D), BF)] * ng, [(g[0].shape, BF) for g in groups],
        (table, *sum(groups, []), *([] if extra is None else [extra])),
    )
    return [cut[0]], cut[1:], 0


def reduce_last(parts, extra, table):
    rows = parts[0].shape[0] + extra * (len(parts) - 1)
    return small_kernel(
        functools.partial(last_kernel, len(parts), extra), [((rows, D), BF)], [], (table, *parts)
    )[0]


def pack_first_kernel(lead_at, emb_real, shard_place, table_ref, emb_ref, wa_ref, wqkv_ref, shard_ref, mine_ref, wide_ref):
    wide_ref[...] = jnp.zeros_like(wide_ref)
    wide_ref[0:emb_real, :] = emb_ref[...]
    seg = wide_ref.shape[0]
    shard_ref[0:seg, :] = pltpu.roll(wide_ref[...], table_ref[lead_at], 0).astype(BF)
    at = seg
    for ref in (wa_ref, wqkv_ref):
        for c in range(3):
            rows = ref.shape[1]
            shard_ref[at : at + rows, :] = ref[0, :, D * c : D * (c + 1)].astype(BF)
            at += rows
    if at < shard_ref.shape[0]:
        shard_ref[at:, :] = jnp.zeros_like(shard_ref[at:, :])
    rows = mine_ref.shape[0]
    mine_ref[...] = shard_ref[pl.ds(pl.multiple_of(table_ref[shard_place] * rows, rows), rows), :]


def pack_first(table, offsets, emb_table, w_in, seg, unit):
    nr = lax.axis_size("rep")
    rows = w_in.shape[1]
    total = -(-(seg + 6 * rows) // unit) * unit
    part = lambda c: pl.BlockSpec((1, rows, 3 * D), lambda i: (0, 0, c))
    return pl.pallas_call(
        functools.partial(pack_first_kernel, offsets["lead"], emb_table.shape[0], offsets["place"]),
        grid=(1,),
        in_specs=[SCALARS, whole(*emb_table.shape), part(0), part(2)],
        out_specs=[whole(total, D), whole(total // nr, D)],
        out_shape=[sds((total, D), BF), sds((total // nr, D), BF)],
        scratch_shapes=[pltpu.VMEM((seg, D), F32)],
        compiler_params=pltpu.CompilerParams(vmem_limit_bytes=VMEM_LIMIT),
    )(table, emb_table, w_in, w_in)


def pack_other_kernel(layouts, shard_place, table_ref, *refs):
    refs = list(refs)
    inputs = [[refs.pop(0) for _ in layout] for layout in layouts]
    shard_refs, mine_ref = refs[:-1], refs[-1]
    put = 0
    for layout, ins, shard_ref in zip(layouts, inputs, shard_refs):
        at = 0
        for ref, count in zip(ins, layout):
            rows = ref.shape[-2]
            for c in range(count):
                cols = slice(D * c, D * (c + 1))
                value = ref[0, :, cols] if len(ref.shape) == 3 else ref[:, cols]
                shard_ref[at : at + rows, :] = value.astype(BF)
                at += rows
            if len(ref.shape) == 2:
                value = ref[:, D * count :]
                shard_ref[at : at + rows, :] = jnp.concatenate(
                    [value, jnp.zeros((rows, D - value.shape[1]), F32)], axis=1
                ).astype(BF)
                at += rows
        if at < shard_ref.shape[0]:
            shard_ref[at:, :] = jnp.zeros_like(shard_ref[at:, :])
        rows = shard_ref.shape[0] * mine_ref.shape[0] // sum(r.shape[0] for r in shard_refs)
        from_rows = pl.ds(pl.multiple_of(table_ref[shard_place] * rows, rows), rows)
        mine_ref[put : put + rows, :] = shard_ref[from_rows, :]
        put += rows


def pack_other(table, offsets, shards):
    nr = lax.axis_size("rep")
    spec = lambda shape, index: pl.BlockSpec(shape, lambda i: index)
    parts = sum((p for _, p in shards), [])
    shapes = [(rows, D) for rows, _ in shards] + [(sum(rows for rows, _ in shards) // nr, D)]
    return pl.pallas_call(
        functools.partial(
            pack_other_kernel, tuple(tuple(p[3] for p in ps) for _, ps in shards), offsets["place"]
        ),
        grid=(1,),
        in_specs=[SCALARS] + [spec(p[1], p[2]) for p in parts],
        out_specs=[whole(*shape) for shape in shapes],
        out_shape=[sds(shape, BF) for shape in shapes],
        compiler_params=pltpu.CompilerParams(vmem_limit_bytes=VMEM_LIMIT),
    )(table, *[p[0] for p in parts])


def fill_full(full_ref, masks, place, member, table_ref, shard_ref, pieces):
    ng = full_ref.shape[0]
    full_ref[table_ref[member]] = shard_ref[...]
    for group, ref in zip(masks, pieces):
        rows = ref.shape[0] // (len(group) * (ng - 1))
        for i, mask in enumerate(group):
            at = pl.ds(pl.multiple_of(table_ref[place + mask] * rows, rows), rows)
            for k in range(1, ng):
                start = (i * (ng - 1) + k - 1) * rows
                full_ref[table_ref[member + k], at, :] = ref[start : start + rows, :]


def take_blocks(full_ref, start, count, out_ref):
    ng = full_ref.shape[0]
    step = D // ng
    for g in range(ng):
        for c in range(count):
            out_ref[step * g : step * (g + 1), D * c : D * (c + 1)] = full_ref[
                g, start + step * c : start + step * (c + 1), :
            ]
    return start + step * count


def take_outer(full_ref, start, wo_ref, wg_ref):
    ng = full_ref.shape[0]
    wide = (D + FF) // ng
    for g in range(ng):
        low, high = wide * g, wide * (g + 1)
        if low < D:
            cut = min(high, D)
            wo_ref[low:cut, :] = full_ref[g, start : start + cut - low, :]
        if high > D:
            cut = max(low, D)
            wg_ref[cut - D : high - D, :] = full_ref[g, start + cut - low : start + wide, :]
    return start + wide


def first_kernel(emb_rows, seg, masks, place, member, table_ref, shard_ref, feats_ref, labels_ref, *refs):
    pieces, rest = refs[: len(masks)], refs[len(masks) :]
    (wp_t_ref, w2_ref, wa_ref, wqkv_ref, wqkv_t_ref, mods_ref, time_act_ref, pre_ref, cond_ref, act_t_ref,
     full_ref, emb_ref) = rest
    fill_full(full_ref, masks, place, member, table_ref, shard_ref, pieces)
    ng = full_ref.shape[0]
    emb_ref[...] = jnp.zeros_like(emb_ref)
    for g in range(ng):
        base = emb_rows * g // 16 * 16
        emb_ref[base : base + seg, :] = emb_ref[base : base + seg, :] + full_ref[g, 0:seg, :]
    at = take_blocks(full_ref, seg, 3, wa_ref)
    take_blocks(full_ref, at, 3, wqkv_ref)
    wqkv_t_ref[...] = wqkv_ref[...].T
    wp_t_ref[...] = emb_ref[0:128, :].T[:, 0:PATCH_IN]
    w1 = emb_ref[PATCH_IN : PATCH_IN + FREQ, :]
    w2_ref[...] = emb_ref[PATCH_IN + FREQ : PATCH_IN + FREQ + D, :]
    classes = emb_ref[PATCH_IN + FREQ + D : PATCH_IN + FREQ + D + CLASSES + 8, :]
    pre = mm(feats_ref[...], w1)
    pre_ref[...] = pre
    time_act = swish_parts(pre)[0].astype(BF)
    time_act_ref[...] = time_act
    hot = labels_ref[...] == lax.broadcasted_iota(jnp.int32, (labels_ref.shape[0], CLASSES + 8), 1)
    cond = mm(time_act, w2_ref[...]) + mm(jnp.where(hot, 1.0, 0.0).astype(BF), classes)
    cond_ref[...] = cond
    act = swish_parts(cond)[0]
    act_t_ref[...] = act.T.astype(BF)
    mods_ref[...] = mm(wa_ref[...].T, act_t_ref[...])


def second_kernel(masks, place, member, table_ref, shard_ref, act_t_ref, *refs):
    pieces, rest = refs[: len(masks)], refs[len(masks) :]
    wo_ref, wg_ref, wo_t_ref, wg_t_ref, wf_ref, wf_t_ref, wa_ref, mods_ref, full_ref = rest
    fill_full(full_ref, masks, place, member, table_ref, shard_ref, pieces)
    at = take_outer(full_ref, 0, wo_ref, wg_ref)
    at = take_blocks(full_ref, at, 4, wf_ref)
    take_blocks(full_ref, at, 3, wa_ref)
    wo_t_ref[...] = wo_ref[...].T
    wg_t_ref[...] = wg_ref[...].T
    wf_t_ref[...] = wf_ref[...].T
    mods_ref[...] = mm(wa_ref[...].T, act_t_ref[...])


def third_kernel(masks, place, member, table_ref, shard_ref, act_t_ref, *refs):
    pieces, rest = refs[: len(masks)], refs[len(masks) :]
    (wo_ref, wg_ref, wo_t_ref, wg_t_ref, wf_ref, wf_t_ref, wqkv_ref, wqkv_t_ref, wa_ref, wm_ref, wy_ref, wy_t_ref,
     mods_ref, modf_ref, full_ref, wide_ref) = rest
    fill_full(full_ref, masks, place, member, table_ref, shard_ref, pieces)
    at = take_outer(full_ref, 0, wo_ref, wg_ref)
    at = take_blocks(full_ref, at, 6, wa_ref)
    at = take_blocks(full_ref, at, 3, wqkv_ref)
    at = take_blocks(full_ref, at, 4, wf_ref)
    at = take_blocks(full_ref, at, 2, wm_ref)
    take_blocks(full_ref, at, 1, wide_ref)
    wo_t_ref[...] = wo_ref[...].T
    wg_t_ref[...] = wg_ref[...].T
    wf_t_ref[...] = wf_ref[...].T
    wqkv_t_ref[...] = wqkv_ref[...].T
    wy_ref[...] = wide_ref[:, 0:PATCH_IN]
    wy_t_ref[...] = wide_ref[...].T[0:PATCH_IN, :]
    mods_ref[...] = mm(wa_ref[...].T, act_t_ref[...])
    modf_ref[...] = mm(wm_ref[...].T, act_t_ref[...])


def assemble(kernel, table, offsets, shard, pieces, extra, outs, scratch):
    ng = lax.axis_size("grp")
    masks = tuple(m for m, v in pieces if v is not None)
    arrays = [v for _, v in pieces if v is not None]
    return small_kernel(
        functools.partial(kernel, masks, offsets["place"], offsets["member"]), outs,
        [((ng,) + shard.shape, BF)] + scratch, (table, shard, *extra, *arrays),
    )


def cond_back_kernel(n, table_ref, gma0_ref, gmb0_ref, gma1_ref, gmb1_ref, gmf_ref, wa0a_ref, wa0b_ref, wa1_ref, wm_ref,
                     w2_ref, cond_ref, pre_ref, time_act_ref, feats_ref, label_ref, squares_ref, rows_ref):
    low = lambda ref: ref[...].astype(BF)
    gact = mm(wm_ref[...], low(gmf_ref))
    gact += mm(wa1_ref[:, 0 : 2 * D], low(gma1_ref)) + mm(wa1_ref[:, 2 * D :], low(gmb1_ref))
    gact += mm(wa0a_ref[:, 0 : 2 * D], low(gma0_ref)) + mm(wa0a_ref[:, 2 * D :], gmb0_ref[0:D, :].astype(BF))
    gact += mm(wa0b_ref[...], gmb0_ref[D:, :].astype(BF))
    gcond = gact.T * swish_parts(cond_ref[...])[1]
    gpre = mm_nt(gcond.astype(BF), w2_ref[...]) * swish_parts(pre_ref[...])[1]
    total = jnp.sum(squares_ref[...]).reshape(1, 1)
    high = total.astype(BF).astype(F32)
    middle = (total - high).astype(BF).astype(F32)
    last = total - high - middle
    lane = lax.broadcasted_iota(jnp.int32, (n, 128), 1)
    row = lax.broadcasted_iota(jnp.int32, (n, 128), 0)
    loss = jnp.where(lane == 0, high, jnp.where(lane == 1, middle, jnp.where(lane == 2, last, 0.0)))
    loss = jnp.where(row == 0, loss, 0.0)
    loss = jnp.where(lane == 3, label_ref[:, 0:1], jnp.where(lane == 4, label_ref[:, 1:2], loss))
    top = jnp.concatenate([time_act_ref[...].astype(F32)[0:n], gpre[0:n]], axis=0)
    feats = jnp.concatenate([feats_ref[...].astype(F32)[0:n], loss], axis=1)
    rows_ref[0 : 2 * n, :] = top.astype(BF)
    rows_ref[2 * n : 4 * n, :] = jnp.concatenate([gcond[0:n], feats], axis=0).astype(BF)


def emb_kernel(n, inv_entries, counts, extra, member, emb_rows, table_ref, patch_ref, w_ref, m_ref, e_ref, *refs):
    pieces, refs = refs[: len(counts)], refs[len(counts) :]
    new_w_ref, new_m_ref, new_e_ref, loss_ref, left_ref, right_ref, grad_ref, own_ref = refs
    at = 0
    for ref, count in zip(pieces, counts):
        each = ref.shape[0] // count
        for i in range(count):
            for base in range(each * (i + 1) - extra, each * (i + 1), 4 * n):
                left_ref[at : at + 2 * n, :] = ref[base : base + 2 * n, :]
                right_ref[at : at + 2 * n, :] = ref[base + 2 * n : base + 4 * n, :]
                at += 2 * n
    total = left_ref.shape[0]
    row = lax.broadcasted_iota(jnp.int32, (total, D), 0)
    top = (row % (2 * n)) < n
    zero = jnp.zeros((total, D), BF)
    act = jnp.where(top, left_ref[...], zero)
    gcond = jnp.where(top, right_ref[...], zero)
    gpre = jnp.where(top, zero, left_ref[...])
    feats = right_ref[:, 0:FREQ]
    tags = right_ref[:, FREQ:].astype(F32).T
    label = (tags[3:4, :] * 32.0 + tags[4:5, :]).astype(jnp.int32)
    label = pltpu.roll(jnp.broadcast_to(label, (8, total)), total - n, 1)[0:1, :]
    hot = label == lax.broadcasted_iota(jnp.int32, (CLASSES + 8, total), 0)
    grad_ref[0:PATCH_IN, :] = patch_ref[0:PATCH_IN, :]
    grad_ref[PATCH_IN : PATCH_IN + FREQ, :] = mm(feats.T, gpre)
    grad_ref[PATCH_IN + FREQ : PATCH_IN + FREQ + D, :] = mm(act.T, gcond)
    grad_ref[PATCH_IN + FREQ + D : PATCH_IN + FREQ + D + CLASSES + 8, :] = mm(jnp.where(hot, 1.0, 0.0).astype(BF), gcond)
    rows = own_ref.shape[0]
    start = emb_rows * table_ref[member]
    low = start // 8 * 8
    block = grad_ref[pl.ds(pl.multiple_of(low, 8), rows), :]
    own_ref[...] = pltpu.roll(block, lax.rem(rows - (start - low), rows), 0)
    new = advance(w_ref[...], m_ref[...], e_ref[...], own_ref[0:emb_rows, :])
    new_w_ref[...], new_m_ref[...], new_e_ref[...] = new
    spot = lax.broadcasted_iota(jnp.int32, tags.shape, 1) % (2 * n) >= n
    spot &= lax.broadcasted_iota(jnp.int32, tags.shape, 0) < 3
    loss_ref[...] = jnp.sum(jnp.where(spot, tags, 0.0)).reshape(1, 1) * inv_entries


def update_kernel(masks, place, member, sizes, step_rows, layout, has_head, n_chain, table_ref, *refs):
    pieces, refs = refs[: len(masks)], refs[len(masks) :]
    count = 9 if has_head else 6
    states, refs = refs[:count], refs[count + n_chain :]
    news, refs = refs[:count], refs[count:]
    rest_ref, shard_refs = (None, refs) if has_head else (refs[0], refs[1:])
    step = pl.program_id(0)

    @pl.when(step == 0)
    def _():
        for group, ref in zip(masks, pieces):
            each = ref.shape[0] // len(group)
            for i, mask in enumerate(group):
                start = each * i
                for rows, shard_ref in zip(sizes, shard_refs):
                    at = pl.ds(pl.multiple_of(table_ref[place + mask] * rows, rows), rows)
                    shard_ref[at, :] = ref[start : start + rows, :]
                    start += rows
        if not has_head:
            shard_ref = shard_refs[1]
            rest_ref[...] = shard_ref[shard_ref.shape[0] - rest_ref.shape[0] :, :].astype(F32)
        else:
            rows = states[6].shape[0]
            state = [r[...] for r in states[6:]]
            start = layout[-1][1] + rows
            for c in range(2):
                cols = slice(D * c, D * (c + 1))
                grad = shard_refs[1][start + rows * c : start + rows * (c + 1), :].astype(F32)
                for ref, value in zip(news[6:], advance(*(x[:, cols] for x in state), grad)):
                    ref[:, cols] = value
            start = layout[7][1] + rows
            flat = shard_refs[0][start : start + PATCH_IN, :].astype(F32)
            turn = jnp.where(table_ref[member] == 0, 0, D - rows * table_ref[member])
            grad = pltpu.roll(flat, turn, 1)[:, 0:128].T[0:rows, :]
            for ref, value in zip(news[6:], advance(*(x[:, 2 * D :] for x in state), grad)):
                ref[:, 2 * D :] = value

    out_rows = states[0].shape[1]
    at = pl.multiple_of(step * out_rows, 16)
    grad = shard_refs[0][pl.ds(at, out_rows), :].astype(F32)
    for ref, value in zip(news[:3], advance(*(r[0] for r in states[:3]), grad)):
        ref[0] = value
    for group, row, block in layout:
        cols = slice(D * block, D * (block + 1))
        at = pl.multiple_of(row + step * step_rows, 16)
        grad = shard_refs[group][pl.ds(at, step_rows), :].astype(F32)
        for ref, value in zip(news[3:6], advance(*(r[0, :, cols] for r in states[3:6]), grad)):
            ref[0, :, cols] = value


def update(table, offsets, pieces, layer, packs, outer, inner, head, chain):
    nr = lax.axis_size("rep")
    rows, wide = inner[0].shape[1], inner[0].shape[2]
    rows_out = outer[0].shape[1]
    step_rows = 16
    steps = rows // step_rows
    masks = tuple(m for m, _ in pieces)
    arrays = [v for _, v in pieces]
    sizes = tuple(p[1] // nr for p in packs)
    layout = [(0, rows_out + rows * i, 9 + i) for i in range(4)]
    layout += [(0, rows_out + rows * (4 + i), 2 + i) for i in range(4)]
    layout += [(1, rows * i, 6 + i) for i in range(3)] + [(1, rows * (3 + i), i) for i in range(2)]
    rests = [] if head else [packs[1][1] - 5 * rows]
    in_spec = pl.BlockSpec((1, step_rows, wide), lambda i: (layer, i, 0))
    out_spec = pl.BlockSpec((1, rows_out // steps, D), lambda i: (layer, i, 0))
    states = list(outer) + list(inner) + list(head or ())
    specs = [out_spec] * 3 + [in_spec] * 3 + [whole(*h.shape) for h in head or ()]
    chain = list(chain) if chain else []
    first = 1 + len(arrays) + len(states)
    return pl.pallas_call(
        functools.partial(
            update_kernel, masks, offsets["place"], offsets["member"], sizes, step_rows, tuple(layout), bool(head),
            len(chain),
        ),
        grid=(steps,),
        in_specs=[SCALARS] + [whole(*a.shape) for a in arrays] + specs
        + [pl.BlockSpec(memory_space=pl.ANY)] * len(chain),
        out_specs=specs + [whole(r, D) for r in rests],
        out_shape=[sds(s.shape, F32) for s in states] + [sds((r, D), F32) for r in rests],
        scratch_shapes=[pltpu.VMEM((p[1], D), BF) for p in packs],
        input_output_aliases={first + i: i for i in range(len(chain))},
        compiler_params=pltpu.CompilerParams(vmem_limit_bytes=VMEM_LIMIT),
    )(table, *arrays, *states, *chain)


def local(
    latents, noise, timesteps, labels, emb_table, emb_mom, emb_ema, w_in, in_mom, in_ema,
    w_out, out_mom, out_ema, head, head_mom, head_ema,
):
    nr, ng = lax.axis_size("rep"), lax.axis_size("grp")
    member = lax.axis_index("grp")
    n = latents.shape[0]
    B = IMAGES_PER_STEP
    unit = 16 * nr
    digits = digit_list(nr)
    rows_d = D // ng
    rows_out = (D + FF) // ng
    emb_rows = emb_table.shape[0]
    seg = -(-(emb_rows + 15) // 16) * 16
    emb_full = emb_rows * (ng - 1) // 16 * 16 + seg
    full_rows = lambda rows: -(-rows // unit) * unit
    table, offsets = place_table(emb_rows)

    shard1, mine1 = pack_first(table, offsets, emb_table, w_in, seg, unit)
    got1 = gather_members(mine1)
    three, one = (1, rows_d, 3 * D), (1, rows_d, D)
    shard2, shard3, mine23 = pack_other(
        table, offsets,
        [
            (full_rows(rows_out + 7 * rows_d),
             [(w_out, (1, rows_out, D), (0, 0, 0), 1), (w_in, three, (0, 0, 3), 3), (w_in, one, (0, 0, 12), 1),
              (w_in, three, (0, 0, 1), 3)]),
            (full_rows(rows_out + 16 * rows_d),
             [(w_out, (1, rows_out, D), (1, 0, 0), 1), (w_in, (1, rows_d, 13 * D), (1, 0, 0), 13),
              (head, head.shape, (0, 0), 2)]),
        ],
    )
    around1 = spread_outer(after(got1, mine23), nr)
    cut2 = shard2.shape[0] // nr
    came1 = [v for m, v in around1 if m != (0,)]
    mine2 = after(mine23[:cut2], got1)
    parts2 = [swap(after(mine2, came1[0]) if k == 3 else mine2, "grp", k) for k in range(1, ng)]
    got2 = jnp.concatenate(parts2, axis=0)
    around2 = spread_outer(got2, nr)
    mine3 = mine23[cut2:]
    got3 = [swap(after(mine3, *parts2, *came1), "grp", k) for k in range(1, ng)]

    levels = plan(timesteps)
    noise_level = jnp.sqrt(jnp.maximum(1.0 - levels, 0.0))
    noisy = (
        jnp.sqrt(levels)[:, None, None] * latents.astype(F32)
        + noise_level[:, None, None] * noise.astype(F32)
    ).astype(BF)
    feats = jnp.pad(time_features(timesteps).astype(BF), ((0, 128 - n), (0, 0)))
    label_column = jnp.pad(labels, (0, 128 - n), constant_values=-1)[:, None]
    label_parts = jnp.pad(
        jnp.stack([labels >> 5, labels & 31], axis=1).astype(F32), ((0, 0), (0, 126))
    )
    pos = positions()

    pieces1 = spread_core(
        [(sum((m for m, _ in around1), ()), jnp.concatenate([v for _, v in around1], axis=0))], nr, parts2[:2]
    )
    wp_t, w2, wa0a, wqkv0, wqkv0_t, mods0a, time_act, pre_time, cond, act_t = assemble(
        functools.partial(first_kernel, emb_rows, seg), table, offsets, shard1, pieces1,
        (feats, label_column),
        [((D, PATCH_IN), BF), ((D, D), BF), ((D, 3 * D), BF), ((D, 3 * D), BF), ((3 * D, D), BF),
         ((3 * D, 128), F32), ((128, D), BF), ((128, D), F32), ((128, D), F32), ((D, 128), BF)],
        [((emb_full, D), BF)],
    )
    early = att_forward(noisy, wp_t, pos, after(mods0a, got2), wqkv0_t, B, 0, 2, ())
    got3 = [after(g, early[0]) for g in got3]
    got3 = jnp.concatenate(got3, axis=0)
    around3 = spread_outer(got3, nr)
    qkv0, lse0, att0 = att_forward(noisy, wp_t, pos, after(mods0a, got3), wqkv0_t, B, 1, 2, early)
    pieces2 = spread_core([(m, after(v, att0)) for m, v in around2], nr)
    wo0, wg0, wo0_t, wg0_t, wf0, wf0_t, wa0b, mods0b = assemble(
        second_kernel, table, offsets, shard2, pieces2, (act_t,),
        [((D, D), BF), ((FF, D), BF), ((D, D), BF), ((D, FF), BF), ((D, FF), BF), ((FF, D), BF),
         ((D, 3 * D), BF), ((3 * D, 128), F32)],
        [],
    )
    mid0, bra0, brb0, hid1 = ffn_forward(noisy, wp_t, pos, att0, mods0a, mods0b, wo0_t, wf0_t, wg0_t, 2 * B)
    pieces3 = spread_core([(m, after(v, hid1)) for m, v in around3], nr)
    (wo1, wg1, wo1_t, wg1_t, wf1, wf1_t, wqkv1, wqkv1_t, wa1, wm, wy, wy_t, mods1, modf) = assemble(
        third_kernel, table, offsets, shard3, pieces3, (act_t,),
        [((D, D), BF), ((FF, D), BF), ((D, D), BF), ((D, FF), BF), ((D, FF), BF), ((FF, D), BF),
         ((D, 3 * D), BF), ((3 * D, D), BF), ((D, 6 * D), BF), ((D, 2 * D), BF), ((D, PATCH_IN), BF),
         ((PATCH_IN, D), BF), ((6 * D, 128), F32), ((2 * D, 128), F32)],
        [((D, D), BF)],
    )
    entries = n * nr * ng * TOK * PATCH_IN
    outer_pack = (ng, full_rows(rows_out + 8 * rows_d + PATCH_IN), D)
    qkv_pack1 = (ng, full_rows(7 * rows_d), D)
    qkv_pack0 = (ng, full_rows(5 * rows_d + PATCH_IN), D)
    qkv1, lse1, go1, gmid1, gmb1, gmf, squares, keep_f1, send_f1 = block_step(
        table, hid1, noise, mods1, modf, wqkv1_t, wo1_t, wf1_t, wg1_t, wo1, wf1, wg1, wy_t, wy, act_t,
        float(entries), B, outer_pack,
    )
    parts_f1 = reduce_first(keep_f1, send_f1)
    ghid1, gma1, keep_a1, send_a1 = att_backward(
        table, (hid1,), qkv1, lse1, go1, gmid1, mods1, wqkv1, act_t, gmf, B, False, qkv_pack1
    )
    parts_a1 = reduce_first(keep_a1, send_a1)

    def outer_stage(parts):
        sends = []
        for number in range(1, len(digits)):
            own, sends, shift = reduce_outer(parts, table, offsets, number)
            parts = exchange(own, sends, "rep", shift)
        return parts, sends

    def member_stage(groups, extra):
        own, sends, shift = reduce_members(groups, extra, table, offsets)
        return exchange(own, sends, "grp", shift), sends

    def held(parts, *marks):
        return [parts[0]] + [after(p, *marks) for p in parts[1:]]

    parts_f1, sends_f1 = outer_stage(held(parts_f1, ghid1))
    go0, gmid0, gmb0, keep_f0, send_f0 = ffn_backward(
        table, after(ghid1, *sends_f1), mid0, att0, bra0, brb0, mods0a, mods0b, wf0_t, wo0, wf0, wg0, act_t,
        B, outer_pack,
    )
    parts_f0 = reduce_first(keep_f0, send_f0)
    parts_f1 = held(parts_f1, gmid0)
    parts_a1, sends_a1 = outer_stage(held(parts_a1, gmid0, *parts_f1[1:]))
    back0 = functools.partial(
        att_backward, table, (noisy, wp_t, pos), qkv0, lse0, go0, mods=mods0a, wqkv=wqkv0, cond=act_t, gmf=None,
        B=B, bottom=True, pack=qkv_pack0, parts=2,
    )
    half = back0(gmid=after(gmid0, *sends_a1), part=0)
    mark = half[0]
    parts_1, sends_1 = member_stage([parts_f1, held(parts_a1, mark)], None)
    parts_f0, sends_f0 = outer_stage([after(p, *sends_1) for p in held(parts_f0, mark)])
    gma0, keep_a0, send_a0 = back0(gmid=after(gmid0, *sends_f0), part=1, before=half)
    parts_a0 = reduce_first(keep_a0, send_a0)
    parts_f0 = held(parts_f0, gma0)
    piece_1 = reduce_last(held(parts_1, gma0), 0, table)
    rows0 = small_kernel(
        functools.partial(cond_back_kernel, n), [((4 * n, D), BF)], [],
        (table, after(gma0, piece_1), gmb0, gma1, gmb1, gmf, wa0a, wa0b, wa1, wm, w2, cond, pre_time,
         time_act, feats, label_parts, squares),
    )[0]
    parts_a0, sends_a0 = outer_stage(held(parts_a0, rows0, *parts_f0[1:]))
    pieces_1 = spread_core(spread_outer(piece_1, nr), nr)
    outer_state, inner_state = (w_out, out_mom, out_ema), (w_in, in_mom, in_ema)
    new_1 = update(table, offsets, pieces_1, 1, (outer_pack, qkv_pack1), outer_state, inner_state, (head, head_mom, head_ema), None)
    parts_0, sends_0 = member_stage([parts_f0, parts_a0], rows0)
    piece_0 = reduce_last(parts_0, 4 * n, table)
    pieces_0 = spread_core([(m, after(v, new_1[0])) for m, v in spread_outer(piece_0, nr)], nr)
    extra = ng * 4 * n
    new_0 = update(table, offsets, pieces_0, 0, (outer_pack, qkv_pack0), outer_state, inner_state, None, new_1[:6])
    own_rows = -(-(emb_rows + 7) // 8) * 8
    grad_rows = max(emb_full, emb_rows * (ng - 1) // 8 * 8 + own_rows)
    new_emb = small_kernel(
        functools.partial(
            emb_kernel, n, 1.0 / entries, tuple(len(m) for m, _ in pieces_0), extra, offsets["member"], emb_rows
        ),
        [(emb_table.shape, F32)] * 3 + [((1, 1), F32)],
        [((2 * n * nr * ng, D), BF)] * 2 + [((grad_rows, D), F32), ((own_rows, D), F32)],
        (table, new_0[6], emb_table, emb_mom, emb_ema, *[v for _, v in pieces_0]),
    )
    return (new_emb[3].reshape(()), *new_emb[:3], *new_0[3:6], *new_0[:3], *new_1[6:9])


def solution(mesh):
    data = P(("rep", "grp"), None, None)
    vector = P(("rep", "grp"))
    flat = P("grp", None)
    deep = P(None, "grp", None)
    return jax.shard_map(
        local,
        mesh=mesh,
        in_specs=(data, data, vector, vector, flat, flat, flat, deep, deep, deep, deep, deep, deep,
                  flat, flat, flat),
        out_specs=(P(), flat, flat, flat, deep, deep, deep, deep, deep, deep, flat, flat, flat),
        check_vma=False,
    )
```
